128 devices in a mesh: frame: 8 (over z, y_lo), space: 16 (over x, y_hi, core).
Axes of the slice: x: 4, y: 4 (y_hi: 2, y_lo: 2; y = y_hi * 2 + y_lo), z: 4, core: 2. Of those that a mesh axis runs over, the one named last changes fastest.
Arguments:
- hidden_in: bfloat16 [8, 4096, 1152], P('frame', 'space'), may hold values from -6 to 6
- query_space: bfloat16 [8, 4096, 1152], P('frame', 'space'), may hold values from -6 to 6
- key_space: bfloat16 [8, 4096, 1152], P('frame', 'space'), may hold values from -6 to 6
- value_space: bfloat16 [8, 4096, 1152], P('frame', 'space'), may hold values from -6 to 6
- cotangent: bfloat16 [8, 4096, 1152], P('frame', 'space'), may hold values from -6 to 6
- w_space_out: bfloat16 [1152, 1152], replicated, may hold values from -0.1875 to 0.1875
- w_time_qkv: bfloat16 [1152, 3456], replicated, may hold values from -1 to 1
- w_time_out: bfloat16 [1152, 1152], replicated, may hold values from -0.1875 to 0.1875
Outputs:
- block_out: bfloat16 [8, 4096, 1152], P('frame', 'space')
- grad_hidden: bfloat16 [8, 4096, 1152], P('frame', 'space')
- grad_query: bfloat16 [8, 4096, 1152], P('frame', 'space')
- grad_key: bfloat16 [8, 4096, 1152], P('frame', 'space')
- grad_value: bfloat16 [8, 4096, 1152], P('frame', 'space')
- grad_space_out: float32 [1152, 1152], P(('frame', 'space'))
- grad_time_qkv: float32 [1152, 3456], P(('frame', 'space'))
- grad_time_out: float32 [1152, 1152], P(('frame', 'space'))
The draws below stay inside these ranges and needn't reach their ends.
All inputs are finite; a program needn't handle non-finite values.
Results may differ from the reference program's by a relative error of at most 0.02.
Values may be sent and summed in bfloat16 or wider, within the bound.
A program may use at most 256 MiB of HBM per device.

```python
import jax
import jax.numpy as jnp
from jax import lax

D = 1152
HEADS = 16
HD = 72
HW = 4096
FRAMES = 8


def draw_hidden_in(key, part):
    key = jax.random.fold_in(key, 7)
    base_key = jax.random.fold_in(key, 1)
    values = jnp.clip(jax.random.normal(base_key, (FRAMES, HW, D), jnp.float32), -6.0, 6.0)
    return values.astype(jnp.bfloat16)


def draw_query_space(key, part):
    key = jax.random.fold_in(key, 3)
    values = jnp.clip(jax.random.normal(key, (FRAMES, HW, D), jnp.float32), -6.0, 6.0)
    return values.astype(jnp.bfloat16)


def draw_key_space(key, part):
    key = jax.random.fold_in(key, 5)
    values = jnp.clip(jax.random.normal(key, (FRAMES, HW, D), jnp.float32), -6.0, 6.0)
    return values.astype(jnp.bfloat16)


def draw_w_time_qkv(key, part):
    key = jax.random.fold_in(key, 11)
    weight_key = jax.random.fold_in(key, 1)
    values = jnp.clip(jax.random.normal(weight_key, (D, 3 * D), jnp.float32), -6.0, 6.0) * D ** (-0.5)
    return values.astype(jnp.bfloat16)


def block_scale(rng, shape, split, least, largest):
    def one(axis_at, blocks):
        steps = jax.random.uniform(jax.random.fold_in(jax.random.fold_in(rng, 6), axis_at), (blocks,), jnp.float32, least / len(split), largest / len(split))
        return jnp.repeat(jnp.exp(steps), shape[axis_at] // blocks).reshape((-1,) + (1,) * (len(shape) - axis_at - 1))

    gain = one(*split[0])
    for cut in split[1:]:
        gain = gain * one(*cut)
    return gain


def bell_draw(own_key, shape, width, bound, pieces=(), held_as=jnp.bfloat16):
    result = jax.random.normal(own_key, shape, jnp.float32) * width
    if len(pieces) > 0:
        result = block_scale(own_key, shape, pieces, -0.22, 0.18) * result
    return jnp.clip(result, min=-bound, max=bound).astype(held_as)


def setup_inputs(seed: int = 0) -> dict:
    keys = jax.random.split(jax.random.key(seed), 9)
    return {
        "hidden_in": draw_hidden_in(jax.random.fold_in(keys[8], 71), 0),
        "query_space": draw_query_space(jax.random.fold_in(keys[8], 71), 0),
        "key_space": draw_key_space(jax.random.fold_in(keys[8], 71), 0),
        "value_space": bell_draw(keys[3], (FRAMES, HW, D), 1.0, 6.0, ((0, 8), (1, 16))),
        "cotangent": bell_draw(keys[4], (FRAMES, HW, D), 1.0, 6.0, ((0, 8), (1, 16))),
        "w_space_out": bell_draw(keys[5], (D, D), D ** -0.5, 0.1875),
        "w_time_qkv": draw_w_time_qkv(jax.random.fold_in(keys[8], 71), 0),
        "w_time_out": bell_draw(keys[7], (D, D), D ** -0.5, 0.1875),
    }


def attend_forward(query, key_rows, value_rows):
    seq_length, head_count, head_dim = query.shape
    score_scale = head_dim ** -0.5
    block_rows = min(512, seq_length)
    block_count = seq_length // block_rows
    query_blocks = query.reshape(block_count, block_rows, head_count, head_dim)
    key_wide = key_rows.astype(jnp.float32)
    value_wide = value_rows.astype(jnp.float32)

    def one_block(query_block):
        scores = jnp.einsum("qhe,khe->hqk", query_block.astype(jnp.float32), key_wide) * score_scale
        row_max = jnp.max(scores, axis=-1, keepdims=True)
        exp_rows = jnp.exp(scores - row_max)
        row_sum = jnp.sum(exp_rows, axis=-1, keepdims=True)
        prob_bf = (exp_rows / row_sum).astype(jnp.bfloat16)
        mixed_out = jnp.einsum("hqk,khe->qhe", prob_bf.astype(jnp.float32), value_wide)
        return mixed_out.astype(jnp.bfloat16), (row_max + jnp.log(row_sum))[..., 0]

    mixed_out, logsum = lax.map(one_block, query_blocks)
    return mixed_out.reshape(seq_length, head_count, head_dim), logsum


def attend_backward(query, key_rows, value_rows, logsum, grad_mixed):
    seq_length, head_count, head_dim = query.shape
    score_scale = head_dim ** -0.5
    block_rows = min(512, seq_length)
    block_count = seq_length // block_rows
    query_blocks = query.reshape(block_count, block_rows, head_count, head_dim)
    grad_blocks = grad_mixed.reshape(block_count, block_rows, head_count, head_dim)
    key_wide = key_rows.astype(jnp.float32)
    value_wide = value_rows.astype(jnp.float32)

    def backward_step(state, inputs):
        acc_key, acc_value = state
        query_block, grad_block, logsum_block = inputs
        query_wide = query_block.astype(jnp.float32)
        grad_wide = grad_block.astype(jnp.float32)
        scores = jnp.einsum("qhe,khe->hqk", query_wide, key_wide) * score_scale
        probs = jnp.exp(scores - logsum_block[..., None])
        grad_probs = jnp.einsum("qhe,khe->hqk", grad_wide, value_wide)
        row_inner = jnp.sum(probs * grad_probs, axis=-1, keepdims=True)
        grad_scores = (probs * (grad_probs - row_inner) * score_scale).astype(jnp.bfloat16).astype(jnp.float32)
        grad_query = jnp.einsum("hqk,khe->qhe", grad_scores, key_wide).astype(jnp.bfloat16)
        acc_key = acc_key + jnp.einsum("hqk,qhe->khe", grad_scores, query_wide)
        prob_bf = probs.astype(jnp.bfloat16).astype(jnp.float32)
        acc_value = acc_value + jnp.einsum("hqk,qhe->khe", prob_bf, grad_wide)
        return (acc_key, acc_value), grad_query

    zero_acc = jnp.zeros((seq_length, head_count, head_dim), jnp.float32)
    (acc_key, acc_value), grad_query = lax.scan(backward_step, (zero_acc, zero_acc), (query_blocks, grad_blocks, logsum))
    return grad_query.reshape(seq_length, head_count, head_dim), acc_key.astype(jnp.bfloat16), acc_value.astype(jnp.bfloat16)


def space_forward(items):
    return attend_forward(items[0], items[1], items[2])


def space_backward(items):
    return attend_backward(items[0], items[1], items[2], items[3], items[4])


def reference(hidden_in, query_space, key_space, value_space, cotangent, w_space_out, w_time_qkv, w_time_out):
    head_shape = (FRAMES, HW, HEADS, HD)
    tokens = FRAMES * HW
    q_heads = query_space.reshape(head_shape)
    k_heads = key_space.reshape(head_shape)
    v_heads = value_space.reshape(head_shape)
    mixed_space, logsum_space = lax.map(space_forward, (q_heads, k_heads, v_heads))
    attn_space = mixed_space.reshape(tokens, D)
    hidden = (hidden_in.reshape(tokens, D).astype(jnp.float32) + jnp.dot(attn_space, w_space_out, preferred_element_type=jnp.float32)).astype(jnp.bfloat16)
    projected = jnp.dot(hidden, w_time_qkv, preferred_element_type=jnp.float32).astype(jnp.bfloat16)
    q_time = projected[:, :D].reshape(head_shape)
    k_time = projected[:, D:2 * D].reshape(head_shape)
    v_time = projected[:, 2 * D:].reshape(head_shape)
    mixed_time, logsum_time = jax.vmap(attend_forward, in_axes=1, out_axes=(1, 0))(q_time, k_time, v_time)
    attn_time = mixed_time.reshape(tokens, D)
    cot_rows = cotangent.reshape(tokens, D)
    block_out = (hidden.astype(jnp.float32) + jnp.dot(attn_time, w_time_out, preferred_element_type=jnp.float32)).astype(jnp.bfloat16)
    grad_time_out = jnp.dot(attn_time.T, cot_rows, preferred_element_type=jnp.float32)
    grad_attn_time = jnp.dot(cot_rows, w_time_out.T, preferred_element_type=jnp.float32).astype(jnp.bfloat16)
    grad_q_time, grad_k_time, grad_v_time = jax.vmap(attend_backward, in_axes=(1, 1, 1, 0, 1), out_axes=1)(q_time, k_time, v_time, logsum_time, grad_attn_time.reshape(head_shape))
    grad_projected = jnp.concatenate([grad_q_time.reshape(tokens, D), grad_k_time.reshape(tokens, D), grad_v_time.reshape(tokens, D)], axis=1)
    grad_time_qkv = jnp.dot(hidden.T, grad_projected, preferred_element_type=jnp.float32)
    grad_hidden = (cot_rows.astype(jnp.float32) + jnp.dot(grad_projected, w_time_qkv.T, preferred_element_type=jnp.float32)).astype(jnp.bfloat16)
    grad_space_out = jnp.dot(attn_space.T, grad_hidden, preferred_element_type=jnp.float32)
    grad_attn_space = jnp.dot(grad_hidden, w_space_out.T, preferred_element_type=jnp.float32).astype(jnp.bfloat16)
    grad_query, grad_key, grad_value = lax.map(space_backward, (q_heads, k_heads, v_heads, logsum_space, grad_attn_space.reshape(head_shape)))
    full_shape = (FRAMES, HW, D)
    return (block_out.reshape(full_shape), grad_hidden.reshape(full_shape), grad_query.reshape(full_shape), grad_key.reshape(full_shape), grad_value.reshape(full_shape), grad_space_out, grad_time_qkv, grad_time_out)
```

```python
import jax
import jax.numpy as jnp
from jax import lax
from jax.experimental import pallas as pl
from jax.experimental.pallas import tpu as pltpu
from jax.sharding import PartitionSpec as P

HEADS = 16
HD = 72
ROWS = 80
SCALE = HD**-0.5
LOG2E = 1.4426950408889634
VMEM_BYTES = 60 * 2**20
BF = jnp.bfloat16
F32 = jnp.float32
ALL = ("frame", "space")


def kernel_call(body, out_shape, scratch_shapes, flops, moved, args):
    return pl.pallas_call(
        body,
        out_shape=out_shape,
        scratch_shapes=scratch_shapes,
        compiler_params=pltpu.CompilerParams(vmem_limit_bytes=VMEM_BYTES),
        cost_estimate=pl.CostEstimate(flops=flops, bytes_accessed=moved, transcendentals=0),
    )(*args)


def shape(dims, dtype):
    return jax.ShapeDtypeStruct(dims, dtype)


def dot(a, b):
    return jnp.dot(a, b, preferred_element_type=F32)


def dot_nt(a, b):
    return lax.dot_general(a, b, (((1,), (1,)), ((), ())), preferred_element_type=F32)


def dot_tn(a, b):
    return lax.dot_general(a, b, (((0,), (0,)), ((), ())), preferred_element_type=F32)


def two_parts(x):
    high = x.astype(BF)
    return [high, (x - high.astype(F32)).astype(BF)]


def three_parts_rows(x, rows):
    high = x.astype(BF).astype(F32)
    rest = x - high
    mid = rest.astype(BF).astype(F32)
    low = rest - mid
    at = lax.broadcasted_iota(jnp.int32, (rows, x.shape[1]), 0)
    return jnp.where(at == 0, high, jnp.where(at == 1, mid, jnp.where(at == 2, low, 0.0))).astype(BF)


def minus_rows(rows, columns):
    at = lax.broadcasted_iota(jnp.int32, (rows, columns), 0)
    return jnp.where(at < 3, -1.0, 0.0).astype(BF)


def split_heads_body(q_ref, k_ref, v_ref, out_ref):
    tokens = q_ref.shape[1]
    at = lax.broadcasted_iota(jnp.int32, (ROWS - HD, tokens), 0)
    ones_row = jnp.where(at == 0, 1.0, 0.0)
    for i, ref in enumerate((q_ref, k_ref, v_ref)):
        flipped = ref[0].astype(F32).T
        for h in range(HEADS):
            fill = ones_row if i == 2 else jnp.zeros_like(ones_row)
            block = jnp.concatenate([flipped[h * HD : (h + 1) * HD], fill], axis=0)
            out_ref[h, i] = block.astype(BF)


def split_heads(query, key_rows, value_rows):
    tokens, width = query.shape[1:]
    return kernel_call(
        split_heads_body,
        shape((HEADS, 3, ROWS, tokens), BF),
        [],
        0,
        3 * tokens * width * 5,
        (query, key_rows, value_rows),
    )


def join_heads_body(in_ref, q_ref, k_ref, v_ref):
    for i, ref in enumerate((q_ref, k_ref, v_ref)):
        blocks = [in_ref[h, i].astype(F32)[:HD] for h in range(HEADS)]
        ref[0] = jnp.concatenate(blocks, axis=0).T.astype(BF)


def join_heads(blocks):
    tokens = blocks.shape[3]
    rows = shape((1, tokens, HEADS * HD), BF)
    return kernel_call(
        join_heads_body, (rows, rows, rows), [], 0, 3 * tokens * HEADS * HD * 5, (blocks,)
    )


def scaled_query(block):
    return two_parts(block.astype(F32) * (SCALE * LOG2E))


def space_forward_body(x_ref, o_ref, o_rows_ref, lse_ref, k_nat, v_rows):
    blocks, _, _, width = x_ref.shape

    def prepare(j, _):
        at = pl.ds(pl.multiple_of(j * width, width), width)
        k_block = x_ref[j, 1]
        k_nat[at, :] = jnp.concatenate([k_block, k_block], axis=0).T
        v_rows[:, at] = x_ref[j, 2]
        return 0

    lax.fori_loop(0, blocks, prepare, 0)

    def step(j, _):
        q_block = jnp.concatenate(scaled_query(x_ref[j, 0]), axis=0)
        scores = dot(k_nat[...], q_block)
        top = jnp.max(scores, axis=0, keepdims=True)
        probs = jnp.exp2(scores - top).astype(BF)
        mixed = dot(v_rows[...], probs)
        total = mixed[HD : HD + 1]
        mixed = mixed / total
        o_rows_ref[j] = mixed
        lse_ref[j] = jnp.broadcast_to(top + jnp.log2(total), (8, width))
        filled = jnp.concatenate([mixed[:HD], jnp.zeros((128 - HD, width), F32)], axis=0)
        o_ref[:, j] = filled.T.astype(BF).reshape(o_ref.shape[0], o_ref.shape[2], 128)
        return 0

    lax.fori_loop(0, blocks, step, 0)


def space_forward(blocks, frames):
    count, _, _, width = blocks.shape
    seq = count * width
    return kernel_call(
        space_forward_body,
        (
            shape((frames, count, width // frames, 128), BF),
            shape((count, ROWS, width), F32),
            shape((count, 8, width), F32),
        ),
        [pltpu.VMEM((seq, 2 * ROWS), BF), pltpu.VMEM((ROWS, seq), BF)],
        4 * seq * seq * 128,
        5 * 2**20,
        (blocks,),
    )


K_STEP = 256
Q_STEP = 1024


def space_backward_body(
    x_ref, o_rows_ref, lse_ref, g_ref, out_ref, q_aug, g_aug, q_rows, g_rows, p_buf, ds_buf, dq_sum
):
    blocks, _, _, width = x_ref.shape
    seq = blocks * width

    def prepare(j, _):
        at = pl.ds(pl.multiple_of(j * width, width), width)
        q_block = x_ref[j, 0]
        parts = scaled_query(q_block) + [three_parts_rows(lse_ref[j][:1], 16)]
        q_aug[at, :] = jnp.concatenate(parts, axis=0).T
        q_rows[:, at] = q_block
        g_block = g_ref[:, j].reshape(width, 128).astype(F32).T[:ROWS]
        inner = jnp.sum(g_block[:HD] * o_rows_ref[j][:HD], axis=0, keepdims=True)
        g_bf = g_block.astype(BF)
        g_rows[:, at] = g_bf
        g_aug[at, :] = jnp.concatenate([g_bf, three_parts_rows(inner, 16)], axis=0).T
        dq_sum[at, :] = jnp.zeros((width, ROWS), F32)
        return 0

    lax.fori_loop(0, blocks, prepare, 0)

    def step(j, _):
        k_block = x_ref[j, 1]
        v_block = x_ref[j, 2]
        k_aug = jnp.concatenate([k_block, k_block, minus_rows(16, width)], axis=0)
        v_aug = jnp.concatenate([v_block, minus_rows(16, width)], axis=0)
        k_nat = k_block.T

        for c in range(seq // Q_STEP):
            at = pl.ds(c * Q_STEP, Q_STEP)
            probs = jnp.exp2(dot(q_aug[at, :], k_aug))
            p_buf[at, :] = probs.astype(BF)
            ds = (probs * dot(g_aug[at, :], v_aug)).astype(BF)
            ds_buf[at, :] = ds
            dq_sum[at, :] += dot(ds, k_nat)

        out_ref[j, 1] = (dot(q_rows[...], ds_buf[...]) * SCALE).astype(BF)
        out_ref[j, 2] = dot(g_rows[...], p_buf[...]).astype(BF)
        return 0

    lax.fori_loop(0, blocks, step, 0)

    def finish(j, _):
        at = pl.ds(pl.multiple_of(j * width, width), width)
        out_ref[j, 0] = (dq_sum[at, :] * SCALE).T.astype(BF)
        return 0

    lax.fori_loop(0, blocks, finish, 0)


def space_backward(blocks, o_rows, lse, grads):
    count, _, _, width = blocks.shape
    seq = count * width
    return kernel_call(
        space_backward_body,
        shape(blocks.shape, BF),
        [
            pltpu.VMEM((seq, 2 * ROWS + 16), BF),
            pltpu.VMEM((seq, ROWS + 16), BF),
            pltpu.VMEM((ROWS, seq), BF),
            pltpu.VMEM((ROWS, seq), BF),
            pltpu.VMEM((seq, width), BF),
            pltpu.VMEM((seq, width), BF),
            pltpu.VMEM((seq, ROWS), F32),
        ],
        10 * seq * seq * 128,
        8 * 2**20,
        (blocks, o_rows, lse, grads),
    )


def middle_body(
    attn_ref,
    hidden_in_ref,
    cot_ref,
    w_space_ref,
    w_qkv_ref,
    w_time_ref,
    g_out_ref,
    gh_ref,
    attn_space_ref,
    hidden_ref,
    attn_time_ref,
    dqkv_ref,
    qkv_ref,
    ga_ref,
):
    frames, _, positions, _ = attn_ref.shape
    tokens = frames * positions
    width = HEADS * HD
    for h in range(HEADS):
        block = attn_ref[:, h].reshape(tokens, 128)
        attn_space_ref[:, h * HD : (h + 1) * HD] = block[:, :HD]
    cot = cot_ref[...].reshape(tokens, width)
    base = hidden_in_ref[...].reshape(tokens, width).astype(F32)
    hidden_ref[...] = (base + dot(attn_space_ref[...], w_space_ref[...])).astype(BF)
    for c in range(3):
        at = pl.ds(c * width, width)
        qkv_ref[:, at] = dot(hidden_ref[...], w_qkv_ref[:, at]).astype(BF)
    ga_ref[...] = dot_nt(cot, w_time_ref[...]).astype(BF)

    same = (
        lax.broadcasted_iota(jnp.int32, (tokens, tokens), 0) % positions
        == lax.broadcasted_iota(jnp.int32, (tokens, tokens), 1) % positions
    )
    for h in range(HEADS):
        lo, hi = h * HD, (h + 1) * HD
        q = qkv_ref[:, lo:hi]
        k = qkv_ref[:, width + lo : width + hi]
        v = qkv_ref[:, 2 * width + lo : 2 * width + hi]
        g = ga_ref[:, lo:hi]
        scores = jnp.where(same, dot_nt(q, k) * SCALE, -jnp.inf)
        exps = jnp.exp(scores - jnp.max(scores, axis=1, keepdims=True))
        probs = exps / jnp.sum(exps, axis=1, keepdims=True)
        probs_bf = probs.astype(BF)
        attn_time_ref[:, lo:hi] = dot(probs_bf, v).astype(BF)
        weighted = probs * dot_nt(g, v)
        ds = ((weighted - probs * jnp.sum(weighted, axis=1, keepdims=True)) * SCALE).astype(BF)
        dqkv_ref[:, lo:hi] = dot(ds, k).astype(BF)
        dqkv_ref[:, width + lo : width + hi] = dot_tn(ds, q).astype(BF)
        dqkv_ref[:, 2 * width + lo : 2 * width + hi] = dot_tn(probs_bf, g).astype(BF)

    gh_ref[...] = (cot.astype(F32) + dot_nt(dqkv_ref[...], w_qkv_ref[...])).astype(BF)
    ga_ref[...] = dot_nt(gh_ref[...], w_space_ref[...]).astype(BF)
    for h in range(HEADS):
        block = ga_ref[:, h * HD : (h + 1) * HD]
        filled = jnp.concatenate([block, jnp.zeros((tokens, 128 - HD), BF)], axis=1)
        g_out_ref[:, h] = filled.reshape(frames, positions, 128)


def middle(attn, hidden_in, cot, w_space_out, w_time_qkv, w_time_out):
    frames, _, positions, _ = attn.shape
    tokens = frames * positions
    width = HEADS * HD
    rows = shape((tokens, width), BF)
    wide = shape((tokens, 3 * width), BF)
    return kernel_call(
        middle_body,
        (shape(attn.shape, BF), rows, rows, rows, rows, wide),
        [pltpu.VMEM((tokens, 3 * width), BF), pltpu.VMEM((tokens, width), BF)],
        2 * tokens * width * width * 9,
        20 * 2**20,
        (attn, hidden_in, cot, w_space_out, w_time_qkv, w_time_out),
    )


def exchange(blocks, axis):
    return lax.all_to_all(blocks, axis, split_axis=0, concat_axis=0, tiled=True)


def exchange_all(blocks):
    flat = exchange(blocks.reshape((-1,) + blocks.shape[2:]), ALL)
    return flat.reshape(blocks.shape)


def grad_terms(rows, grads):
    return lax.dot_general(rows, grads, (((0,), (0,)), ((), ())), preferred_element_type=F32)


def shards(
    hidden_in, query_space, key_space, value_space, cotangent, w_space_out, w_time_qkv, w_time_out
):
    tile_rows, width = hidden_in.shape[1:]
    frames = lax.axis_size("frame")
    positions = tile_rows // frames
    by_frame = (frames, positions, width)

    head_blocks = exchange(split_heads(query_space, key_space, value_space), "space")
    hidden_cols = exchange(hidden_in.reshape(by_frame), "frame")
    cot_cols = exchange(cotangent.reshape(by_frame), "frame")
    mixed, o_rows, lse = space_forward(head_blocks, frames)
    attn = exchange_all(mixed)
    g_out, grad_cols, attn_space, hidden, attn_time, dqkv = middle(
        attn, hidden_cols, cot_cols, w_space_out, w_time_qkv, w_time_out
    )
    grads = exchange_all(g_out)
    cot = cot_cols.reshape(-1, width)
    sums = [
        lax.psum_scatter(terms, ALL, scatter_dimension=0, tiled=True)
        for terms in (
            grad_terms(attn_space, grad_cols),
            grad_terms(hidden, dqkv),
            grad_terms(attn_time, cot),
        )
    ]
    out_cols = (
        hidden.astype(F32) + jnp.dot(attn_time, w_time_out, preferred_element_type=F32)
    ).astype(BF)
    block_out = exchange(out_cols.reshape(by_frame), "frame").reshape(hidden_in.shape)
    grad_hidden = exchange(grad_cols.reshape(by_frame), "frame").reshape(hidden_in.shape)
    back = exchange(space_backward(head_blocks, o_rows, lse, grads), "space")
    return (block_out, grad_hidden, *join_heads(back), *sums)


def solution(mesh):
    rows = P("frame", "space", None)
    weights = P(ALL, None)
    return jax.shard_map(
        shards,
        mesh=mesh,
        in_specs=(rows,) * 5 + (P(),) * 3,
        out_specs=(rows,) * 5 + (weights,) * 3,
        check_vma=False,
    )
```

```python
import jax
import jax.numpy as jnp
from jax import lax
from jax.experimental import pallas as pl
from jax.experimental.pallas import tpu as pltpu
from jax.sharding import PartitionSpec as P

HEADS = 16
HD = 72
ROWS = 80
SCALE = HD**-0.5
LOG2E = 1.4426950408889634
VMEM_BYTES = 62 * 2**20
BF = jnp.bfloat16
F32 = jnp.float32
ALL = ("frame", "space")


def kernel_call(body, out_shape, scratch_shapes, flops, moved, args):
    return pl.pallas_call(
        body,
        out_shape=out_shape,
        scratch_shapes=scratch_shapes,
        compiler_params=pltpu.CompilerParams(vmem_limit_bytes=VMEM_BYTES),
        cost_estimate=pl.CostEstimate(flops=flops, bytes_accessed=moved, transcendentals=0),
    )(*args)


def shape(dims, dtype):
    return jax.ShapeDtypeStruct(dims, dtype)


def dot(a, b):
    return jnp.dot(a, b, preferred_element_type=F32)


def dot_nt(a, b):
    return lax.dot_general(a, b, (((1,), (1,)), ((), ())), preferred_element_type=F32)


def dot_tn(a, b):
    return lax.dot_general(a, b, (((0,), (0,)), ((), ())), preferred_element_type=F32)


def two_parts(x):
    high = x.astype(BF)
    return [high, (x - high.astype(F32)).astype(BF)]


def three_parts_rows(x, rows):
    high = x.astype(BF).astype(F32)
    rest = x - high
    mid = rest.astype(BF).astype(F32)
    low = rest - mid
    at = lax.broadcasted_iota(jnp.int32, (rows, x.shape[1]), 0)
    return jnp.where(at == 0, high, jnp.where(at == 1, mid, jnp.where(at == 2, low, 0.0))).astype(BF)


def minus_rows(rows, columns):
    at = lax.broadcasted_iota(jnp.int32, (rows, columns), 0)
    return jnp.where(at < 3, -1.0, 0.0).astype(BF)


def split_heads_body(q_ref, k_ref, v_ref, out_ref):
    tokens = q_ref.shape[1]
    at = lax.broadcasted_iota(jnp.int32, (ROWS - HD, tokens), 0)
    ones_row = jnp.where(at == 0, 1.0, 0.0)
    for i, ref in enumerate((q_ref, k_ref, v_ref)):
        flipped = ref[0].astype(F32).T
        for h in range(HEADS):
            fill = ones_row if i == 2 else jnp.zeros_like(ones_row)
            block = jnp.concatenate([flipped[h * HD : (h + 1) * HD], fill], axis=0)
            out_ref[h, i] = block.astype(BF)


def split_heads(query, key_rows, value_rows):
    tokens, width = query.shape[1:]
    return kernel_call(
        split_heads_body,
        shape((HEADS, 3, ROWS, tokens), BF),
        [],
        0,
        3 * tokens * width * 5,
        (query, key_rows, value_rows),
    )


def join_heads_body(in_ref, q_ref, k_ref, v_ref):
    for i, ref in enumerate((q_ref, k_ref, v_ref)):
        blocks = [in_ref[h, i].astype(F32)[:HD] for h in range(HEADS)]
        ref[0] = jnp.concatenate(blocks, axis=0).T.astype(BF)


def join_heads(blocks):
    tokens = blocks.shape[3]
    rows = shape((1, tokens, HEADS * HD), BF)
    return kernel_call(
        join_heads_body, (rows, rows, rows), [], 0, 3 * tokens * HEADS * HD * 5, (blocks,)
    )


def scaled_query(block):
    return two_parts(block.astype(F32) * (SCALE * LOG2E))


def space_forward_body(x_ref, o_ref, o_rows_ref, lse_ref, k_nat, v_rows):
    blocks, _, _, width = x_ref.shape

    def prepare(j, _):
        at = pl.ds(pl.multiple_of(j * width, width), width)
        k_block = x_ref[j, 1]
        k_nat[at, :] = jnp.concatenate([k_block, k_block], axis=0).T
        v_rows[:, at] = x_ref[j, 2]
        return 0

    lax.fori_loop(0, blocks, prepare, 0)

    def step(j, _):
        q_block = jnp.concatenate(scaled_query(x_ref[j, 0]), axis=0)
        scores = dot(k_nat[...], q_block)
        top = jnp.max(scores, axis=0, keepdims=True)
        probs = jnp.exp2(scores - top).astype(BF)
        mixed = dot(v_rows[...], probs)
        total = mixed[HD : HD + 1]
        mixed = mixed / total
        o_rows_ref[j] = mixed
        lse_ref[j] = jnp.broadcast_to(top + jnp.log2(total), (8, width))
        filled = jnp.concatenate([mixed[:HD], jnp.zeros((128 - HD, width), F32)], axis=0)
        o_ref[:, j] = filled.T.astype(BF).reshape(o_ref.shape[0], o_ref.shape[2], 128)
        return 0

    lax.fori_loop(0, blocks, step, 0)


def space_forward(blocks, frames):
    count, _, _, width = blocks.shape
    seq = count * width
    return kernel_call(
        space_forward_body,
        (
            shape((frames, count, width // frames, 128), BF),
            shape((count, ROWS, width), F32),
            shape((count, 8, width), F32),
        ),
        [pltpu.VMEM((seq, 2 * ROWS), BF), pltpu.VMEM((ROWS, seq), BF)],
        4 * seq * seq * 128,
        5 * 2**20,
        (blocks,),
    )


Q_STEP = 1024
TILE_ROWS = 144
TILE_COLS = 384


def backward_prepare(x_ref, o_rows_ref, lse_ref, g_ref, q_aug, g_aug, q_rows, g_rows, dq_sum):
    blocks, _, _, width = x_ref.shape

    def prepare(j, _):
        at = pl.ds(pl.multiple_of(j * width, width), width)
        q_block = x_ref[j, 0]
        parts = scaled_query(q_block) + [three_parts_rows(lse_ref[j][:1], 16)]
        q_aug[at, :] = jnp.concatenate(parts, axis=0).T
        q_rows[:, at] = q_block
        g_block = g_ref[:, j].reshape(width, 128).astype(F32).T[:ROWS]
        inner = jnp.sum(g_block[:HD] * o_rows_ref[j][:HD], axis=0, keepdims=True)
        g_bf = g_block.astype(BF)
        g_rows[:, at] = g_bf
        g_aug[at, :] = jnp.concatenate([g_bf, three_parts_rows(inner, 16)], axis=0).T
        dq_sum[at, :] = jnp.zeros((width, ROWS), F32)
        return 0

    lax.fori_loop(0, blocks, prepare, 0)


def backward_steps(
    first, last, x_ref, out_ref, q_aug, g_aug, q_rows, g_rows, p_buf, ds_buf, dq_sum
):
    blocks, _, _, width = x_ref.shape
    seq = blocks * width

    def step(j, _):
        k_block = x_ref[j, 1]
        v_block = x_ref[j, 2]
        k_aug = jnp.concatenate([k_block, k_block, minus_rows(16, width)], axis=0)
        v_aug = jnp.concatenate([v_block, minus_rows(16, width)], axis=0)
        k_nat = k_block.T

        for c in range(seq // Q_STEP):
            at = pl.ds(c * Q_STEP, Q_STEP)
            probs = jnp.exp2(dot(q_aug[at, :], k_aug))
            p_buf[at, :] = probs.astype(BF)
            ds = (probs * dot(g_aug[at, :], v_aug)).astype(BF)
            ds_buf[at, :] = ds
            dq_sum[at, :] += dot(ds, k_nat)

        out_ref[j, 1] = (dot(q_rows[...], ds_buf[...]) * SCALE).astype(BF)
        out_ref[j, 2] = dot(g_rows[...], p_buf[...]).astype(BF)
        return 0

    lax.fori_loop(first, last, step, 0)


def backward_finish(out_ref, dq_sum):
    blocks, _, _, width = out_ref.shape

    def finish(j, _):
        at = pl.ds(pl.multiple_of(j * width, width), width)
        out_ref[j, 0] = (dq_sum[at, :] * SCALE).T.astype(BF)
        return 0

    lax.fori_loop(0, blocks, finish, 0)


def add_into(target, terms, lead):
    count = 1
    for n in lead:
        count *= n

    def one(i, _):
        index = []
        for n in reversed(lead):
            index.insert(0, lax.rem(i, n))
            i = lax.div(i, n)
        total = target(*index)[...].astype(F32)
        for term in terms:
            total = total + term(*index)[...].astype(F32)
        target(*index)[...] = total.astype(BF)
        return 0

    lax.fori_loop(0, count, one, 0)


def space_backward_body(
    x_ref,
    o_rows_ref,
    lse_ref,
    g_ref,
    attn_space_ref,
    hidden_ref,
    attn_time_ref,
    gh_ref,
    dqkv_ref,
    cot_ref,
    out_ref,
    sums_ref,
    q_aug,
    g_aug,
    q_rows,
    g_rows,
    p_buf,
    ds_buf,
    dq_sum,
    terms,
    half,
    x_in_a,
    z_in_b,
    z_in_a,
    x_in_b,
    lo_in,
    hi_in,
    mine,
    gathered,
    send1,
    recv1,
    send2,
    recv2,
    send3,
    recv3,
    send4,
    recv4,
    send6,
    recv6,
):
    frame, space = lax.axis_index("frame"), lax.axis_index("space")
    z, lo = lax.div(frame, 2), lax.rem(frame, 2)
    x, hi, core = lax.div(space, 4), lax.rem(lax.div(space, 2), 2), lax.rem(space, 2)

    def x_peer(i):
        return (frame, lax.rem(x + i, 4) * 4 + hi * 2 + core)

    def z_peer(i):
        return (lax.rem(z + i, 4) * 2 + lo, space)

    def space_peer(i):
        return (frame, lax.rem(space + i, 16))

    lo_peer = (z * 2 + 1 - lo, space)
    hi_peer = (frame, x * 4 + (1 - hi) * 2 + core)
    core_peer = (frame, x * 4 + hi * 2 + 1 - core)

    def copy(src, dst, send_sem, recv_sem, device):
        return pltpu.make_async_remote_copy(
            src_ref=src,
            dst_ref=dst,
            send_sem=send_sem,
            recv_sem=recv_sem,
            device_id=device,
            device_id_type=pl.DeviceIdType.MESH,
        )

    barrier = pltpu.get_barrier_semaphore()
    peers = [space_peer(i) for i in range(1, 16)] + [z_peer(i) for i in range(1, 4)] + [lo_peer]
    for peer in peers:
        pl.semaphore_signal(barrier, inc=1, device_id=peer, device_id_type=pl.DeviceIdType.MESH)

    for t, (rows_ref, grads_ref, offset) in enumerate(
        [(attn_space_ref, gh_ref, c) for c in range(3)]
        + [(hidden_ref, dqkv_ref, c) for c in range(9)]
        + [(attn_time_ref, cot_ref, c) for c in range(3)]
    ):
        part = dot_tn(rows_ref[...], grads_ref[:, offset * TILE_COLS : (offset + 1) * TILE_COLS])
        part = part.astype(BF)
        for f in range(8):
            rows = part[f * TILE_ROWS : (f + 1) * TILE_ROWS]
            terms[f % 2, f // 2, t // 4, t // 2 % 2, t % 2] = rows
    for f in range(8):
        terms[f % 2, f // 2, 3, 1, 1] = jnp.zeros((TILE_ROWS, TILE_COLS), BF)

    pl.semaphore_wait(barrier, len(peers))

    first = [
        copy(
            terms.at[y, w, :, :, 1 - core],
            half.at[y, w],
            send1.at[y, w],
            recv1.at[y, w],
            core_peer,
        )
        for y in range(2)
        for w in range(4)
    ]
    for c in first:
        c.start()

    state = (q_aug, g_aug, q_rows, g_rows)
    backward_prepare(x_ref, o_rows_ref, lse_ref, g_ref, *state, dq_sum)

    def attend(start, stop):
        backward_steps(start, stop, x_ref, out_ref, *state, p_buf, ds_buf, dq_sum)

    attend(0, STAGES[0])

    for c in first:
        c.wait()
    add_into(
        lambda y, w, a, b: half.at[y, w, a, b],
        [lambda y, w, a, b: terms.at[y, w, a, b, core]],
        (2, 4, 4, 2),
    )
    second = []
    for i in range(1, 4):
        to_x, to_z = lax.rem(x + i, 4), lax.rem(z + i, 4)
        s = i - 1
        second.append(
            copy(half.at[0, :, to_x], x_in_a.at[s], send2.at[0, s], recv2.at[0, s], x_peer(i))
        )
        second.append(
            copy(half.at[1, to_z], z_in_b.at[s], send2.at[1, s], recv2.at[1, s], z_peer(i))
        )
    for c in second:
        c.start()

    attend(STAGES[0], STAGES[1])

    for c in second:
        c.wait()
    add_into(
        lambda w, b: half.at[0, w, x, b],
        [lambda w, b, s=s: x_in_a.at[s, w, b] for s in range(3)],
        (4, 2),
    )
    add_into(
        lambda a, b: half.at[1, z, a, b],
        [lambda a, b, s=s: z_in_b.at[s, a, b] for s in range(3)],
        (4, 2),
    )
    third = []
    for i in range(1, 4):
        to_x, to_z = lax.rem(x + i, 4), lax.rem(z + i, 4)
        s = i - 1
        third.append(
            copy(half.at[0, to_z, x], z_in_a.at[s], send3.at[0, s], recv3.at[0, s], z_peer(i))
        )
        third.append(
            copy(half.at[1, z, to_x], x_in_b.at[s], send3.at[1, s], recv3.at[1, s], x_peer(i))
        )
    for c in third:
        c.start()

    attend(STAGES[1], STAGES[2])

    for c in third:
        c.wait()
    add_into(
        lambda b: half.at[0, z, x, b], [lambda b, s=s: z_in_a.at[s, b] for s in range(3)], (2,)
    )
    add_into(
        lambda b: half.at[1, z, x, b], [lambda b, s=s: x_in_b.at[s, b] for s in range(3)], (2,)
    )
    fourth = copy(half.at[1 - lo, z, x], lo_in, send4.at[0], recv4.at[0], lo_peer)
    fourth.start()

    attend(STAGES[2], STAGES[3])

    fourth.wait()
    add_into(lambda b: half.at[lo, z, x, b], [lambda b: lo_in.at[b]], (2,))
    fifth = copy(half.at[lo, z, x, 1 - hi], hi_in, send4.at[1], recv4.at[1], hi_peer)
    fifth.start()

    attend(STAGES[3], 16)

    fifth.wait()
    total = (half[lo, z, x, hi].astype(F32) + hi_in[...].astype(F32)).astype(BF)
    mine[...] = total
    sixth = [
        copy(mine, gathered.at[i - 1], send6.at[i - 1], recv6.at[i - 1], space_peer(i))
        for i in range(1, 16)
    ]
    for c in sixth:
        c.start()

    backward_finish(out_ref, dq_sum)
    sums_ref[space] = total
    for i, c in enumerate(sixth):
        c.wait()
        sums_ref[lax.rem(space + 15 - i, 16)] = gathered[i]


STAGES = (3, 10, 13, 15)


def space_backward(blocks, o_rows, lse, grads, pairs):
    count, _, _, width = blocks.shape
    seq = count * width
    tile = (TILE_ROWS, TILE_COLS)
    dma = pltpu.SemaphoreType.DMA
    return pl.pallas_call(
        space_backward_body,
        out_shape=(shape(blocks.shape, BF), shape((16,) + tile, BF)),
        in_specs=[pl.BlockSpec(memory_space=pltpu.VMEM)] * 10,
        out_specs=[pl.BlockSpec(memory_space=pltpu.VMEM)] * 2,
        scratch_shapes=[
            pltpu.VMEM((seq, 2 * ROWS + 16), BF),
            pltpu.VMEM((seq, ROWS + 16), BF),
            pltpu.VMEM((ROWS, seq), BF),
            pltpu.VMEM((ROWS, seq), BF),
            pltpu.VMEM((seq, width), BF),
            pltpu.VMEM((seq, width), BF),
            pltpu.VMEM((seq, ROWS), F32),
            pltpu.VMEM((2, 4, 4, 2, 2) + tile, BF),
            pltpu.VMEM((2, 4, 4, 2) + tile, BF),
            pltpu.VMEM((3, 4, 2) + tile, BF),
            pltpu.VMEM((3, 4, 2) + tile, BF),
            pltpu.VMEM((3, 2) + tile, BF),
            pltpu.VMEM((3, 2) + tile, BF),
            pltpu.VMEM((2,) + tile, BF),
            pltpu.VMEM(tile, BF),
            pltpu.VMEM(tile, BF),
            pltpu.VMEM((15,) + tile, BF),
            dma((2, 4)),
            dma((2, 4)),
            dma((2, 3)),
            dma((2, 3)),
            dma((2, 3)),
            dma((2, 3)),
            dma((2,)),
            dma((2,)),
            dma((15,)),
            dma((15,)),
        ],
        compiler_params=pltpu.CompilerParams(
            vmem_limit_bytes=VMEM_BYTES, collective_id=0, has_side_effects=True
        ),
        cost_estimate=pl.CostEstimate(
            flops=10 * seq * seq * 128, bytes_accessed=16 * 2**20, transcendentals=0
        ),
    )(blocks, o_rows, lse, grads, *pairs)


def middle_body(
    attn_ref,
    hidden_in_ref,
    cot_ref,
    w_space_ref,
    w_qkv_ref,
    w_time_ref,
    g_out_ref,
    gh_ref,
    out_ref,
    attn_space_ref,
    hidden_ref,
    attn_time_ref,
    dqkv_ref,
    qkv_ref,
    ga_ref,
):
    frames, _, positions, _ = attn_ref.shape
    tokens = frames * positions
    width = HEADS * HD
    for h in range(HEADS):
        block = attn_ref[:, h].reshape(tokens, 128)
        attn_space_ref[:, h * HD : (h + 1) * HD] = block[:, :HD]
    cot = cot_ref[...].reshape(tokens, width)
    base = hidden_in_ref[...].reshape(tokens, width).astype(F32)
    hidden_ref[...] = (base + dot(attn_space_ref[...], w_space_ref[...])).astype(BF)
    for c in range(3):
        at = pl.ds(c * width, width)
        qkv_ref[:, at] = dot(hidden_ref[...], w_qkv_ref[:, at]).astype(BF)
    ga_ref[...] = dot_nt(cot, w_time_ref[...]).astype(BF)

    same = (
        lax.broadcasted_iota(jnp.int32, (tokens, tokens), 0) % positions
        == lax.broadcasted_iota(jnp.int32, (tokens, tokens), 1) % positions
    )
    for h in range(HEADS):
        lo, hi = h * HD, (h + 1) * HD
        q = qkv_ref[:, lo:hi]
        k = qkv_ref[:, width + lo : width + hi]
        v = qkv_ref[:, 2 * width + lo : 2 * width + hi]
        g = ga_ref[:, lo:hi]
        scores = jnp.where(same, dot_nt(q, k) * SCALE, -jnp.inf)
        exps = jnp.exp(scores - jnp.max(scores, axis=1, keepdims=True))
        probs = exps / jnp.sum(exps, axis=1, keepdims=True)
        probs_bf = probs.astype(BF)
        attn_time_ref[:, lo:hi] = dot(probs_bf, v).astype(BF)
        weighted = probs * dot_nt(g, v)
        ds = ((weighted - probs * jnp.sum(weighted, axis=1, keepdims=True)) * SCALE).astype(BF)
        dqkv_ref[:, lo:hi] = dot(ds, k).astype(BF)
        dqkv_ref[:, width + lo : width + hi] = dot_tn(ds, q).astype(BF)
        dqkv_ref[:, 2 * width + lo : 2 * width + hi] = dot_tn(probs_bf, g).astype(BF)

    gh_ref[...] = (cot.astype(F32) + dot_nt(dqkv_ref[...], w_qkv_ref[...])).astype(BF)
    ga_ref[...] = dot_nt(gh_ref[...], w_space_ref[...]).astype(BF)
    for h in range(HEADS):
        block = ga_ref[:, h * HD : (h + 1) * HD]
        filled = jnp.concatenate([block, jnp.zeros((tokens, 128 - HD), BF)], axis=1)
        g_out_ref[:, h] = filled.reshape(frames, positions, 128)
    out = hidden_ref[...].astype(F32) + dot(attn_time_ref[...], w_time_ref[...])
    out_ref[...] = out.astype(BF)


def middle(attn, hidden_in, cot, w_space_out, w_time_qkv, w_time_out):
    frames, _, positions, _ = attn.shape
    tokens = frames * positions
    width = HEADS * HD
    rows = shape((tokens, width), BF)
    wide = shape((tokens, 3 * width), BF)
    return kernel_call(
        middle_body,
        (shape(attn.shape, BF), rows, rows, rows, rows, rows, wide),
        [pltpu.VMEM((tokens, 3 * width), BF), pltpu.VMEM((tokens, width), BF)],
        2 * tokens * width * width * 10,
        20 * 2**20,
        (attn, hidden_in, cot, w_space_out, w_time_qkv, w_time_out),
    )


def exchange(blocks, axis):
    return lax.all_to_all(blocks, axis, split_axis=0, concat_axis=0, tiled=True)


def exchange_all(blocks):
    flat = exchange(blocks.reshape((-1,) + blocks.shape[2:]), ALL)
    return flat.reshape(blocks.shape)


def shards(
    hidden_in, query_space, key_space, value_space, cotangent, w_space_out, w_time_qkv, w_time_out
):
    tile_rows, width = hidden_in.shape[1:]
    frames = lax.axis_size("frame")
    positions = tile_rows // frames
    by_frame = (frames, positions, width)

    head_blocks = exchange(split_heads(query_space, key_space, value_space), "space")
    hidden_cols = exchange(hidden_in.reshape(by_frame), "frame")
    cot_cols = exchange(cotangent.reshape(by_frame), "frame")
    mixed, o_rows, lse = space_forward(head_blocks, frames)
    attn = exchange_all(mixed)
    g_out, grad_cols, out_cols, attn_space, hidden, attn_time, dqkv = middle(
        attn, hidden_cols, cot_cols, w_space_out, w_time_qkv, w_time_out
    )
    grads = exchange_all(g_out)
    pairs = (attn_space, hidden, attn_time, grad_cols, dqkv, cot_cols.reshape(-1, width))
    head_grads, sums = space_backward(head_blocks, o_rows, lse, grads, pairs)
    block_out = exchange(out_cols.reshape(by_frame), "frame").reshape(hidden_in.shape)
    grad_hidden = exchange(grad_cols.reshape(by_frame), "frame").reshape(hidden_in.shape)
    back = exchange(head_grads, "space")
    rows_dev = TILE_ROWS // HEADS
    own = lax.dynamic_slice_in_dim(sums, lax.axis_index("space") * rows_dev, rows_dev, 1)
    own = own.transpose(1, 0, 2).reshape(rows_dev, -1).astype(F32)
    cuts = (own[:, :width], own[:, width : 4 * width], own[:, 4 * width : 5 * width])
    return (block_out, grad_hidden, *join_heads(back), *cuts)


def solution(mesh):
    rows = P("frame", "space", None)
    weights = P(ALL, None)
    return jax.shard_map(
        shards,
        mesh=mesh,
        in_specs=(rows,) * 5 + (P(),) * 3,
        out_specs=(rows,) * 5 + (weights,) * 3,
        check_vma=False,
    )
```

```python
import jax
import jax.numpy as jnp
from jax import lax
from jax.experimental import pallas as pl
from jax.experimental.pallas import tpu as pltpu
from jax.sharding import PartitionSpec as P

HEADS = 16
HD = 72
ROWS = 80
SCALE = HD**-0.5
LOG2E = 1.4426950408889634
VMEM_BYTES = 62 * 2**20
BF = jnp.bfloat16
F32 = jnp.float32
ALL = ("frame", "space")


def kernel_call(body, out_shape, scratch_shapes, flops, moved, args):
    return pl.pallas_call(
        body,
        out_shape=out_shape,
        scratch_shapes=scratch_shapes,
        compiler_params=pltpu.CompilerParams(vmem_limit_bytes=VMEM_BYTES),
        cost_estimate=pl.CostEstimate(flops=flops, bytes_accessed=moved, transcendentals=0),
    )(*args)


def shape(dims, dtype):
    return jax.ShapeDtypeStruct(dims, dtype)


def dot(a, b):
    return jnp.dot(a, b, preferred_element_type=F32)


def dot_nt(a, b):
    return lax.dot_general(a, b, (((1,), (1,)), ((), ())), preferred_element_type=F32)


def dot_tn(a, b):
    return lax.dot_general(a, b, (((0,), (0,)), ((), ())), preferred_element_type=F32)


def two_parts(x):
    high = x.astype(BF)
    return [high, (x - high.astype(F32)).astype(BF)]


def three_parts_rows(x, rows):
    high = x.astype(BF).astype(F32)
    rest = x - high
    mid = rest.astype(BF).astype(F32)
    low = rest - mid
    at = lax.broadcasted_iota(jnp.int32, (rows, x.shape[1]), 0)
    return jnp.where(at == 0, high, jnp.where(at == 1, mid, jnp.where(at == 2, low, 0.0))).astype(BF)


def minus_rows(rows, columns):
    at = lax.broadcasted_iota(jnp.int32, (rows, columns), 0)
    return jnp.where(at < 3, -1.0, 0.0).astype(BF)


def split_heads(ref, out_ref, i):
    tokens = ref.shape[1]
    at = lax.broadcasted_iota(jnp.int32, (ROWS - HD, tokens), 0)
    fill = jnp.where(at == 0, 1.0 if i == 2 else 0.0, 0.0)
    flipped = ref[0].astype(F32).T
    for h in range(HEADS):
        block = jnp.concatenate([flipped[h * HD : (h + 1) * HD], fill], axis=0)
        out_ref[h, i] = block.astype(BF)


def join_heads_body(in_ref, q_ref, k_ref, v_ref):
    for i, ref in enumerate((q_ref, k_ref, v_ref)):
        blocks = [in_ref[h, i].astype(F32)[:HD] for h in range(HEADS)]
        ref[0] = jnp.concatenate(blocks, axis=0).T.astype(BF)


def join_heads(blocks):
    tokens = blocks.shape[3]
    rows = shape((1, tokens, HEADS * HD), BF)
    return kernel_call(
        join_heads_body, (rows, rows, rows), [], 0, 3 * tokens * HEADS * HD * 5, (blocks,)
    )


def copy_to(src, dst, send_sem, recv_sem, device):
    return pltpu.make_async_remote_copy(
        src_ref=src,
        dst_ref=dst,
        send_sem=send_sem,
        recv_sem=recv_sem,
        device_id=device,
        device_id_type=pl.DeviceIdType.MESH,
    )


def signal_all(barrier, peers):
    for peer in peers:
        pl.semaphore_signal(barrier, inc=1, device_id=peer, device_id_type=pl.DeviceIdType.MESH)


def rows_of(ref, i, count):
    return ref.at[pl.ds(pl.multiple_of(i * count, count), count)]


def scaled_query(block):
    return two_parts(block.astype(F32) * (SCALE * LOG2E))


def space_forward_body(
    q_ref,
    k_ref,
    v_ref,
    hidden_ref,
    cot_ref,
    x_ref,
    hidden_cols_ref,
    cot_cols_ref,
    o_ref,
    o_rows_ref,
    lse_ref,
    packed,
    k_nat,
    v_rows,
    s_one,
    s_two,
    send_x,
    recv_x,
    send_f,
    recv_f,
):
    blocks, _, _, width = x_ref.shape
    frames, positions, _ = hidden_cols_ref.shape
    seq = blocks * width
    frame, space = lax.axis_index("frame"), lax.axis_index("space")
    others = [lax.rem(space + i, blocks) for i in range(1, blocks)]
    other_frames = [lax.rem(frame + i, frames) for i in range(1, frames)]
    peers = [(frame, to) for to in others] + [(to, space) for to in other_frames]
    barrier = pltpu.get_barrier_semaphore()
    signal_all(barrier, peers)

    waits = []
    for i, ref in ((1, k_ref), (2, v_ref), (0, q_ref)):
        split_heads(ref, packed, i)
        if not waits:
            pl.semaphore_wait(barrier, len(peers))
        for n, to in enumerate(others):
            c = copy_to(
                packed.at[to, i],
                x_ref.at[space, i],
                send_x.at[i, n],
                recv_x.at[i, n],
                (frame, to),
            )
            c.start()
            waits.append(c)
        x_ref[space, i] = packed[space, i]
    moves = []
    for i, (ref, out) in enumerate(((hidden_ref, hidden_cols_ref), (cot_ref, cot_cols_ref))):
        for n, to in enumerate(other_frames):
            c = copy_to(
                rows_of(ref.at[0], to, positions),
                out.at[frame],
                send_f.at[i, n],
                recv_f.at[i, n],
                (to, space),
            )
            c.start()
            moves.append(c)
        out[frame] = rows_of(ref.at[0], frame, positions)[...]
    for c in waits[: 2 * len(others)]:
        c.wait()

    def prepare(j, _):
        at = pl.ds(pl.multiple_of(j * width, width), width)
        k_block = x_ref[j, 1]
        k_nat[at, :] = jnp.concatenate([k_block, k_block], axis=0).T
        v_rows[:, at] = x_ref[j, 2]
        return 0

    lax.fori_loop(0, blocks, prepare, 0)

    for c in waits[2 * len(others) :]:
        c.wait()

    def score(j, s_ref):
        q_block = jnp.concatenate(scaled_query(x_ref[j, 0]), axis=0)
        top = None
        for c in range(CHUNKS):
            at = slice(c * seq // CHUNKS, (c + 1) * seq // CHUNKS)
            s = dot(k_nat[at, :], q_block)
            s_ref[at, :] = s
            best = jnp.max(s, axis=0, keepdims=True)
            top = best if top is None else jnp.maximum(top, best)
        return top

    def both(j, s_ref, top, after, s_after):
        q_block = jnp.concatenate(scaled_query(x_ref[after, 0]), axis=0)
        top_after = None
        mixed = jnp.zeros((ROWS, width), F32)
        for c in range(CHUNKS):
            at = slice(c * seq // CHUNKS, (c + 1) * seq // CHUNKS)
            s = dot(k_nat[at, :], q_block)
            s_after[at, :] = s
            best = jnp.max(s, axis=0, keepdims=True)
            top_after = best if top_after is None else jnp.maximum(top_after, best)
            probs = jnp.exp2(s_ref[at, :] - top).astype(BF)
            mixed = mixed + dot(v_rows[:, at], probs)
        total = mixed[HD : HD + 1]
        mixed = mixed / total
        o_rows_ref[j] = mixed
        lse_ref[j] = jnp.broadcast_to(top + jnp.log2(total), (8, width))
        filled = jnp.concatenate([mixed[:HD], jnp.zeros((128 - HD, width), F32)], axis=0)
        o_ref[:, j] = filled.T.astype(BF).reshape(o_ref.shape[0], o_ref.shape[2], 128)
        return top_after

    def two_steps(i, top):
        j = 2 * i
        top = both(j, s_one, top, j + 1, s_two)
        return both(j + 1, s_two, top, jnp.minimum(j + 2, blocks - 1), s_one)

    lax.fori_loop(0, blocks // 2, two_steps, score(0, s_one))
    for c in moves:
        c.wait()


CHUNKS = 8


def space_forward(query, key_rows, value_rows, hidden_in, cot, frames):
    tokens, model = query.shape[1:]
    seq = HEADS * tokens
    dma = pltpu.SemaphoreType.DMA
    cols = shape((frames, tokens // frames, model), BF)
    return pl.pallas_call(
        space_forward_body,
        out_shape=(
            shape((HEADS, 3, ROWS, tokens), BF),
            cols,
            cols,
            shape((frames, HEADS, tokens // frames, 128), BF),
            shape((HEADS, ROWS, tokens), F32),
            shape((HEADS, 8, tokens), F32),
        ),
        in_specs=[pl.BlockSpec(memory_space=pltpu.VMEM)] * 5,
        out_specs=[pl.BlockSpec(memory_space=pltpu.VMEM)] * 6,
        scratch_shapes=[
            pltpu.VMEM((HEADS, 3, ROWS, tokens), BF),
            pltpu.VMEM((seq, 2 * ROWS), BF),
            pltpu.VMEM((ROWS, seq), BF),
            pltpu.VMEM((seq, tokens), F32),
            pltpu.VMEM((seq, tokens), F32),
            dma((3, HEADS - 1)),
            dma((3, HEADS - 1)),
            dma((2, frames - 1)),
            dma((2, frames - 1)),
        ],
        compiler_params=pltpu.CompilerParams(
            vmem_limit_bytes=VMEM_BYTES, collective_id=1, has_side_effects=True
        ),
        cost_estimate=pl.CostEstimate(
            flops=4 * seq * seq * 128, bytes_accessed=8 * 2**20, transcendentals=0
        ),
    )(query, key_rows, value_rows, hidden_in, cot)


Q_STEP = 1024
TILE_ROWS = 144
TILE_COLS = 384


def backward_prepare(x_ref, o_rows_ref, lse_ref, g_ref, q_aug, g_aug, q_rows, g_rows, dq_sum):
    blocks, _, _, width = x_ref.shape

    def prepare(j, _):
        at = pl.ds(pl.multiple_of(j * width, width), width)
        q_block = x_ref[j, 0]
        parts = scaled_query(q_block) + [three_parts_rows(lse_ref[j][:1], 16)]
        q_aug[at, :] = jnp.concatenate(parts, axis=0).T
        q_rows[:, at] = q_block
        g_block = g_ref[:, j].reshape(width, 128).astype(F32).T[:ROWS]
        inner = jnp.sum(g_block[:HD] * o_rows_ref[j][:HD], axis=0, keepdims=True)
        g_bf = g_block.astype(BF)
        g_rows[:, at] = g_bf
        g_aug[at, :] = jnp.concatenate([g_bf, three_parts_rows(inner, 16)], axis=0).T
        dq_sum[at, :] = jnp.zeros((width, ROWS), F32)
        return 0

    lax.fori_loop(0, blocks, prepare, 0)


def backward_steps(
    first, last, done, x_ref, out_ref, q_aug, g_aug, q_rows, g_rows, p_buf, ds_buf, dq_sum
):
    blocks, _, _, width = x_ref.shape
    seq = blocks * width

    def step(t, _):
        j = lax.rem(lax.axis_index("space") + 1 + t, blocks)
        k_block = x_ref[j, 1]
        v_block = x_ref[j, 2]
        k_aug = jnp.concatenate([k_block, k_block, minus_rows(16, width)], axis=0)
        v_aug = jnp.concatenate([v_block, minus_rows(16, width)], axis=0)
        k_nat = k_block.T

        for c in range(seq // Q_STEP):
            at = pl.ds(c * Q_STEP, Q_STEP)
            probs = jnp.exp2(dot(q_aug[at, :], k_aug))
            p_buf[at, :] = probs.astype(BF)
            ds = (probs * dot(g_aug[at, :], v_aug)).astype(BF)
            ds_buf[at, :] = ds
            dq_sum[at, :] += dot(ds, k_nat)

        out_ref[j, 1] = (dot(q_rows[...], ds_buf[...]) * SCALE).astype(BF)
        out_ref[j, 2] = dot(g_rows[...], p_buf[...]).astype(BF)
        done(t, last)
        return 0

    lax.fori_loop(first, last, step, 0)


def add_into(target, terms, lead):
    count = 1
    for n in lead:
        count *= n

    def one(i, _):
        index = []
        for n in reversed(lead):
            index.insert(0, lax.rem(i, n))
            i = lax.div(i, n)
        total = target(*index)[...].astype(F32)
        for term in terms:
            total = total + term(*index)[...].astype(F32)
        target(*index)[...] = total.astype(BF)
        return 0

    lax.fori_loop(0, count, one, 0)


def space_backward_body(
    x_ref,
    o_rows_ref,
    lse_ref,
    g_ref,
    attn_space_ref,
    hidden_ref,
    attn_time_ref,
    gh_ref,
    dqkv_ref,
    cot_ref,
    out_cols_ref,
    back_ref,
    sums_ref,
    grad_hidden_ref,
    block_out_ref,
    out_ref,
    q_aug,
    g_aug,
    q_rows,
    g_rows,
    p_buf,
    ds_buf,
    dq_sum,
    terms,
    half,
    x_in_a,
    z_in_b,
    z_in_a,
    x_in_b,
    lo_in,
    hi_in,
    mine,
    send1,
    recv1,
    send2,
    recv2,
    send3,
    recv3,
    send4,
    recv4,
    send6,
    recv6,
    send_f,
    recv_f,
    send_kv,
    recv_kv,
    send_q,
    recv_q,
):
    frame, space = lax.axis_index("frame"), lax.axis_index("space")
    z, lo = lax.div(frame, 2), lax.rem(frame, 2)
    x, hi, core = lax.div(space, 4), lax.rem(lax.div(space, 2), 2), lax.rem(space, 2)

    def x_peer(i):
        return (frame, lax.rem(x + i, 4) * 4 + hi * 2 + core)

    def z_peer(i):
        return (lax.rem(z + i, 4) * 2 + lo, space)

    def space_peer(i):
        return (frame, lax.rem(space + i, 16))

    lo_peer = (z * 2 + 1 - lo, space)
    hi_peer = (frame, x * 4 + (1 - hi) * 2 + core)
    core_peer = (frame, x * 4 + hi * 2 + 1 - core)

    copy = copy_to
    others = [lax.rem(space + i, 16) for i in range(1, 16)]
    other_frames = [lax.rem(frame + i, 8) for i in range(1, 8)]
    peers = [(frame, to) for to in others] + [(to, space) for to in other_frames]
    barrier = pltpu.get_barrier_semaphore()
    signal_all(barrier, peers)

    for t, (rows_ref, grads_ref, offset) in enumerate(
        [(attn_space_ref, gh_ref, c) for c in range(3)]
        + [(hidden_ref, dqkv_ref, c) for c in range(9)]
        + [(attn_time_ref, cot_ref, c) for c in range(3)]
    ):
        part = dot_tn(rows_ref[...], grads_ref[:, offset * TILE_COLS : (offset + 1) * TILE_COLS])
        part = part.astype(BF)
        for f in range(8):
            rows = part[f * TILE_ROWS : (f + 1) * TILE_ROWS]
            terms[f % 2, f // 2, t // 4, t // 2 % 2, t % 2] = rows
    for f in range(8):
        terms[f % 2, f // 2, 3, 1, 1] = jnp.zeros((TILE_ROWS, TILE_COLS), BF)

    pl.semaphore_wait(barrier, len(peers))

    first = [
        copy(
            terms.at[y, w, :, :, 1 - core],
            half.at[y, w],
            send1.at[y, w],
            recv1.at[y, w],
            core_peer,
        )
        for y in range(2)
        for w in range(4)
    ]
    for c in first:
        c.start()
    moves = []
    for i, (ref, out) in enumerate(((gh_ref, grad_hidden_ref), (out_cols_ref, block_out_ref))):
        positions = out.shape[1]
        for n, to in enumerate(other_frames):
            c = copy(
                rows_of(ref, to, positions),
                out.at[frame],
                send_f.at[i, n],
                recv_f.at[i, n],
                (to, space),
            )
            c.start()
            moves.append(c)
        out[frame] = rows_of(ref, frame, positions)[...]

    state = (q_aug, g_aug, q_rows, g_rows)
    backward_prepare(x_ref, o_rows_ref, lse_ref, g_ref, *state, dq_sum)

    def attend(start, stop):
        backward_steps(start, stop, send_step, x_ref, out_ref, *state, p_buf, ds_buf, dq_sum)

    def key_grads(t):
        to = lax.rem(space + 1 + t, 16)
        return copy(
            out_ref.at[to, pl.ds(1, 2)],
            back_ref.at[space, pl.ds(1, 2)],
            send_kv.at[t],
            recv_kv.at[t],
            (frame, to),
        )

    def query_grads(t):
        to = lax.rem(space + 1 + t, 16)
        return copy(
            out_ref.at[to, 0], back_ref.at[space, 0], send_q.at[t], recv_q.at[t], (frame, to)
        )

    def send_step(t, stop):
        if stop < 16:
            key_grads(t).start()

    attend(0, STAGES[0])

    for c in first:
        c.wait()
    add_into(
        lambda y, w, a, b: half.at[y, w, a, b],
        [lambda y, w, a, b: terms.at[y, w, a, b, core]],
        (2, 4, 4, 2),
    )
    second = []
    for i in range(1, 4):
        to_x, to_z = lax.rem(x + i, 4), lax.rem(z + i, 4)
        s = i - 1
        second.append(
            copy(half.at[0, :, to_x], x_in_a.at[s], send2.at[0, s], recv2.at[0, s], x_peer(i))
        )
        second.append(
            copy(half.at[1, to_z], z_in_b.at[s], send2.at[1, s], recv2.at[1, s], z_peer(i))
        )
    for c in second:
        c.start()

    attend(STAGES[0], STAGES[1])

    for c in second:
        c.wait()
    add_into(
        lambda w, b: half.at[0, w, x, b],
        [lambda w, b, s=s: x_in_a.at[s, w, b] for s in range(3)],
        (4, 2),
    )
    add_into(
        lambda a, b: half.at[1, z, a, b],
        [lambda a, b, s=s: z_in_b.at[s, a, b] for s in range(3)],
        (4, 2),
    )
    third = []
    for i in range(1, 4):
        to_x, to_z = lax.rem(x + i, 4), lax.rem(z + i, 4)
        s = i - 1
        third.append(
            copy(half.at[0, to_z, x], z_in_a.at[s], send3.at[0, s], recv3.at[0, s], z_peer(i))
        )
        third.append(
            copy(half.at[1, z, to_x], x_in_b.at[s], send3.at[1, s], recv3.at[1, s], x_peer(i))
        )
    for c in third:
        c.start()

    attend(STAGES[1], STAGES[2])

    for c in third:
        c.wait()
    add_into(
        lambda b: half.at[0, z, x, b], [lambda b, s=s: z_in_a.at[s, b] for s in range(3)], (2,)
    )
    add_into(
        lambda b: half.at[1, z, x, b], [lambda b, s=s: x_in_b.at[s, b] for s in range(3)], (2,)
    )
    fourth = copy(half.at[1 - lo, z, x], lo_in, send4.at[0], recv4.at[0], lo_peer)
    fourth.start()

    attend(STAGES[2], STAGES[3])

    fourth.wait()
    add_into(lambda b: half.at[lo, z, x, b], [lambda b: lo_in.at[b]], (2,))
    fifth = copy(half.at[lo, z, x, 1 - hi], hi_in, send4.at[1], recv4.at[1], hi_peer)
    fifth.start()

    attend(STAGES[3], 15)
    attend(15, 16)

    fifth.wait()
    total = (half[lo, z, x, hi].astype(F32) + hi_in[...].astype(F32)).astype(BF)
    mine[...] = total
    sixth = [
        copy(mine, sums_ref.at[space], send6.at[i - 1], recv6.at[i - 1], space_peer(i))
        for i in range(1, 16)
    ]
    for c in sixth:
        c.start()
    sums_ref[space] = total

    def finish(t, _):
        to = lax.rem(space + 1 + t, 16)
        at = pl.ds(pl.multiple_of(to * width, width), width)
        out_ref[to, 0] = (dq_sum[at, :] * SCALE).T.astype(BF)

        @pl.when(t < 15)
        def _():
            query_grads(t).start()

        return 0

    width = x_ref.shape[3]
    lax.fori_loop(0, 16, finish, 0)
    back_ref[space] = out_ref[space]
    for c in moves + sixth:
        c.wait()
    for t in range(15):
        key_grads(t).wait()
        query_grads(t).wait()


STAGES = (3, 10, 13, 15)


def space_backward(blocks, o_rows, lse, grads, pairs):
    count, _, _, width = blocks.shape
    seq = count * width
    tile = (TILE_ROWS, TILE_COLS)
    by_frame = shape((8, width // 8, HEADS * HD), BF)
    dma = pltpu.SemaphoreType.DMA
    return pl.pallas_call(
        space_backward_body,
        out_shape=(shape(blocks.shape, BF), shape((16,) + tile, BF), by_frame, by_frame),
        in_specs=[pl.BlockSpec(memory_space=pltpu.VMEM)] * 11,
        out_specs=[pl.BlockSpec(memory_space=pltpu.VMEM)] * 4,
        scratch_shapes=[
            pltpu.VMEM(blocks.shape, BF),
            pltpu.VMEM((seq, 2 * ROWS + 16), BF),
            pltpu.VMEM((seq, ROWS + 16), BF),
            pltpu.VMEM((ROWS, seq), BF),
            pltpu.VMEM((ROWS, seq), BF),
            pltpu.VMEM((seq, width), BF),
            pltpu.VMEM((seq, width), BF),
            pltpu.VMEM((seq, ROWS), F32),
            pltpu.VMEM((2, 4, 4, 2, 2) + tile, BF),
            pltpu.VMEM((2, 4, 4, 2) + tile, BF),
            pltpu.VMEM((3, 4, 2) + tile, BF),
            pltpu.VMEM((3, 4, 2) + tile, BF),
            pltpu.VMEM((3, 2) + tile, BF),
            pltpu.VMEM((3, 2) + tile, BF),
            pltpu.VMEM((2,) + tile, BF),
            pltpu.VMEM(tile, BF),
            pltpu.VMEM(tile, BF),
            dma((2, 4)),
            dma((2, 4)),
            dma((2, 3)),
            dma((2, 3)),
            dma((2, 3)),
            dma((2, 3)),
            dma((2,)),
            dma((2,)),
            dma((15,)),
            dma((15,)),
            dma((2, 7)),
            dma((2, 7)),
            dma((15,)),
            dma((15,)),
            dma((15,)),
            dma((15,)),
        ],
        compiler_params=pltpu.CompilerParams(
            vmem_limit_bytes=VMEM_BYTES, collective_id=0, has_side_effects=True
        ),
        cost_estimate=pl.CostEstimate(
            flops=10 * seq * seq * 128, bytes_accessed=16 * 2**20, transcendentals=0
        ),
    )(blocks, o_rows, lse, grads, *pairs)


def middle_body(
    attn_ref,
    hidden_in_ref,
    cot_ref,
    w_space_ref,
    w_qkv_ref,
    w_time_ref,
    g_out_ref,
    gh_ref,
    out_ref,
    attn_space_ref,
    hidden_ref,
    attn_time_ref,
    dqkv_ref,
    qkv_ref,
    ga_ref,
):
    frames, _, positions, _ = attn_ref.shape
    tokens = frames * positions
    width = HEADS * HD
    for h in range(HEADS):
        block = attn_ref[:, h].reshape(tokens, 128)
        attn_space_ref[:, h * HD : (h + 1) * HD] = block[:, :HD]
    cot = cot_ref[...].reshape(tokens, width)
    base = hidden_in_ref[...].reshape(tokens, width).astype(F32)
    hidden_ref[...] = (base + dot(attn_space_ref[...], w_space_ref[...])).astype(BF)
    for c in range(3):
        at = pl.ds(c * width, width)
        qkv_ref[:, at] = dot(hidden_ref[...], w_qkv_ref[:, at]).astype(BF)
    ga_ref[...] = dot_nt(cot, w_time_ref[...]).astype(BF)

    same = (
        lax.broadcasted_iota(jnp.int32, (tokens, tokens), 0) % positions
        == lax.broadcasted_iota(jnp.int32, (tokens, tokens), 1) % positions
    )
    for h in range(HEADS):
        lo, hi = h * HD, (h + 1) * HD
        q = qkv_ref[:, lo:hi]
        k = qkv_ref[:, width + lo : width + hi]
        v = qkv_ref[:, 2 * width + lo : 2 * width + hi]
        g = ga_ref[:, lo:hi]
        scores = jnp.where(same, dot_nt(q, k) * SCALE, -jnp.inf)
        exps = jnp.exp(scores - jnp.max(scores, axis=1, keepdims=True))
        probs = exps / jnp.sum(exps, axis=1, keepdims=True)
        probs_bf = probs.astype(BF)
        attn_time_ref[:, lo:hi] = dot(probs_bf, v).astype(BF)
        weighted = probs * dot_nt(g, v)
        ds = ((weighted - probs * jnp.sum(weighted, axis=1, keepdims=True)) * SCALE).astype(BF)
        dqkv_ref[:, lo:hi] = dot(ds, k).astype(BF)
        dqkv_ref[:, width + lo : width + hi] = dot_tn(ds, q).astype(BF)
        dqkv_ref[:, 2 * width + lo : 2 * width + hi] = dot_tn(probs_bf, g).astype(BF)

    gh_ref[...] = (cot.astype(F32) + dot_nt(dqkv_ref[...], w_qkv_ref[...])).astype(BF)
    ga_ref[...] = dot_nt(gh_ref[...], w_space_ref[...]).astype(BF)
    for h in range(HEADS):
        block = ga_ref[:, h * HD : (h + 1) * HD]
        filled = jnp.concatenate([block, jnp.zeros((tokens, 128 - HD), BF)], axis=1)
        g_out_ref[:, h] = filled.reshape(frames, positions, 128)
    out = hidden_ref[...].astype(F32) + dot(attn_time_ref[...], w_time_ref[...])
    out_ref[...] = out.astype(BF)


def middle(attn, hidden_in, cot, w_space_out, w_time_qkv, w_time_out):
    frames, _, positions, _ = attn.shape
    tokens = frames * positions
    width = HEADS * HD
    rows = shape((tokens, width), BF)
    wide = shape((tokens, 3 * width), BF)
    return kernel_call(
        middle_body,
        (shape(attn.shape, BF), rows, rows, rows, rows, rows, wide),
        [pltpu.VMEM((tokens, 3 * width), BF), pltpu.VMEM((tokens, width), BF)],
        2 * tokens * width * width * 10,
        20 * 2**20,
        (attn, hidden_in, cot, w_space_out, w_time_qkv, w_time_out),
    )


def exchange(blocks, axis):
    return lax.all_to_all(blocks, axis, split_axis=0, concat_axis=0, tiled=True)


def exchange_all(blocks):
    flat = exchange(blocks.reshape((-1,) + blocks.shape[2:]), ALL)
    return flat.reshape(blocks.shape)


def shards(
    hidden_in, query_space, key_space, value_space, cotangent, w_space_out, w_time_qkv, w_time_out
):
    width = hidden_in.shape[2]
    frames = lax.axis_size("frame")
    head_blocks, hidden_cols, cot_cols, mixed, o_rows, lse = space_forward(
        query_space, key_space, value_space, hidden_in, cotangent, frames
    )
    attn = exchange_all(mixed)
    g_out, grad_cols, out_cols, attn_space, hidden, attn_time, dqkv = middle(
        attn, hidden_cols, cot_cols, w_space_out, w_time_qkv, w_time_out
    )
    grads = exchange_all(g_out)
    pairs = (attn_space, hidden, attn_time, grad_cols, dqkv, cot_cols.reshape(-1, width), out_cols)
    back, sums, grad_hidden, block_out = space_backward(head_blocks, o_rows, lse, grads, pairs)
    block_out = block_out.reshape(hidden_in.shape)
    grad_hidden = grad_hidden.reshape(hidden_in.shape)
    rows_dev = TILE_ROWS // HEADS
    own = lax.dynamic_slice_in_dim(sums, lax.axis_index("space") * rows_dev, rows_dev, 1)
    own = own.transpose(1, 0, 2).reshape(rows_dev, -1).astype(F32)
    cuts = (own[:, :width], own[:, width : 4 * width], own[:, 4 * width : 5 * width])
    return (block_out, grad_hidden, *join_heads(back), *cuts)


def solution(mesh):
    rows = P("frame", "space", None)
    weights = P(ALL, None)
    return jax.shard_map(
        shards,
        mesh=mesh,
        in_specs=(rows,) * 5 + (P(),) * 3,
        out_specs=(rows,) * 5 + (weights,) * 3,
        check_vma=False,
    )
```

```python
import jax
import jax.numpy as jnp
from jax import lax
from jax.experimental import pallas as pl
from jax.experimental.pallas import tpu as pltpu
from jax.sharding import PartitionSpec as P

HEADS = 16
HD = 72
ROWS = 80
SCALE = HD**-0.5
LOG2E = 1.4426950408889634
VMEM_BYTES = 62 * 2**20
BF = jnp.bfloat16
F32 = jnp.float32
ALL = ("frame", "space")


def kernel_call(body, out_shape, scratch_shapes, flops, moved, args):
    return pl.pallas_call(
        body,
        out_shape=out_shape,
        scratch_shapes=scratch_shapes,
        compiler_params=pltpu.CompilerParams(vmem_limit_bytes=VMEM_BYTES),
        cost_estimate=pl.CostEstimate(flops=flops, bytes_accessed=moved, transcendentals=0),
    )(*args)


def shape(dims, dtype):
    return jax.ShapeDtypeStruct(dims, dtype)


def dot(a, b):
    return jnp.dot(a, b, preferred_element_type=F32)


def dot_nt(a, b):
    return lax.dot_general(a, b, (((1,), (1,)), ((), ())), preferred_element_type=F32)


def dot_tn(a, b):
    return lax.dot_general(a, b, (((0,), (0,)), ((), ())), preferred_element_type=F32)


def two_parts(x):
    high = x.astype(BF)
    return [high, (x - high.astype(F32)).astype(BF)]


def three_parts_rows(x, rows):
    high = x.astype(BF).astype(F32)
    rest = x - high
    mid = rest.astype(BF).astype(F32)
    low = rest - mid
    at = lax.broadcasted_iota(jnp.int32, (rows, x.shape[1]), 0)
    return jnp.where(at == 0, high, jnp.where(at == 1, mid, jnp.where(at == 2, low, 0.0))).astype(BF)


def minus_rows(rows, columns):
    at = lax.broadcasted_iota(jnp.int32, (rows, columns), 0)
    return jnp.where(at < 3, -1.0, 0.0).astype(BF)


def split_heads(ref, out_ref, i):
    tokens = ref.shape[1]
    at = lax.broadcasted_iota(jnp.int32, (ROWS - HD, tokens), 0)
    fill = jnp.where(at == 0, 1.0 if i == 2 else 0.0, 0.0)
    flipped = ref[0].astype(F32).T
    for h in range(HEADS):
        block = jnp.concatenate([flipped[h * HD : (h + 1) * HD], fill], axis=0)
        out_ref[h, i] = block.astype(BF)


def join_heads_body(in_ref, q_ref, k_ref, v_ref):
    for i, ref in enumerate((q_ref, k_ref, v_ref)):
        blocks = [in_ref[h, i].astype(F32)[:HD] for h in range(HEADS)]
        ref[0] = jnp.concatenate(blocks, axis=0).T.astype(BF)


def join_heads(blocks):
    tokens = blocks.shape[3]
    rows = shape((1, tokens, HEADS * HD), BF)
    return kernel_call(
        join_heads_body, (rows, rows, rows), [], 0, 3 * tokens * HEADS * HD * 5, (blocks,)
    )


def copy_to(src, dst, send_sem, recv_sem, device):
    return pltpu.make_async_remote_copy(
        src_ref=src,
        dst_ref=dst,
        send_sem=send_sem,
        recv_sem=recv_sem,
        device_id=device,
        device_id_type=pl.DeviceIdType.MESH,
    )


def signal_all(barrier, peers):
    for peer in peers:
        pl.semaphore_signal(barrier, inc=1, device_id=peer, device_id_type=pl.DeviceIdType.MESH)


def rows_of(ref, i, count):
    return ref.at[pl.ds(pl.multiple_of(i * count, count), count)]


def scaled_query(block):
    return two_parts(block.astype(F32) * (SCALE * LOG2E))


def space_forward_body(
    q_ref,
    k_ref,
    v_ref,
    hidden_ref,
    cot_ref,
    x_ref,
    hidden_cols_ref,
    cot_cols_ref,
    attn_ref,
    o_rows_ref,
    lse_ref,
    packed,
    o_buf,
    heads_in,
    k_nat,
    v_rows,
    s_one,
    s_two,
    send_x,
    recv_x,
    send_f,
    recv_f,
    send_o,
    recv_o,
    send_a,
    recv_a,
):
    blocks, _, _, width = x_ref.shape
    frames, positions, _ = hidden_cols_ref.shape
    seq = blocks * width
    frame, space = lax.axis_index("frame"), lax.axis_index("space")
    others = [lax.rem(space + i, blocks) for i in range(1, blocks)]
    other_frames = [lax.rem(frame + i, frames) for i in range(1, frames)]
    peers = [(frame, to) for to in others] + [(to, space) for to in other_frames]
    barrier = pltpu.get_barrier_semaphore()
    signal_all(barrier, peers)

    waits = []
    for i, ref in ((1, k_ref), (2, v_ref), (0, q_ref)):
        split_heads(ref, packed, i)
        if not waits:
            pl.semaphore_wait(barrier, len(peers))
        for n, to in enumerate(others):
            c = copy_to(
                packed.at[to, i],
                x_ref.at[space, i],
                send_x.at[i, n],
                recv_x.at[i, n],
                (frame, to),
            )
            c.start()
            waits.append(c)
        x_ref[space, i] = packed[space, i]
    moves = []
    for i, (ref, out) in enumerate(((hidden_ref, hidden_cols_ref), (cot_ref, cot_cols_ref))):
        for n, to in enumerate(other_frames):
            c = copy_to(
                rows_of(ref.at[0], to, positions),
                out.at[frame],
                send_f.at[i, n],
                recv_f.at[i, n],
                (to, space),
            )
            c.start()
            moves.append(c)
        out[frame] = rows_of(ref.at[0], frame, positions)[...]
    for c in waits[: 2 * len(others)]:
        c.wait()

    def prepare(j, _):
        at = pl.ds(pl.multiple_of(j * width, width), width)
        k_block = x_ref[j, 1]
        k_nat[at, :] = jnp.concatenate([k_block, k_block], axis=0).T
        v_rows[:, at] = x_ref[j, 2]
        return 0

    lax.fori_loop(0, blocks, prepare, 0)

    for c in waits[2 * len(others) :]:
        c.wait()

    def score(j, s_ref):
        q_block = jnp.concatenate(scaled_query(x_ref[j, 0]), axis=0)
        top = None
        for c in range(CHUNKS):
            at = slice(c * seq // CHUNKS, (c + 1) * seq // CHUNKS)
            s = dot(k_nat[at, :], q_block)
            s_ref[at, :] = s
            best = jnp.max(s, axis=0, keepdims=True)
            top = best if top is None else jnp.maximum(top, best)
        return top

    def block_at(t):
        return lax.rem(space + 1 + t, blocks)

    def send_block(t):
        to = block_at(t)
        return copy_to(
            o_buf.at[to], heads_in.at[space], send_o.at[t], recv_o.at[t], (frame, to)
        )

    def both(t, s_ref, top, t_after, s_after):
        j, after = block_at(t), block_at(t_after)
        q_block = jnp.concatenate(scaled_query(x_ref[after, 0]), axis=0)
        top_after = None
        mixed = jnp.zeros((ROWS, width), F32)
        for c in range(CHUNKS):
            at = slice(c * seq // CHUNKS, (c + 1) * seq // CHUNKS)
            s = dot(k_nat[at, :], q_block)
            s_after[at, :] = s
            best = jnp.max(s, axis=0, keepdims=True)
            top_after = best if top_after is None else jnp.maximum(top_after, best)
            probs = jnp.exp2(s_ref[at, :] - top).astype(BF)
            mixed = mixed + dot(v_rows[:, at], probs)
        total = mixed[HD : HD + 1]
        mixed = mixed / total
        o_rows_ref[j] = mixed
        lse_ref[j] = jnp.broadcast_to(top + jnp.log2(total), (8, width))
        filled = jnp.concatenate([mixed[:HD], jnp.zeros((128 - HD, width), F32)], axis=0)
        o_buf[j] = filled.T.astype(BF).reshape(frames, positions, 128)

        @pl.when(t < blocks - 1)
        def _():
            send_block(t).start()

        return top_after

    def two_steps(i, top):
        j = 2 * i
        top = both(j, s_one, top, j + 1, s_two)
        return both(j + 1, s_two, top, jnp.minimum(j + 2, blocks - 1), s_one)

    lax.fori_loop(0, blocks // 2, two_steps, score(block_at(0), s_one))
    heads_in[space] = o_buf[space]
    for t in range(blocks - 1):
        send_block(t).wait()
    for n, to in enumerate(other_frames):
        c = copy_to(
            heads_in.at[:, to], attn_ref.at[frame], send_a.at[n], recv_a.at[n], (to, space)
        )
        c.start()
        moves.append(c)
    attn_ref[frame] = heads_in[:, frame]
    for c in moves:
        c.wait()


CHUNKS = 8


def space_forward(query, key_rows, value_rows, hidden_in, cot, frames):
    tokens, model = query.shape[1:]
    seq = HEADS * tokens
    dma = pltpu.SemaphoreType.DMA
    cols = shape((frames, tokens // frames, model), BF)
    return pl.pallas_call(
        space_forward_body,
        out_shape=(
            shape((HEADS, 3, ROWS, tokens), BF),
            cols,
            cols,
            shape((frames, HEADS, tokens // frames, 128), BF),
            shape((HEADS, ROWS, tokens), F32),
            shape((HEADS, 8, tokens), F32),
        ),
        in_specs=[pl.BlockSpec(memory_space=pltpu.VMEM)] * 5,
        out_specs=[pl.BlockSpec(memory_space=pltpu.VMEM)] * 6,
        scratch_shapes=[
            pltpu.VMEM((HEADS, 3, ROWS, tokens), BF),
            pltpu.VMEM((HEADS, frames, tokens // frames, 128), BF),
            pltpu.VMEM((HEADS, frames, tokens // frames, 128), BF),
            pltpu.VMEM((seq, 2 * ROWS), BF),
            pltpu.VMEM((ROWS, seq), BF),
            pltpu.VMEM((seq, tokens), F32),
            pltpu.VMEM((seq, tokens), F32),
            dma((3, HEADS - 1)),
            dma((3, HEADS - 1)),
            dma((2, frames - 1)),
            dma((2, frames - 1)),
            dma((HEADS - 1,)),
            dma((HEADS - 1,)),
            dma((frames - 1,)),
            dma((frames - 1,)),
        ],
        compiler_params=pltpu.CompilerParams(
            vmem_limit_bytes=VMEM_BYTES, collective_id=1, has_side_effects=True
        ),
        cost_estimate=pl.CostEstimate(
            flops=4 * seq * seq * 128, bytes_accessed=8 * 2**20, transcendentals=0
        ),
    )(query, key_rows, value_rows, hidden_in, cot)


Q_STEP = 1024
TILE_ROWS = 144
TILE_COLS = 384


def backward_prepare(x_ref, o_rows_ref, lse_ref, g_ref, q_aug, g_aug, q_rows, g_rows, dq_sum):
    blocks, _, _, width = x_ref.shape

    def prepare(j, _):
        at = pl.ds(pl.multiple_of(j * width, width), width)
        q_block = x_ref[j, 0]
        parts = scaled_query(q_block) + [three_parts_rows(lse_ref[j][:1], 16)]
        q_aug[at, :] = jnp.concatenate(parts, axis=0).T
        q_rows[:, at] = q_block
        g_block = g_ref[:, j].reshape(width, 128).astype(F32).T[:ROWS]
        inner = jnp.sum(g_block[:HD] * o_rows_ref[j][:HD], axis=0, keepdims=True)
        g_bf = g_block.astype(BF)
        g_rows[:, at] = g_bf
        g_aug[at, :] = jnp.concatenate([g_bf, three_parts_rows(inner, 16)], axis=0).T
        dq_sum[at, :] = jnp.zeros((width, ROWS), F32)
        return 0

    lax.fori_loop(0, blocks, prepare, 0)


def backward_steps(
    first, last, done, x_ref, out_ref, q_aug, g_aug, q_rows, g_rows, p_buf, ds_buf, dq_sum
):
    blocks, _, _, width = x_ref.shape
    seq = blocks * width

    def step(t, _):
        j = lax.rem(lax.axis_index("space") + 1 + t, blocks)
        k_block = x_ref[j, 1]
        v_block = x_ref[j, 2]
        k_aug = jnp.concatenate([k_block, k_block, minus_rows(16, width)], axis=0)
        v_aug = jnp.concatenate([v_block, minus_rows(16, width)], axis=0)
        k_nat = k_block.T

        for c in range(seq // Q_STEP):
            at = pl.ds(c * Q_STEP, Q_STEP)
            probs = jnp.exp2(dot(q_aug[at, :], k_aug))
            p_buf[at, :] = probs.astype(BF)
            ds = (probs * dot(g_aug[at, :], v_aug)).astype(BF)
            ds_buf[at, :] = ds
            dq_sum[at, :] += dot(ds, k_nat)

        out_ref[j, 1] = (dot(q_rows[...], ds_buf[...]) * SCALE).astype(BF)
        out_ref[j, 2] = dot(g_rows[...], p_buf[...]).astype(BF)
        done(t, last)
        return 0

    lax.fori_loop(first, last, step, 0)


OWN_ROWS = 9
WINDOW = 32


def window_start(space):
    return jnp.minimum(lax.div(space * OWN_ROWS, 16) * 16, TILE_ROWS - WINDOW)


def window(space):
    return pl.ds(pl.multiple_of(window_start(space), 16), WINDOW)


def add_into(target, terms, lead):
    count = 1
    for n in lead:
        count *= n

    def one(i, _):
        index = []
        for n in reversed(lead):
            index.insert(0, lax.rem(i, n))
            i = lax.div(i, n)
        total = target(*index)[...].astype(F32)
        for term in terms:
            total = total + term(*index)[...].astype(F32)
        target(*index)[...] = total.astype(BF)
        return 0

    lax.fori_loop(0, count, one, 0)


def space_backward_body(
    x_ref,
    o_rows_ref,
    lse_ref,
    g_out_ref,
    attn_space_ref,
    hidden_ref,
    attn_time_ref,
    gh_ref,
    dqkv_ref,
    cot_ref,
    out_cols_ref,
    back_ref,
    sums_ref,
    grad_hidden_ref,
    block_out_ref,
    out_ref,
    g_mid,
    g_ref,
    rows_t,
    q_aug,
    g_aug,
    q_rows,
    g_rows,
    p_buf,
    ds_buf,
    dq_sum,
    terms,
    half,
    x_in_a,
    z_in_b,
    z_in_a,
    x_in_b,
    lo_in,
    hi_in,
    mine,
    send1,
    recv1,
    send2,
    recv2,
    send3,
    recv3,
    send4,
    recv4,
    send6,
    recv6,
    send_f,
    recv_f,
    send_kv,
    recv_kv,
    send_q,
    recv_q,
    send_g,
    recv_g,
    send_h,
    recv_h,
):
    frame, space = lax.axis_index("frame"), lax.axis_index("space")
    z, lo = lax.div(frame, 2), lax.rem(frame, 2)
    x, hi, core = lax.div(space, 4), lax.rem(lax.div(space, 2), 2), lax.rem(space, 2)

    def x_peer(i):
        return (frame, lax.rem(x + i, 4) * 4 + hi * 2 + core)

    def z_peer(i):
        return (lax.rem(z + i, 4) * 2 + lo, space)

    def space_peer(i):
        return (frame, lax.rem(space + i, 16))

    lo_peer = (z * 2 + 1 - lo, space)
    hi_peer = (frame, x * 4 + (1 - hi) * 2 + core)
    core_peer = (frame, x * 4 + hi * 2 + 1 - core)

    copy = copy_to
    others = [lax.rem(space + i, 16) for i in range(1, 16)]
    other_frames = [lax.rem(frame + i, 8) for i in range(1, 8)]
    peers = [(frame, to) for to in others] + [(to, space) for to in other_frames]
    barrier = pltpu.get_barrier_semaphore()
    signal_all(barrier, peers)

    pl.semaphore_wait(barrier, len(peers))
    to_frames = [
        copy(g_out_ref.at[to], g_mid.at[frame], send_g.at[n], recv_g.at[n], (to, space))
        for n, to in enumerate(other_frames)
    ]
    for c in to_frames:
        c.start()
    g_mid[frame] = g_out_ref[frame]

    for rows_ref, grads_ref, begin, tiles in (
        (attn_space_ref, gh_ref, 0, 3),
        (hidden_ref, dqkv_ref, 3, 9),
        (attn_time_ref, cot_ref, 12, 3),
    ):
        rows_t[...] = rows_ref[...].T
        for n in range(tiles):
            t = begin + n
            part = dot(rows_t[...], grads_ref[:, n * TILE_COLS : (n + 1) * TILE_COLS]).astype(BF)
            for f in range(8):
                rows = part[f * TILE_ROWS : (f + 1) * TILE_ROWS]
                terms[f % 2, f // 2, t // 4, t // 2 % 2, t % 2] = rows
    for f in range(8):
        terms[f % 2, f // 2, 3, 1, 1] = jnp.zeros((TILE_ROWS, TILE_COLS), BF)

    first = [
        copy(
            terms.at[y, w, :, :, 1 - core],
            half.at[y, w],
            send1.at[y, w],
            recv1.at[y, w],
            core_peer,
        )
        for y in range(2)
        for w in range(4)
    ]
    for c in first:
        c.start()
    for c in to_frames:
        c.wait()
    to_heads = [
        copy(g_mid.at[:, to], g_ref.at[:, space], send_h.at[n], recv_h.at[n], (frame, to))
        for n, to in enumerate(others)
    ]
    for c in to_heads:
        c.start()
    g_ref[:, space] = g_mid[:, space]

    state = (q_aug, g_aug, q_rows, g_rows)
    def attend(start, stop):
        backward_steps(start, stop, send_step, x_ref, out_ref, *state, p_buf, ds_buf, dq_sum)

    def key_grads(t):
        to = lax.rem(space + 1 + t, 16)
        return copy(
            out_ref.at[to, pl.ds(1, 2)],
            back_ref.at[space, pl.ds(1, 2)],
            send_kv.at[t],
            recv_kv.at[t],
            (frame, to),
        )

    def query_grads(t):
        to = lax.rem(space + 1 + t, 16)
        return copy(
            out_ref.at[to, 0], back_ref.at[space, 0], send_q.at[t], recv_q.at[t], (frame, to)
        )

    def send_step(t, stop):
        if stop < 16:
            key_grads(t).start()

    for c in first:
        c.wait()
    add_into(
        lambda y, w, a, b: half.at[y, w, a, b],
        [lambda y, w, a, b: terms.at[y, w, a, b, core]],
        (2, 4, 4, 2),
    )
    second = []
    for i in range(1, 4):
        to_x, to_z = lax.rem(x + i, 4), lax.rem(z + i, 4)
        s = i - 1
        second.append(
            copy(half.at[0, :, to_x], x_in_a.at[s], send2.at[0, s], recv2.at[0, s], x_peer(i))
        )
        second.append(
            copy(half.at[1, to_z], z_in_b.at[s], send2.at[1, s], recv2.at[1, s], z_peer(i))
        )
    for c in second:
        c.start()
    for c in to_heads:
        c.wait()
    backward_prepare(x_ref, o_rows_ref, lse_ref, g_ref, *state, dq_sum)

    attend(0, STAGES[0])

    for c in second:
        c.wait()
    add_into(
        lambda w, b: half.at[0, w, x, b],
        [lambda w, b, s=s: x_in_a.at[s, w, b] for s in range(3)],
        (4, 2),
    )
    add_into(
        lambda a, b: half.at[1, z, a, b],
        [lambda a, b, s=s: z_in_b.at[s, a, b] for s in range(3)],
        (4, 2),
    )
    third = []
    for i in range(1, 4):
        to_x, to_z = lax.rem(x + i, 4), lax.rem(z + i, 4)
        s = i - 1
        third.append(
            copy(half.at[0, to_z, x], z_in_a.at[s], send3.at[0, s], recv3.at[0, s], z_peer(i))
        )
        third.append(
            copy(half.at[1, z, to_x], x_in_b.at[s], send3.at[1, s], recv3.at[1, s], x_peer(i))
        )
    for c in third:
        c.start()
    moves = []
    for i, (ref, out) in enumerate(((gh_ref, grad_hidden_ref), (out_cols_ref, block_out_ref))):
        positions = out.shape[1]
        for n, to in enumerate(other_frames):
            c = copy(
                rows_of(ref, to, positions),
                out.at[frame],
                send_f.at[i, n],
                recv_f.at[i, n],
                (to, space),
            )
            c.start()
            moves.append(c)
        out[frame] = rows_of(ref, frame, positions)[...]

    attend(STAGES[0], STAGES[1])

    for c in third:
        c.wait()
    add_into(
        lambda b: half.at[0, z, x, b], [lambda b, s=s: z_in_a.at[s, b] for s in range(3)], (2,)
    )
    add_into(
        lambda b: half.at[1, z, x, b], [lambda b, s=s: x_in_b.at[s, b] for s in range(3)], (2,)
    )
    fourth = copy(half.at[1 - lo, z, x], lo_in, send4.at[0], recv4.at[0], lo_peer)
    fourth.start()

    attend(STAGES[1], STAGES[2])

    fourth.wait()
    add_into(lambda b: half.at[lo, z, x, b], [lambda b: lo_in.at[b]], (2,))
    fifth = copy(half.at[lo, z, x, 1 - hi], hi_in, send4.at[1], recv4.at[1], hi_peer)
    fifth.start()

    attend(STAGES[2], 15)
    attend(15, 16)

    fifth.wait()
    total = (half[lo, z, x, hi].astype(F32) + hi_in[...].astype(F32)).astype(BF)
    mine[...] = total
    sixth = [
        copy(
            mine.at[window(lax.rem(space + i, 16))],
            sums_ref.at[space],
            send6.at[i - 1],
            recv6.at[i - 1],
            space_peer(i),
        )
        for i in range(1, 16)
    ]
    for c in sixth:
        c.start()
    sums_ref[space] = mine[window(space)]

    def finish(t, _):
        to = lax.rem(space + 1 + t, 16)
        at = pl.ds(pl.multiple_of(to * width, width), width)
        out_ref[to, 0] = (dq_sum[at, :] * SCALE).T.astype(BF)

        @pl.when(t < 15)
        def _():
            query_grads(t).start()

        return 0

    width = x_ref.shape[3]
    lax.fori_loop(0, 16, finish, 0)
    back_ref[space] = out_ref[space]
    for c in moves + sixth:
        c.wait()
    for t in range(15):
        key_grads(t).wait()
        query_grads(t).wait()


STAGES = (11, 14, 15)


def space_backward(blocks, o_rows, lse, grads, pairs):
    count, _, _, width = blocks.shape
    seq = count * width
    tile = (TILE_ROWS, TILE_COLS)
    by_frame = shape((8, width // 8, HEADS * HD), BF)
    dma = pltpu.SemaphoreType.DMA
    return pl.pallas_call(
        space_backward_body,
        out_shape=(shape(blocks.shape, BF), shape((16, WINDOW, TILE_COLS), BF), by_frame, by_frame),
        in_specs=[pl.BlockSpec(memory_space=pltpu.VMEM)] * 11,
        out_specs=[pl.BlockSpec(memory_space=pltpu.VMEM)] * 4,
        scratch_shapes=[
            pltpu.VMEM(blocks.shape, BF),
            pltpu.VMEM(grads.shape, BF),
            pltpu.VMEM(grads.shape, BF),
            pltpu.VMEM((HEADS * HD, width), BF),
            pltpu.VMEM((seq, 2 * ROWS + 16), BF),
            pltpu.VMEM((seq, ROWS + 16), BF),
            pltpu.VMEM((ROWS, seq), BF),
            pltpu.VMEM((ROWS, seq), BF),
            pltpu.VMEM((seq, width), BF),
            pltpu.VMEM((seq, width), BF),
            pltpu.VMEM((seq, ROWS), F32),
            pltpu.VMEM((2, 4, 4, 2, 2) + tile, BF),
            pltpu.VMEM((2, 4, 4, 2) + tile, BF),
            pltpu.VMEM((3, 4, 2) + tile, BF),
            pltpu.VMEM((3, 4, 2) + tile, BF),
            pltpu.VMEM((3, 2) + tile, BF),
            pltpu.VMEM((3, 2) + tile, BF),
            pltpu.VMEM((2,) + tile, BF),
            pltpu.VMEM(tile, BF),
            pltpu.VMEM(tile, BF),
            dma((2, 4)),
            dma((2, 4)),
            dma((2, 3)),
            dma((2, 3)),
            dma((2, 3)),
            dma((2, 3)),
            dma((2,)),
            dma((2,)),
            dma((15,)),
            dma((15,)),
            dma((2, 7)),
            dma((2, 7)),
            dma((15,)),
            dma((15,)),
            dma((15,)),
            dma((15,)),
            dma((7,)),
            dma((7,)),
            dma((15,)),
            dma((15,)),
        ],
        compiler_params=pltpu.CompilerParams(
            vmem_limit_bytes=VMEM_BYTES, collective_id=0, has_side_effects=True
        ),
        cost_estimate=pl.CostEstimate(
            flops=10 * seq * seq * 128, bytes_accessed=16 * 2**20, transcendentals=0
        ),
    )(blocks, o_rows, lse, grads, *pairs)


def middle_body(
    attn_ref,
    hidden_in_ref,
    cot_ref,
    w_space_ref,
    w_qkv_ref,
    w_time_ref,
    g_out_ref,
    gh_ref,
    out_ref,
    attn_space_ref,
    hidden_ref,
    attn_time_ref,
    dqkv_ref,
    qkv_ref,
    ga_ref,
):
    frames, _, positions, _ = attn_ref.shape
    tokens = frames * positions
    width = HEADS * HD
    for h in range(HEADS):
        block = attn_ref[:, h].reshape(tokens, 128)
        attn_space_ref[:, h * HD : (h + 1) * HD] = block[:, :HD]
    cot = cot_ref[...].reshape(tokens, width)
    base = hidden_in_ref[...].reshape(tokens, width).astype(F32)
    hidden_ref[...] = (base + dot(attn_space_ref[...], w_space_ref[...])).astype(BF)
    for c in range(3):
        at = pl.ds(c * width, width)
        qkv_ref[:, at] = dot(hidden_ref[...], w_qkv_ref[:, at]).astype(BF)
    ga_ref[...] = dot_nt(cot, w_time_ref[...]).astype(BF)

    same = (
        lax.broadcasted_iota(jnp.int32, (tokens, tokens), 0) % positions
        == lax.broadcasted_iota(jnp.int32, (tokens, tokens), 1) % positions
    )
    for h in range(HEADS):
        lo, hi = h * HD, (h + 1) * HD
        q = qkv_ref[:, lo:hi]
        k = qkv_ref[:, width + lo : width + hi]
        v = qkv_ref[:, 2 * width + lo : 2 * width + hi]
        g = ga_ref[:, lo:hi]
        scores = jnp.where(same, dot_nt(q, k) * SCALE, -jnp.inf)
        exps = jnp.exp(scores - jnp.max(scores, axis=1, keepdims=True))
        probs = exps / jnp.sum(exps, axis=1, keepdims=True)
        probs_bf = probs.astype(BF)
        attn_time_ref[:, lo:hi] = dot(probs_bf, v).astype(BF)
        weighted = probs * dot_nt(g, v)
        ds = ((weighted - probs * jnp.sum(weighted, axis=1, keepdims=True)) * SCALE).astype(BF)
        dqkv_ref[:, lo:hi] = dot(ds, k).astype(BF)
        dqkv_ref[:, width + lo : width + hi] = dot_tn(ds, q).astype(BF)
        dqkv_ref[:, 2 * width + lo : 2 * width + hi] = dot_tn(probs_bf, g).astype(BF)

    gh_ref[...] = (cot.astype(F32) + dot_nt(dqkv_ref[...], w_qkv_ref[...])).astype(BF)
    ga_ref[...] = dot_nt(gh_ref[...], w_space_ref[...]).astype(BF)
    for h in range(HEADS):
        block = ga_ref[:, h * HD : (h + 1) * HD]
        filled = jnp.concatenate([block, jnp.zeros((tokens, 128 - HD), BF)], axis=1)
        g_out_ref[:, h] = filled.reshape(frames, positions, 128)
    out = hidden_ref[...].astype(F32) + dot(attn_time_ref[...], w_time_ref[...])
    out_ref[...] = out.astype(BF)


def middle(attn, hidden_in, cot, w_space_out, w_time_qkv, w_time_out):
    frames, _, positions, _ = attn.shape
    tokens = frames * positions
    width = HEADS * HD
    rows = shape((tokens, width), BF)
    wide = shape((tokens, 3 * width), BF)
    return kernel_call(
        middle_body,
        (shape(attn.shape, BF), rows, rows, rows, rows, rows, wide),
        [pltpu.VMEM((tokens, 3 * width), BF), pltpu.VMEM((tokens, width), BF)],
        2 * tokens * width * width * 10,
        20 * 2**20,
        (attn, hidden_in, cot, w_space_out, w_time_qkv, w_time_out),
    )


def shards(
    hidden_in, query_space, key_space, value_space, cotangent, w_space_out, w_time_qkv, w_time_out
):
    width = hidden_in.shape[2]
    frames = lax.axis_size("frame")
    head_blocks, hidden_cols, cot_cols, attn, o_rows, lse = space_forward(
        query_space, key_space, value_space, hidden_in, cotangent, frames
    )
    g_out, grad_cols, out_cols, attn_space, hidden, attn_time, dqkv = middle(
        attn, hidden_cols, cot_cols, w_space_out, w_time_qkv, w_time_out
    )
    pairs = (attn_space, hidden, attn_time, grad_cols, dqkv, cot_cols.reshape(-1, width), out_cols)
    back, sums, grad_hidden, block_out = space_backward(head_blocks, o_rows, lse, g_out, pairs)
    block_out = block_out.reshape(hidden_in.shape)
    grad_hidden = grad_hidden.reshape(hidden_in.shape)
    space = lax.axis_index("space")
    own = lax.dynamic_slice_in_dim(sums, space * OWN_ROWS - window_start(space), OWN_ROWS, 1)
    own = own.transpose(1, 0, 2).reshape(OWN_ROWS, -1).astype(F32)
    cuts = (own[:, :width], own[:, width : 4 * width], own[:, 4 * width : 5 * width])
    return (block_out, grad_hidden, *join_heads(back), *cuts)


def solution(mesh):
    rows = P("frame", "space", None)
    weights = P(ALL, None)
    return jax.shard_map(
        shards,
        mesh=mesh,
        in_specs=(rows,) * 5 + (P(),) * 3,
        out_specs=(rows,) * 5 + (weights,) * 3,
        check_vma=False,
    )
```

```python
import jax
import jax.numpy as jnp
from jax import lax
from jax.experimental import pallas as pl
from jax.experimental.pallas import tpu as pltpu
from jax.sharding import PartitionSpec as P

HEADS = 16
HD = 72
ROWS = 80
SCALE = HD**-0.5
LOG2E = 1.4426950408889634
VMEM_BYTES = 62 * 2**20
BF = jnp.bfloat16
F32 = jnp.float32
ALL = ("frame", "space")


def kernel_call(body, out_shape, scratch_shapes, flops, moved, args):
    return pl.pallas_call(
        body,
        out_shape=out_shape,
        scratch_shapes=scratch_shapes,
        compiler_params=pltpu.CompilerParams(vmem_limit_bytes=VMEM_BYTES),
        cost_estimate=pl.CostEstimate(flops=flops, bytes_accessed=moved, transcendentals=0),
    )(*args)


def shape(dims, dtype):
    return jax.ShapeDtypeStruct(dims, dtype)


def dot(a, b):
    return jnp.dot(a, b, preferred_element_type=F32)


def dot_nt(a, b):
    return lax.dot_general(a, b, (((1,), (1,)), ((), ())), preferred_element_type=F32)


def dot_tn(a, b):
    return lax.dot_general(a, b, (((0,), (0,)), ((), ())), preferred_element_type=F32)


def two_parts(x):
    high = x.astype(BF)
    return [high, (x - high.astype(F32)).astype(BF)]


def three_parts_rows(x, rows):
    high = x.astype(BF).astype(F32)
    rest = x - high
    mid = rest.astype(BF).astype(F32)
    low = rest - mid
    at = lax.broadcasted_iota(jnp.int32, (rows, x.shape[1]), 0)
    return jnp.where(at == 0, high, jnp.where(at == 1, mid, jnp.where(at == 2, low, 0.0))).astype(BF)


def minus_rows(rows, columns):
    at = lax.broadcasted_iota(jnp.int32, (rows, columns), 0)
    return jnp.where(at < 3, -1.0, 0.0).astype(BF)


def split_heads(ref, out_ref, i):
    tokens = ref.shape[1]
    at = lax.broadcasted_iota(jnp.int32, (ROWS - HD, tokens), 0)
    fill = jnp.where(at == 0, 1.0 if i == 2 else 0.0, 0.0)
    flipped = ref[0].astype(F32).T
    for h in range(HEADS):
        block = jnp.concatenate([flipped[h * HD : (h + 1) * HD], fill], axis=0)
        out_ref[h, i] = block.astype(BF)


def join_heads_body(in_ref, q_ref, k_ref, v_ref):
    for i, ref in enumerate((q_ref, k_ref, v_ref)):
        blocks = [in_ref[h, i].astype(F32)[:HD] for h in range(HEADS)]
        ref[0] = jnp.concatenate(blocks, axis=0).T.astype(BF)


def join_heads(blocks):
    tokens = blocks.shape[3]
    rows = shape((1, tokens, HEADS * HD), BF)
    return kernel_call(
        join_heads_body, (rows, rows, rows), [], 0, 3 * tokens * HEADS * HD * 5, (blocks,)
    )


def copy_to(src, dst, send_sem, recv_sem, device):
    return pltpu.make_async_remote_copy(
        src_ref=src,
        dst_ref=dst,
        send_sem=send_sem,
        recv_sem=recv_sem,
        device_id=device,
        device_id_type=pl.DeviceIdType.MESH,
    )


def signal_all(barrier, peers):
    for peer in peers:
        pl.semaphore_signal(barrier, inc=1, device_id=peer, device_id_type=pl.DeviceIdType.MESH)


def rows_of(ref, i, count):
    return ref.at[pl.ds(pl.multiple_of(i * count, count), count)]


def scaled_query(block):
    return two_parts(block.astype(F32) * (SCALE * LOG2E))


def space_forward_body(
    q_ref,
    k_ref,
    v_ref,
    hidden_ref,
    cot_ref,
    x_ref,
    hidden_cols_ref,
    cot_cols_ref,
    attn_ref,
    o_rows_ref,
    lse_ref,
    packed,
    o_buf,
    heads_in,
    k_nat,
    v_rows,
    s_one,
    s_two,
    send_x,
    recv_x,
    send_f,
    recv_f,
    send_o,
    recv_o,
    send_a,
    recv_a,
):
    blocks, _, _, width = x_ref.shape
    frames, positions, _ = hidden_cols_ref.shape
    seq = blocks * width
    frame, space = lax.axis_index("frame"), lax.axis_index("space")
    others = [lax.rem(space + i, blocks) for i in range(1, blocks)]
    other_frames = [lax.rem(frame + i, frames) for i in range(1, frames)]
    peers = [(frame, to) for to in others] + [(to, space) for to in other_frames]
    barrier = pltpu.get_barrier_semaphore()
    signal_all(barrier, peers)

    waits = []
    for i, ref in ((1, k_ref), (2, v_ref), (0, q_ref)):
        split_heads(ref, packed, i)
        if not waits:
            pl.semaphore_wait(barrier, len(peers))
        for n, to in enumerate(others):
            c = copy_to(
                packed.at[to, i],
                x_ref.at[space, i],
                send_x.at[i, n],
                recv_x.at[i, n],
                (frame, to),
            )
            c.start()
            waits.append(c)
        x_ref[space, i] = packed[space, i]
    moves = []
    for i, (ref, out) in enumerate(((hidden_ref, hidden_cols_ref), (cot_ref, cot_cols_ref))):
        for n, to in enumerate(other_frames):
            c = copy_to(
                rows_of(ref.at[0], to, positions),
                out.at[frame],
                send_f.at[i, n],
                recv_f.at[i, n],
                (to, space),
            )
            c.start()
            moves.append(c)
        out[frame] = rows_of(ref.at[0], frame, positions)[...]
    for c in waits[: 2 * len(others)]:
        c.wait()

    def prepare(j, _):
        at = pl.ds(pl.multiple_of(j * width, width), width)
        k_block = x_ref[j, 1]
        k_nat[at, :] = jnp.concatenate([k_block, k_block], axis=0).T
        v_rows[:, at] = x_ref[j, 2]
        return 0

    lax.fori_loop(0, blocks, prepare, 0)

    for c in waits[2 * len(others) :]:
        c.wait()

    def score(j, s_ref):
        q_block = jnp.concatenate(scaled_query(x_ref[j, 0]), axis=0)
        top = None
        for c in range(CHUNKS):
            at = slice(c * seq // CHUNKS, (c + 1) * seq // CHUNKS)
            s = dot(k_nat[at, :], q_block)
            s_ref[at, :] = s
            best = jnp.max(s, axis=0, keepdims=True)
            top = best if top is None else jnp.maximum(top, best)
        return top

    def block_at(t):
        return lax.rem(space + 1 + t, blocks)

    def send_block(t):
        to = block_at(t)
        return copy_to(
            o_buf.at[to], heads_in.at[space], send_o.at[t], recv_o.at[t], (frame, to)
        )

    def both(t, s_ref, top, t_after, s_after):
        j, after = block_at(t), block_at(t_after)
        q_block = jnp.concatenate(scaled_query(x_ref[after, 0]), axis=0)
        top_after = None
        mixed = jnp.zeros((ROWS, width), F32)
        for c in range(CHUNKS):
            at = slice(c * seq // CHUNKS, (c + 1) * seq // CHUNKS)
            s = dot(k_nat[at, :], q_block)
            s_after[at, :] = s
            best = jnp.max(s, axis=0, keepdims=True)
            top_after = best if top_after is None else jnp.maximum(top_after, best)
            probs = jnp.exp2(s_ref[at, :] - top).astype(BF)
            mixed = mixed + dot(v_rows[:, at], probs)
        total = mixed[HD : HD + 1]
        mixed = mixed / total
        o_rows_ref[j] = mixed
        lse_ref[j] = jnp.broadcast_to(top + jnp.log2(total), (8, width))
        filled = jnp.concatenate([mixed[:HD], jnp.zeros((128 - HD, width), F32)], axis=0)
        o_buf[j] = filled.T.astype(BF).reshape(frames, positions, 128)

        @pl.when(t < blocks - 1)
        def _():
            send_block(t).start()

        return top_after

    def two_steps(i, top):
        j = 2 * i
        top = both(j, s_one, top, j + 1, s_two)
        return both(j + 1, s_two, top, jnp.minimum(j + 2, blocks - 1), s_one)

    lax.fori_loop(0, blocks // 2, two_steps, score(block_at(0), s_one))
    heads_in[space] = o_buf[space]
    for t in range(blocks - 1):
        send_block(t).wait()
    for n, to in enumerate(other_frames):
        c = copy_to(
            heads_in.at[:, to], attn_ref.at[frame], send_a.at[n], recv_a.at[n], (to, space)
        )
        c.start()
        moves.append(c)
    attn_ref[frame] = heads_in[:, frame]
    for c in moves:
        c.wait()


CHUNKS = 8


def space_forward(query, key_rows, value_rows, hidden_in, cot, frames):
    tokens, model = query.shape[1:]
    seq = HEADS * tokens
    dma = pltpu.SemaphoreType.DMA
    cols = shape((frames, tokens // frames, model), BF)
    return pl.pallas_call(
        space_forward_body,
        out_shape=(
            shape((HEADS, 3, ROWS, tokens), BF),
            cols,
            cols,
            shape((frames, HEADS, tokens // frames, 128), BF),
            shape((HEADS, ROWS, tokens), F32),
            shape((HEADS, 8, tokens), F32),
        ),
        in_specs=[pl.BlockSpec(memory_space=pltpu.VMEM)] * 5,
        out_specs=[pl.BlockSpec(memory_space=pltpu.VMEM)] * 6,
        scratch_shapes=[
            pltpu.VMEM((HEADS, 3, ROWS, tokens), BF),
            pltpu.VMEM((HEADS, frames, tokens // frames, 128), BF),
            pltpu.VMEM((HEADS, frames, tokens // frames, 128), BF),
            pltpu.VMEM((seq, 2 * ROWS), BF),
            pltpu.VMEM((ROWS, seq), BF),
            pltpu.VMEM((seq, tokens), F32),
            pltpu.VMEM((seq, tokens), F32),
            dma((3, HEADS - 1)),
            dma((3, HEADS - 1)),
            dma((2, frames - 1)),
            dma((2, frames - 1)),
            dma((HEADS - 1,)),
            dma((HEADS - 1,)),
            dma((frames - 1,)),
            dma((frames - 1,)),
        ],
        compiler_params=pltpu.CompilerParams(
            vmem_limit_bytes=VMEM_BYTES, collective_id=1, has_side_effects=True
        ),
        cost_estimate=pl.CostEstimate(
            flops=4 * seq * seq * 128, bytes_accessed=8 * 2**20, transcendentals=0
        ),
    )(query, key_rows, value_rows, hidden_in, cot)


Q_STEP = 1024
TILE_ROWS = 144
PART_ROWS = 48
TILE_COLS = 384


def backward_prepare(x_ref, o_rows_ref, lse_ref, g_ref, q_aug, g_aug, q_rows, g_rows, dq_sum):
    blocks, _, _, width = x_ref.shape

    def prepare(j, _):
        at = pl.ds(pl.multiple_of(j * width, width), width)
        q_block = x_ref[j, 0]
        parts = scaled_query(q_block) + [three_parts_rows(lse_ref[j][:1], 16)]
        q_aug[at, :] = jnp.concatenate(parts, axis=0).T
        q_rows[:, at] = q_block
        g_block = g_ref[:, j].reshape(width, 128).astype(F32).T[:ROWS]
        inner = jnp.sum(g_block[:HD] * o_rows_ref[j][:HD], axis=0, keepdims=True)
        g_bf = g_block.astype(BF)
        g_rows[:, at] = g_bf
        g_aug[at, :] = jnp.concatenate([g_bf, three_parts_rows(inner, 16)], axis=0).T
        dq_sum[at, :] = jnp.zeros((width, ROWS), F32)
        return 0

    lax.fori_loop(0, blocks, prepare, 0)


def backward_steps(
    first, last, done, x_ref, out_ref, q_aug, g_aug, q_rows, g_rows, p_buf, ds_buf, dq_sum
):
    blocks, _, _, width = x_ref.shape
    seq = blocks * width

    def step(t, _):
        j = lax.rem(lax.axis_index("space") + 1 + t, blocks)
        k_block = x_ref[j, 1]
        v_block = x_ref[j, 2]
        k_aug = jnp.concatenate([k_block, k_block, minus_rows(16, width)], axis=0)
        v_aug = jnp.concatenate([v_block, minus_rows(16, width)], axis=0)
        k_nat = k_block.T

        for c in range(seq // Q_STEP):
            at = pl.ds(c * Q_STEP, Q_STEP)
            probs = jnp.exp2(dot(q_aug[at, :], k_aug))
            p_buf[at, :] = probs.astype(BF)
            ds = (probs * dot(g_aug[at, :], v_aug)).astype(BF)
            ds_buf[at, :] = ds
            dq_sum[at, :] += dot(ds, k_nat)

        out_ref[j, 1] = (dot(q_rows[...], ds_buf[...]) * SCALE).astype(BF)
        out_ref[j, 2] = dot(g_rows[...], p_buf[...]).astype(BF)
        done(t, last)
        return 0

    lax.fori_loop(first, last, step, 0)


OWN_ROWS = 9
WINDOW = 32


def window_start(space):
    return jnp.minimum(lax.div(space * OWN_ROWS, 16) * 16, TILE_ROWS - WINDOW)


def window(space):
    return pl.ds(pl.multiple_of(window_start(space), 16), WINDOW)


def add_into(target, terms, lead):
    count = 1
    for n in lead:
        count *= n

    def one(i, _):
        index = []
        for n in reversed(lead):
            index.insert(0, lax.rem(i, n))
            i = lax.div(i, n)
        total = target(*index)[...].astype(F32)
        for term in terms:
            total = total + term(*index)[...].astype(F32)
        target(*index)[...] = total.astype(BF)
        return 0

    lax.fori_loop(0, count, one, 0)


def space_backward_body(
    x_ref,
    o_rows_ref,
    lse_ref,
    g_out_ref,
    attn_space_ref,
    hidden_ref,
    attn_time_ref,
    gh_ref,
    dqkv_ref,
    cot_ref,
    out_cols_ref,
    back_ref,
    sums_ref,
    grad_hidden_ref,
    block_out_ref,
    out_ref,
    g_mid,
    g_ref,
    rows_t,
    q_aug,
    g_aug,
    q_rows,
    g_rows,
    p_buf,
    ds_buf,
    dq_sum,
    terms,
    half,
    in_a1,
    in_b1,
    in_c1,
    in_a2,
    in_b2,
    in_c2,
    in_3,
    mine,
    send1,
    recv1,
    sends,
    recvs,
    send6,
    recv6,
    send_f,
    recv_f,
    send_kv,
    recv_kv,
    send_q,
    recv_q,
    send_g,
    recv_g,
    send_h,
    recv_h,
):
    frame, space = lax.axis_index("frame"), lax.axis_index("space")
    z, lo = lax.div(frame, 2), lax.rem(frame, 2)
    x, hi, core = lax.div(space, 4), lax.rem(lax.div(space, 2), 2), lax.rem(space, 2)

    def x_peer(i):
        return (frame, lax.rem(x + i, 4) * 4 + hi * 2 + core)

    def z_peer(i):
        return (lax.rem(z + i, 4) * 2 + lo, space)

    def space_peer(i):
        return (frame, lax.rem(space + i, 16))

    def y_index(i):
        return (1 - lo if i % 2 else lo), (1 - hi if i // 2 else hi)

    def y_peer(i):
        to_lo, to_hi = y_index(i)
        return (z * 2 + to_lo, x * 4 + to_hi * 2 + core)

    core_peer = (frame, x * 4 + hi * 2 + 1 - core)
    copy = copy_to
    others = [lax.rem(space + i, 16) for i in range(1, 16)]
    other_frames = [lax.rem(frame + i, 8) for i in range(1, 8)]
    peers = [(frame, to) for to in others] + [(to, space) for to in other_frames]
    peers.append(y_peer(3))
    barrier = pltpu.get_barrier_semaphore()
    signal_all(barrier, peers)

    pl.semaphore_wait(barrier, len(peers))
    to_frames = [
        copy(g_out_ref.at[to], g_mid.at[frame], send_g.at[n], recv_g.at[n], (to, space))
        for n, to in enumerate(other_frames)
    ]
    for c in to_frames:
        c.start()
    g_mid[frame] = g_out_ref[frame]

    first = []

    def store_terms(t, part):
        for f in range(8):
            for p in range(3):
                begin = f * TILE_ROWS + p * PART_ROWS
                terms[p, t // 4, f % 2, f // 2, t // 2 % 2, t % 2] = part[begin : begin + PART_ROWS]
        if t % 4 == 3:
            for p in range(3):
                c = copy(
                    terms.at[p, t // 4, :, :, :, 1 - core],
                    half.at[p, t // 4],
                    send1.at[p, t // 4],
                    recv1.at[p, t // 4],
                    core_peer,
                )
                c.start()
                first.append(c)

    for rows_ref, grads_ref, begin, tiles in (
        (attn_space_ref, gh_ref, 0, 3),
        (hidden_ref, dqkv_ref, 3, 9),
        (attn_time_ref, cot_ref, 12, 3),
    ):
        rows_t[...] = rows_ref[...].T
        for n in range(tiles):
            part = dot(rows_t[...], grads_ref[:, n * TILE_COLS : (n + 1) * TILE_COLS])
            store_terms(begin + n, part.astype(BF))
    store_terms(15, jnp.zeros((8 * TILE_ROWS, TILE_COLS), BF))

    for c in to_frames:
        c.wait()
    to_heads = [
        copy(g_mid.at[:, to], g_ref.at[:, space], send_h.at[n], recv_h.at[n], (frame, to))
        for n, to in enumerate(others)
    ]
    for c in to_heads:
        c.start()
    g_ref[:, space] = g_mid[:, space]

    state = (q_aug, g_aug, q_rows, g_rows)
    def attend(start, stop):
        backward_steps(start, stop, send_step, x_ref, out_ref, *state, p_buf, ds_buf, dq_sum)

    def key_grads(t):
        to = lax.rem(space + 1 + t, 16)
        return copy(
            out_ref.at[to, pl.ds(1, 2)],
            back_ref.at[space, pl.ds(1, 2)],
            send_kv.at[t],
            recv_kv.at[t],
            (frame, to),
        )

    def query_grads(t):
        to = lax.rem(space + 1 + t, 16)
        return copy(
            out_ref.at[to, 0], back_ref.at[space, 0], send_q.at[t], recv_q.at[t], (frame, to)
        )

    def send_step(t, stop):
        if stop < 16:
            key_grads(t).start()

    for c in first:
        c.wait()
    add_into(
        lambda p, a, y, w: half.at[p, a, y, w],
        [lambda p, a, y, w: terms.at[p, a, y, w, :, core]],
        (3, 4, 2, 4),
    )

    def stage(n, along_x, along_z, along_y):
        started = []
        for i in range(1, 4):
            for source, slots, index, peer in (
                (*along_x, lax.rem(x + i, 4), x_peer(i)),
                (*along_z, lax.rem(z + i, 4), z_peer(i)),
                (*along_y, y_index(i), y_peer(i)),
            ):
                at = len(started)
                started.append(
                    copy(source(index), slots(i - 1), sends.at[n, at], recvs.at[n, at], peer)
                )
        for c in started:
            c.start()
        return started

    def add_all(started, *sums):
        for c in started:
            c.wait()
        for target, slots, lead in sums:
            add_into(target, [lambda *at, k=k: slots(k, *at) for k in range(3)], lead)

    a1 = lambda k, *at: in_a1.at[(k, *at)]
    b1 = lambda k, *at: in_b1.at[(k, *at)]
    c1 = lambda k, *at: in_c1.at[(k, *at)]
    a2 = lambda k, *at: in_a2.at[(k, *at)]
    b2 = lambda k, *at: in_b2.at[(k, *at)]
    c2 = lambda k, *at: in_c2.at[(k, *at)]

    started = stage(
        0,
        (lambda i: half.at[0, i], a1),
        (lambda i: half.at[1, :, :, i], b1),
        (lambda i: half.at[2, :, i[0], :, i[1]], c1),
    )
    for c in to_heads:
        c.wait()
    backward_prepare(x_ref, o_rows_ref, lse_ref, g_ref, *state, dq_sum)
    attend(0, STAGES[0])
    add_all(
        started,
        (lambda y, w: half.at[0, x, y, w], a1, (2, 4)),
        (lambda a, y: half.at[1, a, y, z], b1, (4, 2)),
        (lambda a, w: half.at[2, a, lo, w, hi], c1, (4, 4)),
    )
    started = stage(
        1,
        (lambda i: half.at[2, i, lo, :, hi], c2),
        (lambda i: half.at[0, x, :, i], a2),
        (lambda i: half.at[1, :, i[0], z, i[1]], b2),
    )
    moves = []
    for i, (ref, out) in enumerate(((gh_ref, grad_hidden_ref), (out_cols_ref, block_out_ref))):
        positions = out.shape[1]
        for n, to in enumerate(other_frames):
            c = copy(
                rows_of(ref, to, positions),
                out.at[frame],
                send_f.at[i, n],
                recv_f.at[i, n],
                (to, space),
            )
            c.start()
            moves.append(c)
        out[frame] = rows_of(ref, frame, positions)[...]

    attend(STAGES[0], STAGES[1])
    add_all(
        started,
        (lambda y: half.at[0, x, y, z], a2, (2,)),
        (lambda a: half.at[1, a, lo, z, hi], b2, (4,)),
        (lambda w: half.at[2, x, lo, w, hi], c2, (4,)),
    )
    started = stage(
        2,
        (lambda i: half.at[1, i, lo, z, hi], lambda k: in_3.at[1, k]),
        (lambda i: half.at[2, x, lo, i, hi], lambda k: in_3.at[2, k]),
        (lambda i: half.at[0, x, i[0], z, i[1]], lambda k: in_3.at[0, k]),
    )
    attend(STAGES[1], STAGES[2])
    for c in started:
        c.wait()
    for p in range(3):
        total = half[p, x, lo, z, hi].astype(F32)
        for k in range(3):
            total = total + in_3[p, k].astype(F32)
        mine[p * PART_ROWS : (p + 1) * PART_ROWS] = total.astype(BF)
    sixth = [
        copy(
            mine.at[window(lax.rem(space + i, 16))],
            sums_ref.at[space],
            send6.at[i - 1],
            recv6.at[i - 1],
            space_peer(i),
        )
        for i in range(1, 16)
    ]
    for c in sixth:
        c.start()
    sums_ref[space] = mine[window(space)]
    attend(STAGES[2], 15)
    attend(15, 16)

    def finish(t, _):
        to = lax.rem(space + 1 + t, 16)
        at = pl.ds(pl.multiple_of(to * width, width), width)
        out_ref[to, 0] = (dq_sum[at, :] * SCALE).T.astype(BF)

        @pl.when(t < 15)
        def _():
            query_grads(t).start()

        return 0

    width = x_ref.shape[3]
    lax.fori_loop(0, 16, finish, 0)
    back_ref[space] = out_ref[space]
    for c in moves + sixth:
        c.wait()
    for t in range(15):
        key_grads(t).wait()
        query_grads(t).wait()


STAGES = (9, 12, 14)


def space_backward(blocks, o_rows, lse, grads, pairs):
    count, _, _, width = blocks.shape
    seq = count * width
    part = (PART_ROWS, TILE_COLS)
    by_frame = shape((8, width // 8, HEADS * HD), BF)
    dma = pltpu.SemaphoreType.DMA
    return pl.pallas_call(
        space_backward_body,
        out_shape=(shape(blocks.shape, BF), shape((16, WINDOW, TILE_COLS), BF), by_frame, by_frame),
        in_specs=[pl.BlockSpec(memory_space=pltpu.VMEM)] * 11,
        out_specs=[pl.BlockSpec(memory_space=pltpu.VMEM)] * 4,
        scratch_shapes=[
            pltpu.VMEM(blocks.shape, BF),
            pltpu.VMEM(grads.shape, BF),
            pltpu.VMEM(grads.shape, BF),
            pltpu.VMEM((HEADS * HD, width), BF),
            pltpu.VMEM((seq, 2 * ROWS + 16), BF),
            pltpu.VMEM((seq, ROWS + 16), BF),
            pltpu.VMEM((ROWS, seq), BF),
            pltpu.VMEM((ROWS, seq), BF),
            pltpu.VMEM((seq, width), BF),
            pltpu.VMEM((seq, width), BF),
            pltpu.VMEM((seq, ROWS), F32),
            pltpu.VMEM((3, 4, 2, 4, 2, 2) + part, BF),
            pltpu.VMEM((3, 4, 2, 4, 2) + part, BF),
            pltpu.VMEM((3, 2, 4, 2) + part, BF),
            pltpu.VMEM((3, 4, 2, 2) + part, BF),
            pltpu.VMEM((3, 4, 4) + part, BF),
            pltpu.VMEM((3, 2, 2) + part, BF),
            pltpu.VMEM((3, 4) + part, BF),
            pltpu.VMEM((3, 4) + part, BF),
            pltpu.VMEM((3, 3) + part, BF),
            pltpu.VMEM((TILE_ROWS, TILE_COLS), BF),
            dma((3, 4)),
            dma((3, 4)),
            dma((3, 9)),
            dma((3, 9)),
            dma((15,)),
            dma((15,)),
            dma((2, 7)),
            dma((2, 7)),
            dma((15,)),
            dma((15,)),
            dma((15,)),
            dma((15,)),
            dma((7,)),
            dma((7,)),
            dma((15,)),
            dma((15,)),
        ],
        compiler_params=pltpu.CompilerParams(
            vmem_limit_bytes=VMEM_BYTES, collective_id=0, has_side_effects=True
        ),
        cost_estimate=pl.CostEstimate(
            flops=10 * seq * seq * 128, bytes_accessed=16 * 2**20, transcendentals=0
        ),
    )(blocks, o_rows, lse, grads, *pairs)


def middle_body(
    attn_ref,
    hidden_in_ref,
    cot_ref,
    w_space_ref,
    w_qkv_ref,
    w_time_ref,
    g_out_ref,
    gh_ref,
    out_ref,
    attn_space_ref,
    hidden_ref,
    attn_time_ref,
    dqkv_ref,
    qkv_ref,
    ga_ref,
):
    frames, _, positions, _ = attn_ref.shape
    tokens = frames * positions
    width = HEADS * HD
    for h in range(HEADS):
        block = attn_ref[:, h].reshape(tokens, 128)
        attn_space_ref[:, h * HD : (h + 1) * HD] = block[:, :HD]
    cot = cot_ref[...].reshape(tokens, width)
    base = hidden_in_ref[...].reshape(tokens, width).astype(F32)
    hidden_ref[...] = (base + dot(attn_space_ref[...], w_space_ref[...])).astype(BF)
    for c in range(3):
        at = pl.ds(c * width, width)
        qkv_ref[:, at] = dot(hidden_ref[...], w_qkv_ref[:, at]).astype(BF)
    ga_ref[...] = dot_nt(cot, w_time_ref[...]).astype(BF)

    same = (
        lax.broadcasted_iota(jnp.int32, (tokens, tokens), 0) % positions
        == lax.broadcasted_iota(jnp.int32, (tokens, tokens), 1) % positions
    )
    for h in range(HEADS):
        lo, hi = h * HD, (h + 1) * HD
        q = qkv_ref[:, lo:hi]
        k = qkv_ref[:, width + lo : width + hi]
        v = qkv_ref[:, 2 * width + lo : 2 * width + hi]
        g = ga_ref[:, lo:hi]
        scores = jnp.where(same, dot_nt(q, k) * SCALE, -jnp.inf)
        exps = jnp.exp(scores - jnp.max(scores, axis=1, keepdims=True))
        probs = exps / jnp.sum(exps, axis=1, keepdims=True)
        probs_bf = probs.astype(BF)
        attn_time_ref[:, lo:hi] = dot(probs_bf, v).astype(BF)
        weighted = probs * dot_nt(g, v)
        ds = ((weighted - probs * jnp.sum(weighted, axis=1, keepdims=True)) * SCALE).astype(BF)
        dqkv_ref[:, lo:hi] = dot(ds, k).astype(BF)
        dqkv_ref[:, width + lo : width + hi] = dot_tn(ds, q).astype(BF)
        dqkv_ref[:, 2 * width + lo : 2 * width + hi] = dot_tn(probs_bf, g).astype(BF)

    gh_ref[...] = (cot.astype(F32) + dot_nt(dqkv_ref[...], w_qkv_ref[...])).astype(BF)
    ga_ref[...] = dot_nt(gh_ref[...], w_space_ref[...]).astype(BF)
    for h in range(HEADS):
        block = ga_ref[:, h * HD : (h + 1) * HD]
        filled = jnp.concatenate([block, jnp.zeros((tokens, 128 - HD), BF)], axis=1)
        g_out_ref[:, h] = filled.reshape(frames, positions, 128)
    out = hidden_ref[...].astype(F32) + dot(attn_time_ref[...], w_time_ref[...])
    out_ref[...] = out.astype(BF)


def middle(attn, hidden_in, cot, w_space_out, w_time_qkv, w_time_out):
    frames, _, positions, _ = attn.shape
    tokens = frames * positions
    width = HEADS * HD
    rows = shape((tokens, width), BF)
    wide = shape((tokens, 3 * width), BF)
    return kernel_call(
        middle_body,
        (shape(attn.shape, BF), rows, rows, rows, rows, rows, wide),
        [pltpu.VMEM((tokens, 3 * width), BF), pltpu.VMEM((tokens, width), BF)],
        2 * tokens * width * width * 10,
        20 * 2**20,
        (attn, hidden_in, cot, w_space_out, w_time_qkv, w_time_out),
    )


def shards(
    hidden_in, query_space, key_space, value_space, cotangent, w_space_out, w_time_qkv, w_time_out
):
    width = hidden_in.shape[2]
    frames = lax.axis_size("frame")
    head_blocks, hidden_cols, cot_cols, attn, o_rows, lse = space_forward(
        query_space, key_space, value_space, hidden_in, cotangent, frames
    )
    g_out, grad_cols, out_cols, attn_space, hidden, attn_time, dqkv = middle(
        attn, hidden_cols, cot_cols, w_space_out, w_time_qkv, w_time_out
    )
    pairs = (attn_space, hidden, attn_time, grad_cols, dqkv, cot_cols.reshape(-1, width), out_cols)
    back, sums, grad_hidden, block_out = space_backward(head_blocks, o_rows, lse, g_out, pairs)
    block_out = block_out.reshape(hidden_in.shape)
    grad_hidden = grad_hidden.reshape(hidden_in.shape)
    space = lax.axis_index("space")
    own = lax.dynamic_slice_in_dim(sums, space * OWN_ROWS - window_start(space), OWN_ROWS, 1)
    own = own.transpose(1, 0, 2).reshape(OWN_ROWS, -1).astype(F32)
    cuts = (own[:, :width], own[:, width : 4 * width], own[:, 4 * width : 5 * width])
    return (block_out, grad_hidden, *join_heads(back), *cuts)


def solution(mesh):
    rows = P("frame", "space", None)
    weights = P(ALL, None)
    return jax.shard_map(
        shards,
        mesh=mesh,
        in_specs=(rows,) * 5 + (P(),) * 3,
        out_specs=(rows,) * 5 + (weights,) * 3,
        check_vma=False,
    )
```

```python
import jax
import jax.numpy as jnp
from jax import lax
from jax.experimental import pallas as pl
from jax.experimental.pallas import tpu as pltpu
from jax.sharding import PartitionSpec as P

HEADS = 16
HD = 72
ROWS = 80
SCALE = HD**-0.5
LOG2E = 1.4426950408889634
VMEM_BYTES = 62 * 2**20
BF = jnp.bfloat16
F32 = jnp.float32
ALL = ("frame", "space")


def kernel_call(body, out_shape, scratch_shapes, flops, moved, args):
    return pl.pallas_call(
        body,
        out_shape=out_shape,
        scratch_shapes=scratch_shapes,
        compiler_params=pltpu.CompilerParams(vmem_limit_bytes=VMEM_BYTES),
        cost_estimate=pl.CostEstimate(flops=flops, bytes_accessed=moved, transcendentals=0),
    )(*args)


def shape(dims, dtype):
    return jax.ShapeDtypeStruct(dims, dtype)


def dot(a, b):
    return jnp.dot(a, b, preferred_element_type=F32)


def dot_nt(a, b):
    return lax.dot_general(a, b, (((1,), (1,)), ((), ())), preferred_element_type=F32)


def dot_tn(a, b):
    return lax.dot_general(a, b, (((0,), (0,)), ((), ())), preferred_element_type=F32)


def two_parts(x):
    high = x.astype(BF)
    return [high, (x - high.astype(F32)).astype(BF)]


def three_parts_rows(x, rows):
    high = x.astype(BF).astype(F32)
    rest = x - high
    mid = rest.astype(BF).astype(F32)
    low = rest - mid
    at = lax.broadcasted_iota(jnp.int32, (rows, x.shape[1]), 0)
    return jnp.where(at == 0, high, jnp.where(at == 1, mid, jnp.where(at == 2, low, 0.0))).astype(BF)


def minus_rows(rows, columns):
    at = lax.broadcasted_iota(jnp.int32, (rows, columns), 0)
    return jnp.where(at < 3, -1.0, 0.0).astype(BF)


def split_heads(ref, out_ref, i):
    tokens = ref.shape[1]
    at = lax.broadcasted_iota(jnp.int32, (ROWS - HD, tokens), 0)
    fill = jnp.where(at == 0, 1.0 if i == 2 else 0.0, 0.0)
    flipped = ref[0].astype(F32).T
    for h in range(HEADS):
        block = jnp.concatenate([flipped[h * HD : (h + 1) * HD], fill], axis=0)
        out_ref[h, i] = block.astype(BF)


def join_heads_body(in_ref, q_ref, k_ref, v_ref):
    for i, ref in enumerate((q_ref, k_ref, v_ref)):
        blocks = [in_ref[h, i].astype(F32)[:HD] for h in range(HEADS)]
        ref[0] = jnp.concatenate(blocks, axis=0).T.astype(BF)


def join_heads(blocks):
    tokens = blocks.shape[3]
    rows = shape((1, tokens, HEADS * HD), BF)
    return kernel_call(
        join_heads_body, (rows, rows, rows), [], 0, 3 * tokens * HEADS * HD * 5, (blocks,)
    )


def copy_to(src, dst, send_sem, recv_sem, device):
    return pltpu.make_async_remote_copy(
        src_ref=src,
        dst_ref=dst,
        send_sem=send_sem,
        recv_sem=recv_sem,
        device_id=device,
        device_id_type=pl.DeviceIdType.MESH,
    )


def signal_all(barrier, peers):
    for peer in peers:
        pl.semaphore_signal(barrier, inc=1, device_id=peer, device_id_type=pl.DeviceIdType.MESH)


def rows_of(ref, i, count):
    return ref.at[pl.ds(pl.multiple_of(i * count, count), count)]


def scaled_query(block):
    return two_parts(block.astype(F32) * (SCALE * LOG2E))


def space_forward_body(
    q_ref,
    k_ref,
    v_ref,
    hidden_ref,
    cot_ref,
    x_ref,
    hidden_cols_ref,
    cot_cols_ref,
    attn_ref,
    o_rows_ref,
    lse_ref,
    packed,
    o_buf,
    heads_in,
    k_nat,
    v_rows,
    s_one,
    s_two,
    send_x,
    recv_x,
    send_f,
    recv_f,
    send_o,
    recv_o,
    send_a,
    recv_a,
):
    blocks, _, _, width = x_ref.shape
    frames, positions, _ = hidden_cols_ref.shape
    seq = blocks * width
    frame, space = lax.axis_index("frame"), lax.axis_index("space")
    others = [lax.rem(space + i, blocks) for i in range(1, blocks)]
    other_frames = [lax.rem(frame + i, frames) for i in range(1, frames)]
    peers = [(frame, to) for to in others] + [(to, space) for to in other_frames]
    barrier = pltpu.get_barrier_semaphore()
    signal_all(barrier, peers)

    waits = []
    for i, ref in ((1, k_ref), (2, v_ref), (0, q_ref)):
        split_heads(ref, packed, i)
        if not waits:
            pl.semaphore_wait(barrier, len(peers))
        for n, to in enumerate(others):
            c = copy_to(
                packed.at[to, i],
                x_ref.at[space, i],
                send_x.at[i, n],
                recv_x.at[i, n],
                (frame, to),
            )
            c.start()
            waits.append(c)
        x_ref[space, i] = packed[space, i]
    moves = []
    for i, (ref, out) in enumerate(((hidden_ref, hidden_cols_ref), (cot_ref, cot_cols_ref))):
        for n, to in enumerate(other_frames):
            c = copy_to(
                rows_of(ref.at[0], to, positions),
                out.at[frame],
                send_f.at[i, n],
                recv_f.at[i, n],
                (to, space),
            )
            c.start()
            moves.append(c)
        out[frame] = rows_of(ref.at[0], frame, positions)[...]
    for c in waits[: 2 * len(others)]:
        c.wait()

    def prepare(j, _):
        at = pl.ds(pl.multiple_of(j * width, width), width)
        k_block = x_ref[j, 1]
        k_nat[at, :] = jnp.concatenate([k_block, k_block], axis=0).T
        v_rows[:, at] = x_ref[j, 2]
        return 0

    lax.fori_loop(0, blocks, prepare, 0)

    def score(j, s_ref):
        q_block = jnp.concatenate(scaled_query(x_ref[j, 0]), axis=0)
        top = None
        for c in range(CHUNKS):
            at = slice(c * seq // CHUNKS, (c + 1) * seq // CHUNKS)
            s = dot(k_nat[at, :], q_block)
            s_ref[at, :] = s
            best = jnp.max(s, axis=0, keepdims=True)
            top = best if top is None else jnp.maximum(top, best)
        return top

    def block_at(t):
        return lax.rem(space + 2 * blocks - 1 - t, blocks)

    def query_block(t):
        to = lax.rem(space + 1 + t, blocks)
        return copy_to(
            packed.at[to, 0], x_ref.at[space, 0], send_x.at[0, t], recv_x.at[0, t], (frame, to)
        )

    def send_block(t):
        to = block_at(t)
        return copy_to(o_buf.at[to], heads_in.at[t], send_o.at[t], recv_o.at[t], (frame, to))

    def both(t, s_ref, top, t_after, s_after):
        j, after = block_at(t), block_at(t_after)

        @pl.when(t_after < blocks - 1)
        def _():
            query_block(t_after).wait_recv()

        q_block = jnp.concatenate(scaled_query(x_ref[after, 0]), axis=0)
        top_after = None
        mixed = jnp.zeros((ROWS, width), F32)
        for c in range(CHUNKS):
            at = slice(c * seq // CHUNKS, (c + 1) * seq // CHUNKS)
            s = dot(k_nat[at, :], q_block)
            s_after[at, :] = s
            best = jnp.max(s, axis=0, keepdims=True)
            top_after = best if top_after is None else jnp.maximum(top_after, best)
            probs = jnp.exp2(s_ref[at, :] - top).astype(BF)
            mixed = mixed + dot(v_rows[:, at], probs)
        total = mixed[HD : HD + 1]
        mixed = mixed / total
        o_rows_ref[j] = mixed
        lse_ref[j] = jnp.broadcast_to(top + jnp.log2(total), (8, width))
        filled = jnp.concatenate([mixed[:HD], jnp.zeros((128 - HD, width), F32)], axis=0)
        o_buf[j] = filled.T.astype(BF).reshape(frames, positions, 128)

        @pl.when(t < blocks - 1)
        def _():
            send_block(t).start()

        return top_after

    def two_steps(i, top):
        j = 2 * i
        top = both(j, s_one, top, j + 1, s_two)
        return both(j + 1, s_two, top, jnp.minimum(j + 2, blocks - 1), s_one)

    def pass_on(g, begin, count):
        some = pl.ds(begin, count)
        for n, to in enumerate(other_frames):
            c = copy_to(
                heads_in.at[some, to],
                attn_ref.at[frame, some],
                send_a.at[g, n],
                recv_a.at[g, n],
                (to, space),
            )
            c.start()
            moves.append(c)
        attn_ref[frame, some] = heads_in[some, frame]

    query_block(0).wait_recv()
    top = lax.fori_loop(0, PASS_AFTER // 2, two_steps, score(block_at(0), s_one))
    for t in range(PASS_FIRST):
        send_block(t).wait()
    pass_on(0, 0, PASS_FIRST)
    lax.fori_loop(PASS_AFTER // 2, blocks // 2, two_steps, top)
    heads_in[blocks - 1] = o_buf[space]
    for t in range(PASS_FIRST, blocks - 1):
        send_block(t).wait()
    pass_on(1, PASS_FIRST, blocks - PASS_FIRST)
    for t in range(blocks - 1):
        query_block(t).wait_send()
    for c in moves:
        c.wait()


CHUNKS = 8
PASS_FIRST = 10
PASS_AFTER = 12


def space_forward(query, key_rows, value_rows, hidden_in, cot, frames):
    tokens, model = query.shape[1:]
    seq = HEADS * tokens
    dma = pltpu.SemaphoreType.DMA
    cols = shape((frames, tokens // frames, model), BF)
    return pl.pallas_call(
        space_forward_body,
        out_shape=(
            shape((HEADS, 3, ROWS, tokens), BF),
            cols,
            cols,
            shape((frames, HEADS, tokens // frames, 128), BF),
            shape((HEADS, ROWS, tokens), F32),
            shape((HEADS, 8, tokens), F32),
        ),
        in_specs=[pl.BlockSpec(memory_space=pltpu.VMEM)] * 5,
        out_specs=[pl.BlockSpec(memory_space=pltpu.VMEM)] * 6,
        scratch_shapes=[
            pltpu.VMEM((HEADS, 3, ROWS, tokens), BF),
            pltpu.VMEM((HEADS, frames, tokens // frames, 128), BF),
            pltpu.VMEM((HEADS, frames, tokens // frames, 128), BF),
            pltpu.VMEM((seq, 2 * ROWS), BF),
            pltpu.VMEM((ROWS, seq), BF),
            pltpu.VMEM((seq, tokens), F32),
            pltpu.VMEM((seq, tokens), F32),
            dma((3, HEADS - 1)),
            dma((3, HEADS - 1)),
            dma((2, frames - 1)),
            dma((2, frames - 1)),
            dma((HEADS - 1,)),
            dma((HEADS - 1,)),
            dma((2, frames - 1)),
            dma((2, frames - 1)),
        ],
        compiler_params=pltpu.CompilerParams(
            vmem_limit_bytes=VMEM_BYTES, collective_id=1, has_side_effects=True
        ),
        cost_estimate=pl.CostEstimate(
            flops=4 * seq * seq * 128, bytes_accessed=8 * 2**20, transcendentals=0
        ),
    )(query, key_rows, value_rows, hidden_in, cot)


Q_STEP = 1024
TILE_ROWS = 144
PART_ROWS = 48
TILE_COLS = 384


def backward_prepare(x_ref, o_rows_ref, lse_ref, g_ref, q_aug, g_aug, q_rows, g_rows, dq_sum):
    blocks, _, _, width = x_ref.shape

    def prepare(j, _):
        at = pl.ds(pl.multiple_of(j * width, width), width)
        q_block = x_ref[j, 0]
        parts = scaled_query(q_block) + [three_parts_rows(lse_ref[j][:1], 16)]
        q_aug[at, :] = jnp.concatenate(parts, axis=0).T
        q_rows[:, at] = q_block
        g_block = g_ref[:, j].reshape(width, 128).astype(F32).T[:ROWS]
        inner = jnp.sum(g_block[:HD] * o_rows_ref[j][:HD], axis=0, keepdims=True)
        g_bf = g_block.astype(BF)
        g_rows[:, at] = g_bf
        g_aug[at, :] = jnp.concatenate([g_bf, three_parts_rows(inner, 16)], axis=0).T
        dq_sum[at, :] = jnp.zeros((width, ROWS), F32)
        return 0

    lax.fori_loop(0, blocks, prepare, 0)


def backward_steps(
    first, last, done, x_ref, out_ref, q_aug, g_aug, q_rows, g_rows, p_buf, ds_buf, dq_sum
):
    blocks, _, _, width = x_ref.shape
    seq = blocks * width

    def step(t, _):
        j = lax.rem(lax.axis_index("space") + 1 + t, blocks)
        k_block = x_ref[j, 1]
        v_block = x_ref[j, 2]
        k_aug = jnp.concatenate([k_block, k_block, minus_rows(16, width)], axis=0)
        v_aug = jnp.concatenate([v_block, minus_rows(16, width)], axis=0)
        k_nat = k_block.T

        for c in range(seq // Q_STEP):
            at = pl.ds(c * Q_STEP, Q_STEP)
            probs = jnp.exp2(dot(q_aug[at, :], k_aug))
            p_buf[at, :] = probs.astype(BF)
            ds = (probs * dot(g_aug[at, :], v_aug)).astype(BF)
            ds_buf[at, :] = ds
            dq_sum[at, :] += dot(ds, k_nat)

        out_ref[j, 1] = (dot(q_rows[...], ds_buf[...]) * SCALE).astype(BF)
        out_ref[j, 2] = dot(g_rows[...], p_buf[...]).astype(BF)
        done(t, last)
        return 0

    lax.fori_loop(first, last, step, 0)


OWN_ROWS = 9
WINDOW = 32


def window_start(space):
    return jnp.minimum(lax.div(space * OWN_ROWS, 16) * 16, TILE_ROWS - WINDOW)


def window(space):
    return pl.ds(pl.multiple_of(window_start(space), 16), WINDOW)


def add_into(target, terms, lead):
    count = 1
    for n in lead:
        count *= n

    def one(i, _):
        index = []
        for n in reversed(lead):
            index.insert(0, lax.rem(i, n))
            i = lax.div(i, n)
        total = target(*index)[...].astype(F32)
        for term in terms:
            total = total + term(*index)[...].astype(F32)
        target(*index)[...] = total.astype(BF)
        return 0

    lax.fori_loop(0, count, one, 0)


def space_backward_body(
    x_ref,
    o_rows_ref,
    lse_ref,
    g_out_ref,
    attn_space_ref,
    hidden_ref,
    attn_time_ref,
    gh_ref,
    dqkv_ref,
    cot_ref,
    out_cols_ref,
    back_ref,
    sums_ref,
    grad_hidden_ref,
    block_out_ref,
    out_ref,
    g_mid,
    g_ref,
    rows_t,
    q_aug,
    g_aug,
    q_rows,
    g_rows,
    p_buf,
    ds_buf,
    dq_sum,
    terms,
    half,
    in_a1,
    in_b1,
    in_c1,
    in_a2,
    in_b2,
    in_c2,
    in_3,
    mine,
    send1,
    recv1,
    sends,
    recvs,
    send6,
    recv6,
    send_f,
    recv_f,
    send_kv,
    recv_kv,
    send_q,
    recv_q,
    send_g,
    recv_g,
    send_h,
    recv_h,
):
    frame, space = lax.axis_index("frame"), lax.axis_index("space")
    z, lo = lax.div(frame, 2), lax.rem(frame, 2)
    x, hi, core = lax.div(space, 4), lax.rem(lax.div(space, 2), 2), lax.rem(space, 2)

    def x_peer(i):
        return (frame, lax.rem(x + i, 4) * 4 + hi * 2 + core)

    def z_peer(i):
        return (lax.rem(z + i, 4) * 2 + lo, space)

    def space_peer(i):
        return (frame, lax.rem(space + i, 16))

    def y_index(i):
        return (1 - lo if i % 2 else lo), (1 - hi if i // 2 else hi)

    def y_peer(i):
        to_lo, to_hi = y_index(i)
        return (z * 2 + to_lo, x * 4 + to_hi * 2 + core)

    core_peer = (frame, x * 4 + hi * 2 + 1 - core)
    copy = copy_to
    others = [lax.rem(space + i, 16) for i in range(1, 16)]
    other_frames = [lax.rem(frame + i, 8) for i in range(1, 8)]
    peers = [(frame, to) for to in others] + [(to, space) for to in other_frames]
    peers.append(y_peer(3))
    barrier = pltpu.get_barrier_semaphore()
    signal_all(barrier, peers)

    pl.semaphore_wait(barrier, len(peers))
    to_frames = [
        copy(g_out_ref.at[to], g_mid.at[frame], send_g.at[n], recv_g.at[n], (to, space))
        for n, to in enumerate(other_frames)
    ]
    for c in to_frames:
        c.start()
    g_mid[frame] = g_out_ref[frame]

    first = []

    def store_terms(t, part):
        for f in range(8):
            for p in range(3):
                begin = f * TILE_ROWS + p * PART_ROWS
                terms[p, t // 4, f % 2, f // 2, t // 2 % 2, t % 2] = part[begin : begin + PART_ROWS]
        if t % 4 == 3:
            for p in range(3):
                c = copy(
                    terms.at[p, t // 4, :, :, :, 1 - core],
                    half.at[p, t // 4],
                    send1.at[p, t // 4],
                    recv1.at[p, t // 4],
                    core_peer,
                )
                c.start()
                first.append(c)

    for rows_ref, grads_ref, begin, tiles in (
        (attn_space_ref, gh_ref, 0, 3),
        (hidden_ref, dqkv_ref, 3, 9),
        (attn_time_ref, cot_ref, 12, 3),
    ):
        rows_t[...] = rows_ref[...].T
        for n in range(tiles):
            part = dot(rows_t[...], grads_ref[:, n * TILE_COLS : (n + 1) * TILE_COLS])
            store_terms(begin + n, part.astype(BF))
    store_terms(15, jnp.zeros((8 * TILE_ROWS, TILE_COLS), BF))

    for c in to_frames:
        c.wait()
    to_heads = [
        copy(g_mid.at[:, to], g_ref.at[:, space], send_h.at[n], recv_h.at[n], (frame, to))
        for n, to in enumerate(others)
    ]
    for c in to_heads:
        c.start()
    g_ref[:, space] = g_mid[:, space]

    state = (q_aug, g_aug, q_rows, g_rows)
    def attend(start, stop):
        backward_steps(start, stop, send_step, x_ref, out_ref, *state, p_buf, ds_buf, dq_sum)

    def key_grads(t):
        to = lax.rem(space + 1 + t, 16)
        return copy(
            out_ref.at[to, pl.ds(1, 2)],
            back_ref.at[space, pl.ds(1, 2)],
            send_kv.at[t],
            recv_kv.at[t],
            (frame, to),
        )

    def query_grads(t):
        to = lax.rem(space + 1 + t, 16)
        return copy(
            out_ref.at[to, 0], back_ref.at[space, 0], send_q.at[t], recv_q.at[t], (frame, to)
        )

    def send_step(t, stop):
        if stop < 16:
            key_grads(t).start()

    for c in first:
        c.wait()
    add_into(
        lambda p, a, y, w: half.at[p, a, y, w],
        [lambda p, a, y, w: terms.at[p, a, y, w, :, core]],
        (3, 4, 2, 4),
    )

    def stage(n, along_x, along_z, along_y):
        started = []
        for i in range(1, 4):
            for source, slots, index, peer in (
                (*along_x, lax.rem(x + i, 4), x_peer(i)),
                (*along_z, lax.rem(z + i, 4), z_peer(i)),
                (*along_y, y_index(i), y_peer(i)),
            ):
                at = len(started)
                started.append(
                    copy(source(index), slots(i - 1), sends.at[n, at], recvs.at[n, at], peer)
                )
        for c in started:
            c.start()
        return started

    def add_all(started, *sums):
        for c in started:
            c.wait()
        for target, slots, lead in sums:
            add_into(target, [lambda *at, k=k: slots(k, *at) for k in range(3)], lead)

    a1 = lambda k, *at: in_a1.at[(k, *at)]
    b1 = lambda k, *at: in_b1.at[(k, *at)]
    c1 = lambda k, *at: in_c1.at[(k, *at)]
    a2 = lambda k, *at: in_a2.at[(k, *at)]
    b2 = lambda k, *at: in_b2.at[(k, *at)]
    c2 = lambda k, *at: in_c2.at[(k, *at)]

    started = stage(
        0,
        (lambda i: half.at[0, i], a1),
        (lambda i: half.at[1, :, :, i], b1),
        (lambda i: half.at[2, :, i[0], :, i[1]], c1),
    )
    for c in to_heads:
        c.wait()
    backward_prepare(x_ref, o_rows_ref, lse_ref, g_ref, *state, dq_sum)
    attend(0, STAGES[0])
    add_all(
        started,
        (lambda y, w: half.at[0, x, y, w], a1, (2, 4)),
        (lambda a, y: half.at[1, a, y, z], b1, (4, 2)),
        (lambda a, w: half.at[2, a, lo, w, hi], c1, (4, 4)),
    )
    started = stage(
        1,
        (lambda i: half.at[2, i, lo, :, hi], c2),
        (lambda i: half.at[0, x, :, i], a2),
        (lambda i: half.at[1, :, i[0], z, i[1]], b2),
    )
    attend(STAGES[0], STAGES[1])
    add_all(
        started,
        (lambda y: half.at[0, x, y, z], a2, (2,)),
        (lambda a: half.at[1, a, lo, z, hi], b2, (4,)),
        (lambda w: half.at[2, x, lo, w, hi], c2, (4,)),
    )
    started = stage(
        2,
        (lambda i: half.at[1, i, lo, z, hi], lambda k: in_3.at[1, k]),
        (lambda i: half.at[2, x, lo, i, hi], lambda k: in_3.at[2, k]),
        (lambda i: half.at[0, x, i[0], z, i[1]], lambda k: in_3.at[0, k]),
    )
    moves = []
    for i, (ref, out) in enumerate(((gh_ref, grad_hidden_ref), (out_cols_ref, block_out_ref))):
        positions = out.shape[1]
        for n, to in enumerate(other_frames):
            c = copy(
                rows_of(ref, to, positions),
                out.at[frame],
                send_f.at[i, n],
                recv_f.at[i, n],
                (to, space),
            )
            c.start()
            moves.append(c)
        out[frame] = rows_of(ref, frame, positions)[...]

    attend(STAGES[1], STAGES[2])
    for c in started:
        c.wait()
    for p in range(3):
        total = half[p, x, lo, z, hi].astype(F32)
        for k in range(3):
            total = total + in_3[p, k].astype(F32)
        mine[p * PART_ROWS : (p + 1) * PART_ROWS] = total.astype(BF)
    sixth = [
        copy(
            mine.at[window(lax.rem(space + i, 16))],
            sums_ref.at[space],
            send6.at[i - 1],
            recv6.at[i - 1],
            space_peer(i),
        )
        for i in range(1, 16)
    ]
    for c in sixth:
        c.start()
    sums_ref[space] = mine[window(space)]
    attend(STAGES[2], 15)
    attend(15, 16)

    def finish(t, _):
        to = lax.rem(space + 1 + t, 16)
        at = pl.ds(pl.multiple_of(to * width, width), width)
        out_ref[to, 0] = (dq_sum[at, :] * SCALE).T.astype(BF)

        @pl.when(t < 15)
        def _():
            query_grads(t).start()

        return 0

    width = x_ref.shape[3]
    lax.fori_loop(0, 16, finish, 0)
    back_ref[space] = out_ref[space]
    for c in moves + sixth:
        c.wait()
    for t in range(15):
        key_grads(t).wait()
        query_grads(t).wait()


STAGES = (9, 12, 14)


def space_backward(blocks, o_rows, lse, grads, pairs):
    count, _, _, width = blocks.shape
    seq = count * width
    part = (PART_ROWS, TILE_COLS)
    by_frame = shape((8, width // 8, HEADS * HD), BF)
    dma = pltpu.SemaphoreType.DMA
    return pl.pallas_call(
        space_backward_body,
        out_shape=(shape(blocks.shape, BF), shape((16, WINDOW, TILE_COLS), BF), by_frame, by_frame),
        in_specs=[pl.BlockSpec(memory_space=pltpu.VMEM)] * 11,
        out_specs=[pl.BlockSpec(memory_space=pltpu.VMEM)] * 4,
        scratch_shapes=[
            pltpu.VMEM(blocks.shape, BF),
            pltpu.VMEM(grads.shape, BF),
            pltpu.VMEM(grads.shape, BF),
            pltpu.VMEM((HEADS * HD, width), BF),
            pltpu.VMEM((seq, 2 * ROWS + 16), BF),
            pltpu.VMEM((seq, ROWS + 16), BF),
            pltpu.VMEM((ROWS, seq), BF),
            pltpu.VMEM((ROWS, seq), BF),
            pltpu.VMEM((seq, width), BF),
            pltpu.VMEM((seq, width), BF),
            pltpu.VMEM((seq, ROWS), F32),
            pltpu.VMEM((3, 4, 2, 4, 2, 2) + part, BF),
            pltpu.VMEM((3, 4, 2, 4, 2) + part, BF),
            pltpu.VMEM((3, 2, 4, 2) + part, BF),
            pltpu.VMEM((3, 4, 2, 2) + part, BF),
            pltpu.VMEM((3, 4, 4) + part, BF),
            pltpu.VMEM((3, 2, 2) + part, BF),
            pltpu.VMEM((3, 4) + part, BF),
            pltpu.VMEM((3, 4) + part, BF),
            pltpu.VMEM((3, 3) + part, BF),
            pltpu.VMEM((TILE_ROWS, TILE_COLS), BF),
            dma((3, 4)),
            dma((3, 4)),
            dma((3, 9)),
            dma((3, 9)),
            dma((15,)),
            dma((15,)),
            dma((2, 7)),
            dma((2, 7)),
            dma((15,)),
            dma((15,)),
            dma((15,)),
            dma((15,)),
            dma((7,)),
            dma((7,)),
            dma((15,)),
            dma((15,)),
        ],
        compiler_params=pltpu.CompilerParams(
            vmem_limit_bytes=VMEM_BYTES, collective_id=0, has_side_effects=True
        ),
        cost_estimate=pl.CostEstimate(
            flops=10 * seq * seq * 128, bytes_accessed=16 * 2**20, transcendentals=0
        ),
    )(blocks, o_rows, lse, grads, *pairs)


def middle_body(
    attn_ref,
    hidden_in_ref,
    cot_ref,
    w_space_ref,
    w_qkv_ref,
    w_time_ref,
    g_out_ref,
    gh_ref,
    out_ref,
    attn_space_ref,
    hidden_ref,
    attn_time_ref,
    dqkv_ref,
    qkv_ref,
    ga_ref,
):
    frames, _, positions, _ = attn_ref.shape
    tokens = frames * positions
    width = HEADS * HD
    space = lax.axis_index("space")
    for h in range(HEADS):
        slot = lax.rem(h + 2 * HEADS - 1 - space, HEADS)
        block = attn_ref[:, slot].reshape(tokens, 128)
        attn_space_ref[:, h * HD : (h + 1) * HD] = block[:, :HD]
    cot = cot_ref[...].reshape(tokens, width)
    base = hidden_in_ref[...].reshape(tokens, width).astype(F32)
    hidden_ref[...] = (base + dot(attn_space_ref[...], w_space_ref[...])).astype(BF)
    for c in range(3):
        at = pl.ds(c * width, width)
        qkv_ref[:, at] = dot(hidden_ref[...], w_qkv_ref[:, at]).astype(BF)
    ga_ref[...] = dot_nt(cot, w_time_ref[...]).astype(BF)

    same = (
        lax.broadcasted_iota(jnp.int32, (tokens, tokens), 0) % positions
        == lax.broadcasted_iota(jnp.int32, (tokens, tokens), 1) % positions
    )
    for h in range(HEADS):
        lo, hi = h * HD, (h + 1) * HD
        q = qkv_ref[:, lo:hi]
        k = qkv_ref[:, width + lo : width + hi]
        v = qkv_ref[:, 2 * width + lo : 2 * width + hi]
        g = ga_ref[:, lo:hi]
        scores = jnp.where(same, dot_nt(q, k) * SCALE, -jnp.inf)
        exps = jnp.exp(scores - jnp.max(scores, axis=1, keepdims=True))
        probs = exps / jnp.sum(exps, axis=1, keepdims=True)
        probs_bf = probs.astype(BF)
        attn_time_ref[:, lo:hi] = dot(probs_bf, v).astype(BF)
        weighted = probs * dot_nt(g, v)
        ds = ((weighted - probs * jnp.sum(weighted, axis=1, keepdims=True)) * SCALE).astype(BF)
        dqkv_ref[:, lo:hi] = dot(ds, k).astype(BF)
        dqkv_ref[:, width + lo : width + hi] = dot_tn(ds, q).astype(BF)
        dqkv_ref[:, 2 * width + lo : 2 * width + hi] = dot_tn(probs_bf, g).astype(BF)

    gh_ref[...] = (cot.astype(F32) + dot_nt(dqkv_ref[...], w_qkv_ref[...])).astype(BF)
    ga_ref[...] = dot_nt(gh_ref[...], w_space_ref[...]).astype(BF)
    for h in range(HEADS):
        block = ga_ref[:, h * HD : (h + 1) * HD]
        filled = jnp.concatenate([block, jnp.zeros((tokens, 128 - HD), BF)], axis=1)
        g_out_ref[:, h] = filled.reshape(frames, positions, 128)
    out = hidden_ref[...].astype(F32) + dot(attn_time_ref[...], w_time_ref[...])
    out_ref[...] = out.astype(BF)


def middle(attn, hidden_in, cot, w_space_out, w_time_qkv, w_time_out):
    frames, _, positions, _ = attn.shape
    tokens = frames * positions
    width = HEADS * HD
    rows = shape((tokens, width), BF)
    wide = shape((tokens, 3 * width), BF)
    return kernel_call(
        middle_body,
        (shape(attn.shape, BF), rows, rows, rows, rows, rows, wide),
        [pltpu.VMEM((tokens, 3 * width), BF), pltpu.VMEM((tokens, width), BF)],
        2 * tokens * width * width * 10,
        20 * 2**20,
        (attn, hidden_in, cot, w_space_out, w_time_qkv, w_time_out),
    )


def shards(
    hidden_in, query_space, key_space, value_space, cotangent, w_space_out, w_time_qkv, w_time_out
):
    width = hidden_in.shape[2]
    frames = lax.axis_size("frame")
    head_blocks, hidden_cols, cot_cols, attn, o_rows, lse = space_forward(
        query_space, key_space, value_space, hidden_in, cotangent, frames
    )
    g_out, grad_cols, out_cols, attn_space, hidden, attn_time, dqkv = middle(
        attn, hidden_cols, cot_cols, w_space_out, w_time_qkv, w_time_out
    )
    pairs = (attn_space, hidden, attn_time, grad_cols, dqkv, cot_cols.reshape(-1, width), out_cols)
    back, sums, grad_hidden, block_out = space_backward(head_blocks, o_rows, lse, g_out, pairs)
    block_out = block_out.reshape(hidden_in.shape)
    grad_hidden = grad_hidden.reshape(hidden_in.shape)
    space = lax.axis_index("space")
    own = lax.dynamic_slice_in_dim(sums, space * OWN_ROWS - window_start(space), OWN_ROWS, 1)
    own = own.transpose(1, 0, 2).reshape(OWN_ROWS, -1).astype(F32)
    cuts = (own[:, :width], own[:, width : 4 * width], own[:, 4 * width : 5 * width])
    return (block_out, grad_hidden, *join_heads(back), *cuts)


def solution(mesh):
    rows = P("frame", "space", None)
    weights = P(ALL, None)
    return jax.shard_map(
        shards,
        mesh=mesh,
        in_specs=(rows,) * 5 + (P(),) * 3,
        out_specs=(rows,) * 5 + (weights,) * 3,
        check_vma=False,
    )
```

```python
import jax
import jax.numpy as jnp
from jax import lax
from jax.experimental import pallas as pl
from jax.experimental.pallas import tpu as pltpu
from jax.sharding import PartitionSpec as P

HEADS = 16
HD = 72
ROWS = 80
SCALE = HD**-0.5
LOG2E = 1.4426950408889634
VMEM_BYTES = 62 * 2**20
BF = jnp.bfloat16
F32 = jnp.float32
ALL = ("frame", "space")


def kernel_call(body, out_shape, scratch_shapes, flops, moved, args):
    return pl.pallas_call(
        body,
        out_shape=out_shape,
        scratch_shapes=scratch_shapes,
        compiler_params=pltpu.CompilerParams(vmem_limit_bytes=VMEM_BYTES),
        cost_estimate=pl.CostEstimate(flops=flops, bytes_accessed=moved, transcendentals=0),
    )(*args)


def shape(dims, dtype):
    return jax.ShapeDtypeStruct(dims, dtype)


def dot(a, b):
    return jnp.dot(a, b, preferred_element_type=F32)


def dot_nt(a, b):
    return lax.dot_general(a, b, (((1,), (1,)), ((), ())), preferred_element_type=F32)


def dot_tn(a, b):
    return lax.dot_general(a, b, (((0,), (0,)), ((), ())), preferred_element_type=F32)


def two_parts(x):
    high = x.astype(BF)
    return [high, (x - high.astype(F32)).astype(BF)]


def three_parts_rows(x, rows):
    high = x.astype(BF).astype(F32)
    rest = x - high
    mid = rest.astype(BF).astype(F32)
    low = rest - mid
    at = lax.broadcasted_iota(jnp.int32, (rows, x.shape[1]), 0)
    return jnp.where(at == 0, high, jnp.where(at == 1, mid, jnp.where(at == 2, low, 0.0))).astype(BF)


def minus_rows(rows, columns):
    at = lax.broadcasted_iota(jnp.int32, (rows, columns), 0)
    return jnp.where(at < 3, -1.0, 0.0).astype(BF)


def split_heads(ref, out_ref, i):
    tokens = ref.shape[1]
    at = lax.broadcasted_iota(jnp.int32, (ROWS - HD, tokens), 0)
    fill = jnp.where(at == 0, 1.0 if i == 2 else 0.0, 0.0)
    flipped = ref[0].astype(F32).T
    for h in range(HEADS):
        block = jnp.concatenate([flipped[h * HD : (h + 1) * HD], fill], axis=0)
        out_ref[h, i] = block.astype(BF)


def join_heads_body(in_ref, q_ref, k_ref, v_ref):
    for i, ref in enumerate((q_ref, k_ref, v_ref)):
        blocks = [in_ref[h, i].astype(F32)[:HD] for h in range(HEADS)]
        ref[0] = jnp.concatenate(blocks, axis=0).T.astype(BF)


def join_heads(blocks):
    tokens = blocks.shape[3]
    rows = shape((1, tokens, HEADS * HD), BF)
    return kernel_call(
        join_heads_body, (rows, rows, rows), [], 0, 3 * tokens * HEADS * HD * 5, (blocks,)
    )


def copy_to(src, dst, send_sem, recv_sem, device):
    return pltpu.make_async_remote_copy(
        src_ref=src,
        dst_ref=dst,
        send_sem=send_sem,
        recv_sem=recv_sem,
        device_id=device,
        device_id_type=pl.DeviceIdType.MESH,
    )


def signal_all(barrier, peers):
    for peer in peers:
        pl.semaphore_signal(barrier, inc=1, device_id=peer, device_id_type=pl.DeviceIdType.MESH)


def rows_of(ref, i, count):
    return ref.at[pl.ds(pl.multiple_of(i * count, count), count)]


def scaled_query(block):
    return two_parts(block.astype(F32) * (SCALE * LOG2E))


def space_forward_body(
    q_ref,
    k_ref,
    v_ref,
    hidden_ref,
    cot_ref,
    x_ref,
    hidden_cols_ref,
    cot_cols_ref,
    attn_ref,
    o_rows_ref,
    lse_ref,
    packed,
    o_buf,
    heads_in,
    k_nat,
    v_rows,
    s_one,
    s_two,
    send_x,
    recv_x,
    send_f,
    recv_f,
    send_o,
    recv_o,
    send_a,
    recv_a,
):
    blocks, _, _, width = x_ref.shape
    frames, positions, _ = hidden_cols_ref.shape
    seq = blocks * width
    frame, space = lax.axis_index("frame"), lax.axis_index("space")
    others = [lax.rem(space + i, blocks) for i in range(1, blocks)]
    other_frames = [lax.rem(frame + i, frames) for i in range(1, frames)]
    peers = [(frame, to) for to in others] + [(to, space) for to in other_frames]
    barrier = pltpu.get_barrier_semaphore()
    signal_all(barrier, peers)

    waits = []
    for i, ref in ((1, k_ref), (2, v_ref), (0, q_ref)):
        split_heads(ref, packed, i)
        if not waits:
            pl.semaphore_wait(barrier, len(peers))
        for n, to in enumerate(others):
            c = copy_to(
                packed.at[to, i],
                x_ref.at[space, i],
                send_x.at[i, n],
                recv_x.at[i, n],
                (frame, to),
            )
            c.start()
            waits.append(c)
        x_ref[space, i] = packed[space, i]
    moves = []
    for i, (ref, out) in enumerate(((hidden_ref, hidden_cols_ref), (cot_ref, cot_cols_ref))):
        for n, to in enumerate(other_frames):
            c = copy_to(
                rows_of(ref.at[0], to, positions),
                out.at[frame],
                send_f.at[i, n],
                recv_f.at[i, n],
                (to, space),
            )
            c.start()
            moves.append(c)
        out[frame] = rows_of(ref.at[0], frame, positions)[...]
    for c in waits[: 2 * len(others)]:
        c.wait()

    def prepare(j, _):
        at = pl.ds(pl.multiple_of(j * width, width), width)
        k_block = x_ref[j, 1]
        k_nat[at, :] = jnp.concatenate([k_block, k_block], axis=0).T
        v_rows[:, at] = x_ref[j, 2]
        return 0

    lax.fori_loop(0, blocks, prepare, 0)

    def score(j, s_ref):
        q_block = jnp.concatenate(scaled_query(x_ref[j, 0]), axis=0)
        top = None
        for c in range(CHUNKS):
            at = slice(c * seq // CHUNKS, (c + 1) * seq // CHUNKS)
            s = dot(k_nat[at, :], q_block)
            s_ref[at, :] = s
            best = jnp.max(s, axis=0, keepdims=True)
            top = best if top is None else jnp.maximum(top, best)
        return top

    def block_at(t):
        return lax.rem(space + 2 * blocks - 1 - t, blocks)

    def query_block(t):
        to = lax.rem(space + 1 + t, blocks)
        return copy_to(
            packed.at[to, 0], x_ref.at[space, 0], send_x.at[0, t], recv_x.at[0, t], (frame, to)
        )

    def send_block(t):
        to = block_at(t)
        return copy_to(o_buf.at[to], heads_in.at[t], send_o.at[t], recv_o.at[t], (frame, to))

    def both(t, s_ref, top, t_after, s_after):
        j, after = block_at(t), block_at(t_after)

        @pl.when(t_after < blocks - 1)
        def _():
            query_block(t_after).wait_recv()

        q_block = jnp.concatenate(scaled_query(x_ref[after, 0]), axis=0)
        top_after = None
        mixed = jnp.zeros((ROWS, width), F32)
        for c in range(CHUNKS):
            at = slice(c * seq // CHUNKS, (c + 1) * seq // CHUNKS)
            s = dot(k_nat[at, :], q_block)
            s_after[at, :] = s
            best = jnp.max(s, axis=0, keepdims=True)
            top_after = best if top_after is None else jnp.maximum(top_after, best)
            probs = jnp.exp2(s_ref[at, :] - top).astype(BF)
            mixed = mixed + dot(v_rows[:, at], probs)
        total = mixed[HD : HD + 1]
        mixed = mixed / total
        o_rows_ref[j] = mixed
        lse_ref[j] = jnp.broadcast_to(top + jnp.log2(total), (8, width))
        filled = jnp.concatenate([mixed[:HD], jnp.zeros((128 - HD, width), F32)], axis=0)
        o_buf[j] = filled.T.astype(BF).reshape(frames, positions, 128)

        @pl.when(t < blocks - 1)
        def _():
            send_block(t).start()

        return top_after

    def two_steps(i, top):
        j = 2 * i
        top = both(j, s_one, top, j + 1, s_two)
        return both(j + 1, s_two, top, jnp.minimum(j + 2, blocks - 1), s_one)

    def pass_on(g, begin, count):
        some = pl.ds(begin, count)
        for n, to in enumerate(other_frames):
            c = copy_to(
                heads_in.at[some, to],
                attn_ref.at[frame, some],
                send_a.at[g, n],
                recv_a.at[g, n],
                (to, space),
            )
            c.start()
            moves.append(c)
        attn_ref[frame, some] = heads_in[some, frame]

    query_block(0).wait_recv()
    top = lax.fori_loop(0, PASS_AFTER // 2, two_steps, score(block_at(0), s_one))
    for t in range(PASS_FIRST):
        send_block(t).wait()
    pass_on(0, 0, PASS_FIRST)
    lax.fori_loop(PASS_AFTER // 2, blocks // 2, two_steps, top)
    heads_in[blocks - 1] = o_buf[space]
    for t in range(PASS_FIRST, blocks - 1):
        send_block(t).wait()
    pass_on(1, PASS_FIRST, blocks - PASS_FIRST)
    for t in range(blocks - 1):
        query_block(t).wait_send()
    for c in moves:
        c.wait()


CHUNKS = 8
PASS_FIRST = 10
PASS_AFTER = 12


def space_forward(query, key_rows, value_rows, hidden_in, cot, frames):
    tokens, model = query.shape[1:]
    seq = HEADS * tokens
    dma = pltpu.SemaphoreType.DMA
    cols = shape((frames, tokens // frames, model), BF)
    return pl.pallas_call(
        space_forward_body,
        out_shape=(
            shape((HEADS, 3, ROWS, tokens), BF),
            cols,
            cols,
            shape((frames, HEADS, tokens // frames, 128), BF),
            shape((HEADS, ROWS, tokens), F32),
            shape((HEADS, 8, tokens), F32),
        ),
        in_specs=[pl.BlockSpec(memory_space=pltpu.VMEM)] * 5,
        out_specs=[pl.BlockSpec(memory_space=pltpu.VMEM)] * 6,
        scratch_shapes=[
            pltpu.VMEM((HEADS, 3, ROWS, tokens), BF),
            pltpu.VMEM((HEADS, frames, tokens // frames, 128), BF),
            pltpu.VMEM((HEADS, frames, tokens // frames, 128), BF),
            pltpu.VMEM((seq, 2 * ROWS), BF),
            pltpu.VMEM((ROWS, seq), BF),
            pltpu.VMEM((seq, tokens), F32),
            pltpu.VMEM((seq, tokens), F32),
            dma((3, HEADS - 1)),
            dma((3, HEADS - 1)),
            dma((2, frames - 1)),
            dma((2, frames - 1)),
            dma((HEADS - 1,)),
            dma((HEADS - 1,)),
            dma((2, frames - 1)),
            dma((2, frames - 1)),
        ],
        compiler_params=pltpu.CompilerParams(
            vmem_limit_bytes=VMEM_BYTES, collective_id=1, has_side_effects=True
        ),
        cost_estimate=pl.CostEstimate(
            flops=4 * seq * seq * 128, bytes_accessed=8 * 2**20, transcendentals=0
        ),
    )(query, key_rows, value_rows, hidden_in, cot)


Q_STEP = 1024
TILE_ROWS = 144
PART_ROWS = 48
TILE_COLS = 384


def backward_prepare(x_ref, o_rows_ref, lse_ref, g_ref, q_aug, g_aug, q_rows, g_rows, dq_sum):
    blocks, _, _, width = x_ref.shape

    def prepare(j, _):
        at = pl.ds(pl.multiple_of(j * width, width), width)
        q_block = x_ref[j, 0]
        parts = scaled_query(q_block) + [three_parts_rows(lse_ref[j][:1], 16)]
        q_aug[at, :] = jnp.concatenate(parts, axis=0).T
        q_rows[:, at] = q_block
        g_block = g_ref[:, j].reshape(width, 128).astype(F32).T[:ROWS]
        inner = jnp.sum(g_block[:HD] * o_rows_ref[j][:HD], axis=0, keepdims=True)
        g_bf = g_block.astype(BF)
        g_rows[:, at] = g_bf
        g_aug[at, :] = jnp.concatenate([g_bf, three_parts_rows(inner, 16)], axis=0).T
        dq_sum[at, :] = jnp.zeros((width, ROWS), F32)
        return 0

    lax.fori_loop(0, blocks, prepare, 0)


def backward_steps(
    first, last, done, x_ref, out_ref, q_aug, g_aug, q_rows, g_rows, p_buf, ds_buf, dq_sum
):
    blocks, _, _, width = x_ref.shape
    seq = blocks * width

    def step(t, _):
        j = lax.rem(lax.axis_index("space") + 1 + t, blocks)
        k_block = x_ref[j, 1]
        v_block = x_ref[j, 2]
        k_aug = jnp.concatenate([k_block, k_block, minus_rows(16, width)], axis=0)
        v_aug = jnp.concatenate([v_block, minus_rows(16, width)], axis=0)
        k_nat = k_block.T

        for c in range(seq // Q_STEP):
            at = pl.ds(c * Q_STEP, Q_STEP)
            probs = jnp.exp2(dot(q_aug[at, :], k_aug))
            p_buf[at, :] = probs.astype(BF)
            ds = (probs * dot(g_aug[at, :], v_aug)).astype(BF)
            ds_buf[at, :] = ds
            dq_sum[at, :] += dot(ds, k_nat)

        out_ref[j, 1] = (dot(q_rows[...], ds_buf[...]) * SCALE).astype(BF)
        out_ref[j, 2] = dot(g_rows[...], p_buf[...]).astype(BF)
        done(t, last)
        return 0

    lax.fori_loop(first, last, step, 0)


OWN_ROWS = 9
WINDOW = 32


def window_start(space):
    return jnp.minimum(lax.div(space * OWN_ROWS, 16) * 16, TILE_ROWS - WINDOW)


def window(space):
    return pl.ds(pl.multiple_of(window_start(space), 16), WINDOW)


def add_into(target, terms, lead):
    count = 1
    for n in lead:
        count *= n

    def one(i, _):
        index = []
        for n in reversed(lead):
            index.insert(0, lax.rem(i, n))
            i = lax.div(i, n)
        total = target(*index)[...].astype(F32)
        for term in terms:
            total = total + term(*index)[...].astype(F32)
        target(*index)[...] = total.astype(BF)
        return 0

    lax.fori_loop(0, count, one, 0)


def space_backward_body(
    x_ref,
    o_rows_ref,
    lse_ref,
    g_out_ref,
    attn_space_ref,
    hidden_ref,
    attn_time_ref,
    gh_ref,
    dqkv_ref,
    cot_ref,
    out_cols_ref,
    back_ref,
    sums_ref,
    grad_hidden_ref,
    block_out_ref,
    out_ref,
    g_mid,
    g_ref,
    rows_t,
    q_aug,
    g_aug,
    q_rows,
    g_rows,
    p_buf,
    ds_buf,
    dq_sum,
    terms,
    half,
    in_a1,
    in_b1,
    in_c1,
    in_a2,
    in_b2,
    in_c2,
    in_3,
    mine,
    send1,
    recv1,
    sends,
    recvs,
    send6,
    recv6,
    send_f,
    recv_f,
    send_kv,
    recv_kv,
    send_q,
    recv_q,
    send_g,
    recv_g,
    send_h,
    recv_h,
):
    frame, space = lax.axis_index("frame"), lax.axis_index("space")
    z, lo = lax.div(frame, 2), lax.rem(frame, 2)
    x, hi, core = lax.div(space, 4), lax.rem(lax.div(space, 2), 2), lax.rem(space, 2)

    def x_peer(i):
        return (frame, lax.rem(x + i, 4) * 4 + hi * 2 + core)

    def z_peer(i):
        return (lax.rem(z + i, 4) * 2 + lo, space)

    def space_peer(i):
        return (frame, lax.rem(space + i, 16))

    def y_index(i):
        return (1 - lo if i % 2 else lo), (1 - hi if i // 2 else hi)

    def y_peer(i):
        to_lo, to_hi = y_index(i)
        return (z * 2 + to_lo, x * 4 + to_hi * 2 + core)

    core_peer = (frame, x * 4 + hi * 2 + 1 - core)
    copy = copy_to
    others = [lax.rem(space + i, 16) for i in range(1, 16)]
    other_frames = [lax.rem(frame + i, 8) for i in range(1, 8)]
    peers = [(frame, to) for to in others] + [(to, space) for to in other_frames]
    peers.append(y_peer(3))
    barrier = pltpu.get_barrier_semaphore()
    signal_all(barrier, peers)

    pl.semaphore_wait(barrier, len(peers))
    to_frames = [
        copy(g_out_ref.at[to], g_mid.at[frame], send_g.at[n], recv_g.at[n], (to, space))
        for n, to in enumerate(other_frames)
    ]
    for c in to_frames:
        c.start()
    g_mid[frame] = g_out_ref[frame]

    first = []

    def store_terms(t, part):
        for f in range(8):
            for p in range(3):
                begin = f * TILE_ROWS + p * PART_ROWS
                terms[p, t // 4, f % 2, f // 2, t // 2 % 2, t % 2] = part[begin : begin + PART_ROWS]
        if t % 4 == 3:
            for p in range(3):
                c = copy(
                    terms.at[p, t // 4, :, :, :, 1 - core],
                    half.at[p, t // 4],
                    send1.at[p, t // 4],
                    recv1.at[p, t // 4],
                    core_peer,
                )
                c.start()
                first.append(c)

    for rows_ref, grads_ref, begin, tiles in (
        (attn_space_ref, gh_ref, 0, 3),
        (hidden_ref, dqkv_ref, 3, 9),
        (attn_time_ref, cot_ref, 12, 3),
    ):
        rows_t[...] = rows_ref[...].T
        for n in range(tiles):
            part = dot(rows_t[...], grads_ref[:, n * TILE_COLS : (n + 1) * TILE_COLS])
            store_terms(begin + n, part.astype(BF))
    store_terms(15, jnp.zeros((8 * TILE_ROWS, TILE_COLS), BF))

    for c in to_frames:
        c.wait()
    to_heads = [
        copy(g_mid.at[:, to], g_ref.at[:, space], send_h.at[n], recv_h.at[n], (frame, to))
        for n, to in enumerate(others)
    ]
    for c in to_heads:
        c.start()
    g_ref[:, space] = g_mid[:, space]

    state = (q_aug, g_aug, q_rows, g_rows)
    def attend(start, stop):
        backward_steps(start, stop, send_step, x_ref, out_ref, *state, p_buf, ds_buf, dq_sum)

    def key_grads(t):
        to = lax.rem(space + 1 + t, 16)
        return copy(
            out_ref.at[to, pl.ds(1, 2)],
            back_ref.at[space, pl.ds(1, 2)],
            send_kv.at[t],
            recv_kv.at[t],
            (frame, to),
        )

    def query_grads(t):
        to = lax.rem(space + 1 + t, 16)
        return copy(
            out_ref.at[to, 0], back_ref.at[space, 0], send_q.at[t], recv_q.at[t], (frame, to)
        )

    def send_step(t, stop):
        if stop < 16:
            key_grads(t).start()

    for c in first:
        c.wait()
    add_into(
        lambda p, a, y, w: half.at[p, a, y, w],
        [lambda p, a, y, w: terms.at[p, a, y, w, :, core]],
        (3, 4, 2, 4),
    )

    def stage(n, along_x, along_z, along_y):
        started = []
        for i in range(1, 4):
            for source, slots, index, peer in (
                (*along_x, lax.rem(x + i, 4), x_peer(i)),
                (*along_z, lax.rem(z + i, 4), z_peer(i)),
                (*along_y, y_index(i), y_peer(i)),
            ):
                at = len(started)
                started.append(
                    copy(source(index), slots(i - 1), sends.at[n, at], recvs.at[n, at], peer)
                )
        for c in started:
            c.start()
        return started

    def add_all(started, *sums):
        for c in started:
            c.wait()
        for target, slots, lead in sums:
            add_into(target, [lambda *at, k=k: slots(k, *at) for k in range(3)], lead)

    a1 = lambda k, *at: in_a1.at[(k, *at)]
    b1 = lambda k, *at: in_b1.at[(k, *at)]
    c1 = lambda k, *at: in_c1.at[(k, *at)]
    a2 = lambda k, *at: in_a2.at[(k, *at)]
    b2 = lambda k, *at: in_b2.at[(k, *at)]
    c2 = lambda k, *at: in_c2.at[(k, *at)]

    started = stage(
        0,
        (lambda i: half.at[0, i], a1),
        (lambda i: half.at[1, :, :, i], b1),
        (lambda i: half.at[2, :, i[0], :, i[1]], c1),
    )
    for c in to_heads:
        c.wait()
    backward_prepare(x_ref, o_rows_ref, lse_ref, g_ref, *state, dq_sum)
    attend(0, STAGES[0])
    add_all(
        started,
        (lambda y, w: half.at[0, x, y, w], a1, (2, 4)),
        (lambda a, y: half.at[1, a, y, z], b1, (4, 2)),
        (lambda a, w: half.at[2, a, lo, w, hi], c1, (4, 4)),
    )
    started = stage(
        1,
        (lambda i: half.at[2, i, lo, :, hi], c2),
        (lambda i: half.at[0, x, :, i], a2),
        (lambda i: half.at[1, :, i[0], z, i[1]], b2),
    )
    moves = []
    for i, (ref, out) in enumerate(((gh_ref, grad_hidden_ref), (out_cols_ref, block_out_ref))):
        positions = out.shape[1]
        for n, to in enumerate(other_frames):
            c = copy(
                rows_of(ref, to, positions),
                out.at[frame],
                send_f.at[i, n],
                recv_f.at[i, n],
                (to, space),
            )
            c.start()
            moves.append(c)
        out[frame] = rows_of(ref, frame, positions)[...]

    attend(STAGES[0], STAGES[1])
    add_all(
        started,
        (lambda y: half.at[0, x, y, z], a2, (2,)),
        (lambda a: half.at[1, a, lo, z, hi], b2, (4,)),
        (lambda w: half.at[2, x, lo, w, hi], c2, (4,)),
    )
    started = stage(
        2,
        (lambda i: half.at[1, i, lo, z, hi], lambda k: in_3.at[1, k]),
        (lambda i: half.at[2, x, lo, i, hi], lambda k: in_3.at[2, k]),
        (lambda i: half.at[0, x, i[0], z, i[1]], lambda k: in_3.at[0, k]),
    )
    attend(STAGES[1], STAGES[2])
    for c in started:
        c.wait()
    for p in range(3):
        total = half[p, x, lo, z, hi].astype(F32)
        for k in range(3):
            total = total + in_3[p, k].astype(F32)
        mine[p * PART_ROWS : (p + 1) * PART_ROWS] = total.astype(BF)
    sixth = [
        copy(
            mine.at[window(lax.rem(space + i, 16))],
            sums_ref.at[space],
            send6.at[i - 1],
            recv6.at[i - 1],
            space_peer(i),
        )
        for i in range(1, 16)
    ]
    for c in sixth:
        c.start()
    sums_ref[space] = mine[window(space)]
    attend(STAGES[2], 15)
    attend(15, 16)

    def finish(t, _):
        to = lax.rem(space + 1 + t, 16)
        at = pl.ds(pl.multiple_of(to * width, width), width)
        out_ref[to, 0] = (dq_sum[at, :] * SCALE).T.astype(BF)

        @pl.when(t < 15)
        def _():
            query_grads(t).start()

        return 0

    width = x_ref.shape[3]
    lax.fori_loop(0, 16, finish, 0)
    back_ref[space] = out_ref[space]
    for c in moves + sixth:
        c.wait()
    for t in range(15):
        key_grads(t).wait()
        query_grads(t).wait()


STAGES = (9, 12, 14)


def space_backward(blocks, o_rows, lse, grads, pairs):
    count, _, _, width = blocks.shape
    seq = count * width
    part = (PART_ROWS, TILE_COLS)
    by_frame = shape((8, width // 8, HEADS * HD), BF)
    dma = pltpu.SemaphoreType.DMA
    return pl.pallas_call(
        space_backward_body,
        out_shape=(shape(blocks.shape, BF), shape((16, WINDOW, TILE_COLS), BF), by_frame, by_frame),
        in_specs=[pl.BlockSpec(memory_space=pltpu.VMEM)] * 11,
        out_specs=[pl.BlockSpec(memory_space=pltpu.VMEM)] * 4,
        scratch_shapes=[
            pltpu.VMEM(blocks.shape, BF),
            pltpu.VMEM(grads.shape, BF),
            pltpu.VMEM(grads.shape, BF),
            pltpu.VMEM((HEADS * HD, width), BF),
            pltpu.VMEM((seq, 2 * ROWS + 16), BF),
            pltpu.VMEM((seq, ROWS + 16), BF),
            pltpu.VMEM((ROWS, seq), BF),
            pltpu.VMEM((ROWS, seq), BF),
            pltpu.VMEM((seq, width), BF),
            pltpu.VMEM((seq, width), BF),
            pltpu.VMEM((seq, ROWS), F32),
            pltpu.VMEM((3, 4, 2, 4, 2, 2) + part, BF),
            pltpu.VMEM((3, 4, 2, 4, 2) + part, BF),
            pltpu.VMEM((3, 2, 4, 2) + part, BF),
            pltpu.VMEM((3, 4, 2, 2) + part, BF),
            pltpu.VMEM((3, 4, 4) + part, BF),
            pltpu.VMEM((3, 2, 2) + part, BF),
            pltpu.VMEM((3, 4) + part, BF),
            pltpu.VMEM((3, 4) + part, BF),
            pltpu.VMEM((3, 3) + part, BF),
            pltpu.VMEM((TILE_ROWS, TILE_COLS), BF),
            dma((3, 4)),
            dma((3, 4)),
            dma((3, 9)),
            dma((3, 9)),
            dma((15,)),
            dma((15,)),
            dma((2, 7)),
            dma((2, 7)),
            dma((15,)),
            dma((15,)),
            dma((15,)),
            dma((15,)),
            dma((7,)),
            dma((7,)),
            dma((15,)),
            dma((15,)),
        ],
        compiler_params=pltpu.CompilerParams(
            vmem_limit_bytes=VMEM_BYTES, collective_id=0, has_side_effects=True
        ),
        cost_estimate=pl.CostEstimate(
            flops=10 * seq * seq * 128, bytes_accessed=16 * 2**20, transcendentals=0
        ),
    )(blocks, o_rows, lse, grads, *pairs)


def middle_body(
    attn_ref,
    hidden_in_ref,
    cot_ref,
    w_space_ref,
    w_qkv_ref,
    w_time_ref,
    g_out_ref,
    gh_ref,
    out_ref,
    attn_space_ref,
    hidden_ref,
    attn_time_ref,
    dqkv_ref,
    qkv_ref,
    ga_ref,
):
    frames, _, positions, _ = attn_ref.shape
    tokens = frames * positions
    width = HEADS * HD
    space = lax.axis_index("space")
    for h in range(HEADS):
        slot = lax.rem(h + 2 * HEADS - 1 - space, HEADS)
        block = attn_ref[:, slot].reshape(tokens, 128)
        attn_space_ref[:, h * HD : (h + 1) * HD] = block[:, :HD]
    cot = cot_ref[...].reshape(tokens, width)
    base = hidden_in_ref[...].reshape(tokens, width).astype(F32)
    hidden_ref[...] = (base + dot(attn_space_ref[...], w_space_ref[...])).astype(BF)
    for c in range(3):
        at = pl.ds(c * width, width)
        qkv_ref[:, at] = dot(hidden_ref[...], w_qkv_ref[:, at]).astype(BF)
    ga_ref[...] = dot_nt(cot, w_time_ref[...]).astype(BF)

    same = (
        lax.broadcasted_iota(jnp.int32, (tokens, tokens), 0) % positions
        == lax.broadcasted_iota(jnp.int32, (tokens, tokens), 1) % positions
    )
    for h in range(HEADS):
        lo, hi = h * HD, (h + 1) * HD
        q = qkv_ref[:, lo:hi]
        k = qkv_ref[:, width + lo : width + hi]
        v = qkv_ref[:, 2 * width + lo : 2 * width + hi]
        g = ga_ref[:, lo:hi]
        scores = jnp.where(same, dot_nt(q, k) * SCALE, -jnp.inf)
        exps = jnp.exp(scores - jnp.max(scores, axis=1, keepdims=True))
        probs = exps / jnp.sum(exps, axis=1, keepdims=True)
        probs_bf = probs.astype(BF)
        attn_time_ref[:, lo:hi] = dot(probs_bf, v).astype(BF)
        weighted = probs * dot_nt(g, v)
        ds = ((weighted - probs * jnp.sum(weighted, axis=1, keepdims=True)) * SCALE).astype(BF)
        dqkv_ref[:, lo:hi] = dot(ds, k).astype(BF)
        dqkv_ref[:, width + lo : width + hi] = dot_tn(ds, q).astype(BF)
        dqkv_ref[:, 2 * width + lo : 2 * width + hi] = dot_tn(probs_bf, g).astype(BF)

    gh_ref[...] = (cot.astype(F32) + dot_nt(dqkv_ref[...], w_qkv_ref[...])).astype(BF)
    ga_ref[...] = dot_nt(gh_ref[...], w_space_ref[...]).astype(BF)
    for h in range(HEADS):
        block = ga_ref[:, h * HD : (h + 1) * HD]
        filled = jnp.concatenate([block, jnp.zeros((tokens, 128 - HD), BF)], axis=1)
        g_out_ref[:, h] = filled.reshape(frames, positions, 128)
    out = hidden_ref[...].astype(F32) + dot(attn_time_ref[...], w_time_ref[...])
    out_ref[...] = out.astype(BF)


def middle(attn, hidden_in, cot, w_space_out, w_time_qkv, w_time_out):
    frames, _, positions, _ = attn.shape
    tokens = frames * positions
    width = HEADS * HD
    rows = shape((tokens, width), BF)
    wide = shape((tokens, 3 * width), BF)
    return kernel_call(
        middle_body,
        (shape(attn.shape, BF), rows, rows, rows, rows, rows, wide),
        [pltpu.VMEM((tokens, 3 * width), BF), pltpu.VMEM((tokens, width), BF)],
        2 * tokens * width * width * 10,
        20 * 2**20,
        (attn, hidden_in, cot, w_space_out, w_time_qkv, w_time_out),
    )


def shards(
    hidden_in, query_space, key_space, value_space, cotangent, w_space_out, w_time_qkv, w_time_out
):
    width = hidden_in.shape[2]
    frames = lax.axis_size("frame")
    head_blocks, hidden_cols, cot_cols, attn, o_rows, lse = space_forward(
        query_space, key_space, value_space, hidden_in, cotangent, frames
    )
    g_out, grad_cols, out_cols, attn_space, hidden, attn_time, dqkv = middle(
        attn, hidden_cols, cot_cols, w_space_out, w_time_qkv, w_time_out
    )
    pairs = (attn_space, hidden, attn_time, grad_cols, dqkv, cot_cols.reshape(-1, width), out_cols)
    back, sums, grad_hidden, block_out = space_backward(head_blocks, o_rows, lse, g_out, pairs)
    block_out = block_out.reshape(hidden_in.shape)
    grad_hidden = grad_hidden.reshape(hidden_in.shape)
    space = lax.axis_index("space")
    own = lax.dynamic_slice_in_dim(sums, space * OWN_ROWS - window_start(space), OWN_ROWS, 1)
    own = own.transpose(1, 0, 2).reshape(OWN_ROWS, -1).astype(F32)
    cuts = (own[:, :width], own[:, width : 4 * width], own[:, 4 * width : 5 * width])
    return (block_out, grad_hidden, *join_heads(back), *cuts)


def solution(mesh):
    rows = P("frame", "space", None)
    weights = P(ALL, None)
    return jax.shard_map(
        shards,
        mesh=mesh,
        in_specs=(rows,) * 5 + (P(),) * 3,
        out_specs=(rows,) * 5 + (weights,) * 3,
        check_vma=False,
    )
```
